32 devices in a mesh: blk: 8 (over z, y), sp: 4 (over x, core).
Axes of the slice: x: 2, y: 2, z: 4, core: 2. Of those that a mesh axis runs over, the one named last changes fastest.
Arguments:
- species: float32 [8, 256, 4096], P('sp', 'blk'), may hold values from 0 to 0.25
- interface_normal_flow: float32 [3, 256, 4096], P(None, 'blk'), may hold values from -6 to 6
- face_diffusion: float32 [3, 256, 4096], P(None, 'blk'), may hold values from 0.3 to 3
- inv_volume: float32 [256, 4096], P('blk'), may hold values from 0.5 to 2
- diffusivity: float32 [8], P('sp'), may hold values from 0.2 to 2
- low_partner: int32 [8, 64], P('blk'), may hold values from 0 to 7, as said below
- high_partner: int32 [8, 64], P('blk'), may hold values from 0 to 7, as said below
- low_orient: int32 [8, 64], P('blk'), may hold values from 0 to 7
- high_orient: int32 [8, 64], P('blk'), may hold values from 0 to 7, as said below
- droplet_table: float32 [8192, 128], P(('blk', 'sp')), may hold values from -6 to 6
- parcel_block: int32 [8192, 1], P(('blk', 'sp')), may hold values from 0 to 7; in each aligned block of 256 rows (0 to 255, 256 to 511, ...) at most 48 rows name the same one
- parcel_cell: int32 [8192], P(('blk', 'sp')), may hold values from 0 to 131071
- parcel_live: int32 [8192], P(('blk', 'sp')), may hold values 0 or 1
Outputs:
- new_species: float32 [8, 256, 4096], P('sp', 'blk')
- arrived: float32 [12288, 128], P(('blk', 'sp'))
The draws below stay inside these ranges and needn't reach their ends.
Inputs may be any that keep to these rules, and one draw needn't show every extreme that they name: low_partner: in each row no block appears more than 8 times and some block appears exactly 8 times; high_partner[c, t] = b exactly when low_partner[b, t] = c. high_partner: in each row no block appears more than 8 times and some block appears exactly 8 times. high_orient[c, t] = low_orient[high_partner[c, t], t]. parcel_block: among the slots of one device no block is named more than 48 times.
All inputs are finite; a program needn't handle non-finite values. No bound on the sum of `parcel_live` on one device may be relied on, other than what follows from the above.
Results may differ from the reference program's by a relative error of at most 0.00002.
Values sent between devices are 32-bit elements; how exact they have to be, the bound alone decides.
No kernel may reach another device: no remote copies, remote signals or barrier semaphores. Data moves between devices by JAX's collectives and lax.ppermute only.
A program may use at most 192 MiB of HBM per device.

```python
import math
import jax
import jax.numpy as jnp
import numpy as np
from jax import lax

NSPEC = 8
PV = 128
BJ = 64
BK = 64
TILE_SIDE = 8
CI = 32
PAR_DEV = 256
NBLOCKS = 8
JK = 4096
TILES = 64
PCAP = 48
N_SP = 4


def matching(key):
    base_key = jax.random.fold_in(key, 4711)
    key_outer, key_inner, key_shift, key_orient = jax.random.split(base_key, 4)
    outer_order = jax.random.permutation(key_outer, NBLOCKS).astype(jnp.int32)
    inner_order = jax.random.permutation(key_inner, NBLOCKS).astype(jnp.int32)
    shifts = jax.random.permutation(key_shift, NBLOCKS).astype(jnp.int32)[jnp.arange(TILES) % NBLOCKS]
    numbers = jnp.arange(NBLOCKS, dtype=jnp.int32)
    outer_inverse = jnp.zeros((NBLOCKS,), jnp.int32).at[outer_order].set(numbers)
    inner_inverse = jnp.zeros((NBLOCKS,), jnp.int32).at[inner_order].set(numbers)
    low_partner = outer_order[(inner_order[:, None] + shifts[None, :]) % NBLOCKS]
    high_partner = inner_inverse[(outer_inverse[:, None] - shifts[None, :]) % NBLOCKS]
    low_orient = jax.random.randint(key_orient, (NBLOCKS, TILES), 0, 8).astype(jnp.int32)
    high_orient = low_orient[high_partner, jnp.arange(TILES)[None, :]]
    return (low_partner.astype(jnp.int32), high_partner.astype(jnp.int32), low_orient, high_orient.astype(jnp.int32))


def draw_low_partner(key, part):
    return matching(key)[0]


def draw_high_partner(key, part):
    return matching(key)[1]


def draw_low_orient(key, part):
    return matching(key)[2]


def draw_high_orient(key, part):
    return matching(key)[3]


def set_ends(array, own_key, least, largest):
    index_at = [jax.random.randint(jax.random.fold_in(own_key, axis), (), 0, length) for axis, length in enumerate(array.shape)]
    widest = array.shape.index(max(array.shape))
    next_to = index_at[:widest] + [(index_at[widest] + 1) % array.shape[widest]] + index_at[widest + 1:]
    return array.at[tuple(index_at)].set(least).at[tuple(next_to)].set(largest)


def block_levels(rng, dims, shards, smallest, top_value):
    def one(axis_at, parts):
        heights = jax.random.uniform(jax.random.fold_in(jax.random.fold_in(rng, 6), axis_at), (parts,), jnp.float32, smallest / len(shards), top_value / len(shards))
        return jnp.repeat(jnp.exp(heights), dims[axis_at] // parts).reshape((-1,) + (1,) * (len(dims) - axis_at - 1))

    loudness = one(*shards[0])
    for cut in shards[1:]:
        loudness = loudness * one(*cut)
    return loudness


def assign_block(stream_key, own, number, rows, count, top, limit, lean):
    sequence = jax.random.permutation(stream_key, count)
    packed, usual = load_shares(count, rows * top, limit, lean, True), load_shares(count, rows * top, limit, lean, False)
    places = jnp.arange(count)

    def named(tallies, turn):
        used = int((tallies > 0).sum())
        fixed = max(1, used // 4)
        shifted = fixed + (places - fixed + turn * (used - fixed)) % max(1, count - fixed)
        return jnp.zeros((count,), jnp.int32).at[sequence[jnp.where(places < fixed, places, shifted)]].set(jnp.asarray(tallies, jnp.int32))

    tallies = jnp.where(number % 4 == 0, named(packed, number // 4), named(usual, number - number // 4 - 1))
    mixed = jax.random.permutation(jax.random.fold_in(own, 3), count)
    giver, taker = mixed[0:count // 2 * 2:2], mixed[1:count // 2 * 2:2]
    slack = jnp.minimum(tallies[giver] - 1, limit - tallies[taker]) // 2
    slack = jnp.where((giver == sequence[0]) | (taker == sequence[0]) | (tallies[taker] == 0), 0, jnp.maximum(slack, 0))
    shifted = jax.random.randint(jax.random.fold_in(own, 4), (count // 2,), 0, 1 << 20) % (slack + 1)
    tallies = tallies.at[giver].add(-shifted).at[taker].add(shifted)
    members = jnp.searchsorted(jnp.cumsum(tallies), jnp.arange(rows * top), side="right").astype(jnp.int32)
    table = members.reshape(top, rows).T
    table = table[jax.random.permutation(jax.random.fold_in(own, 1), rows)]
    turn = jax.random.randint(jax.random.fold_in(own, 2), (rows, 1), 0, top)
    return jnp.take_along_axis(table, (jnp.arange(top)[None, :] + turn) % top, axis=1)


def load_shares(amount, total, limit, skew, full):
    weights = [(1 << 20) // math.isqrt(standing ** skew) + 1 for standing in range(1, amount + 1)]
    largest = limit if full else min(limit, max(-(-total // amount), total * weights[0] // sum(weights)))
    least = 1 if total - largest >= amount - 1 else 0
    given, surplus = [largest] + [least] * (amount - 1), total - largest - least * (amount - 1)
    while surplus > 0:
        candidates = [i for i in range(1, amount) if given[i] < largest] or [i for i in range(1, amount) if given[i] < limit]
        whole, budget = sum([weights[i] for i in candidates]), surplus
        for i in candidates:
            more = min(limit - given[i], max(1, budget * weights[i] // whole), surplus)
            given[i] = given[i] + more
            surplus = surplus - more
    return np.array(given)


def bell_draw(own_key, shape, deviation, bound, pieces=(), kind=jnp.bfloat16):
    factor_of = block_levels(own_key, shape, pieces, -0.22, 0.18) if pieces else 1.0
    result = jax.random.normal(own_key, shape, jnp.float32) * deviation * factor_of
    return jnp.minimum(jnp.maximum(result, -bound), bound).astype(kind)


def setup_inputs(seed: int = 0) -> dict:
    key_list = jax.random.split(jax.random.key(seed), 14)
    species = jnp.clip(0.25 * jax.random.uniform(key_list[0], (NSPEC, NBLOCKS * CI, JK), jnp.float32) ** block_levels(key_list[0], (NSPEC, NBLOCKS * CI, JK), ((0, 4), (1, 8)), -0.2, 0.2), 0.0, 0.25)
    interface_normal_flow = bell_draw(key_list[1], (3, NBLOCKS * CI, JK), 1.0, 6.0, ((1, 8),), jnp.float32)
    face_diffusion = jnp.clip(jnp.exp(math.log(3.0) - 2.3025851 * jax.random.uniform(key_list[2], (3, NBLOCKS * CI, JK), jnp.float32) ** block_levels(key_list[2], (3, NBLOCKS * CI, JK), ((1, 8),), -0.2, 0.2)), 0.3, 3.0)
    inv_volume = jnp.clip(jnp.exp(math.log(2.0) - 1.3862944 * jax.random.uniform(key_list[3], (NBLOCKS * CI, JK), jnp.float32) ** block_levels(key_list[3], (NBLOCKS * CI, JK), ((0, 8),), -0.2, 0.2)), 0.5, 2.0)
    diffusivity = jnp.clip(jnp.exp(math.log(2.0) - 2.3025851 * jax.random.uniform(key_list[4], (NSPEC,), jnp.float32) ** block_levels(key_list[4], (NSPEC,), ((0, 4),), -0.2, 0.2)), 0.2, 2.0)
    low_partner = draw_low_partner(jax.random.fold_in(key_list[13], 71), 0)
    high_partner = draw_high_partner(jax.random.fold_in(key_list[13], 71), 0)
    low_orient = draw_low_orient(jax.random.fold_in(key_list[13], 71), 0)
    high_orient = draw_high_orient(jax.random.fold_in(key_list[13], 71), 0)
    droplet_table = bell_draw(key_list[9], (NBLOCKS * N_SP * PAR_DEV, PV), 1.0, 6.0, ((0, 32),), jnp.float32)
    parcel_block_keys = jax.random.split(jax.random.fold_in(key_list[10], 1), (NBLOCKS * N_SP * PAR_DEV) // PAR_DEV)
    parcel_block_turns = jax.random.permutation(jax.random.fold_in(key_list[10], 3), (NBLOCKS * N_SP * PAR_DEV) // PAR_DEV)
    parcel_block = jax.vmap(lambda own, number: assign_block(jax.random.fold_in(key_list[10], 2), own, number, PAR_DEV, NBLOCKS, 1, PCAP, 2))(parcel_block_keys, parcel_block_turns).reshape((NBLOCKS * N_SP * PAR_DEV, 1))
    parcel_cell = set_ends(jax.random.randint(key_list[11], (NBLOCKS * N_SP * PAR_DEV,), 0, CI * JK), jax.random.fold_in(key_list[11], 1), 0, (CI * JK) - 1).astype(jnp.int32)
    parcel_live = set_ends((jax.random.randint(key_list[12], (NBLOCKS * N_SP * PAR_DEV,), 0, 4) < 3).astype(jnp.int32), jax.random.fold_in(key_list[12], 1), 0, 1)
    return dict(species=species, interface_normal_flow=interface_normal_flow, face_diffusion=face_diffusion, inv_volume=inv_volume, diffusivity=diffusivity, low_partner=low_partner, high_partner=high_partner, low_orient=low_orient, high_orient=high_orient, droplet_table=droplet_table, parcel_block=parcel_block, parcel_cell=parcel_cell, parcel_live=parcel_live)


section_step = 0.5
friction_timescale = 0.3


def face_tiles(face):
    leading = face.shape[:-1]
    levels = len(leading)
    blocked = face.reshape(leading + (BJ // TILE_SIDE, TILE_SIDE, BK // TILE_SIDE, TILE_SIDE))
    axes_order = tuple(range(levels)) + (levels, levels + 2, levels + 1, levels + 3)
    return jnp.transpose(blocked, axes_order).reshape(leading + (TILES, TILE_SIDE * TILE_SIDE))


def tile_face(tiles):
    leading = tiles.shape[:-2]
    levels = len(leading)
    blocked = tiles.reshape(leading + (BJ // TILE_SIDE, BK // TILE_SIDE, TILE_SIDE, TILE_SIDE))
    axes_order = tuple(range(levels)) + (levels, levels + 2, levels + 1, levels + 3)
    return jnp.transpose(blocked, axes_order).reshape(leading + (BJ * BK,))


def orient(tiles, codes, inverse):
    square = tiles.reshape(tiles.shape[:-1] + (TILE_SIDE, TILE_SIDE))
    selector = codes[..., None, None, None]
    transposed = (selector // 4) % 2 == 1
    flip_rows = selector % 2 == 1
    flip_columns = (selector // 2) % 2 == 1
    if not inverse:
        square = jnp.where(transposed, jnp.swapaxes(square, -1, -2), square)
    square = jnp.where(flip_rows, jnp.flip(square, -2), square)
    square = jnp.where(flip_columns, jnp.flip(square, -1), square)
    if inverse:
        square = jnp.where(transposed, jnp.swapaxes(square, -1, -2), square)
    return square.reshape(tiles.shape)


def face_terms(ghost_low, values, ghost_high):
    extended = jnp.concatenate([ghost_low[:, None], values, ghost_high[:, None]], axis=1)
    upper_side = extended[:, 1:]
    lower_side = extended[:, :-1]
    previous_row = jnp.roll(values, BK, axis=-1)
    previous_column = jnp.roll(values, 1, axis=-1)
    differences = (upper_side - lower_side, values - previous_row, values - previous_column)
    averages = (0.5 * (upper_side + lower_side), 0.5 * (values + previous_row), 0.5 * (values + previous_column))
    return differences, averages


def partial_weights(differences, diffusivity):
    scaled = diffusivity[:, None, None]
    return tuple(jnp.sum(scaled * difference, axis=0) for difference in differences)


def advance(values, differences, averages, weights, velocity_faces, diffusion_faces, diffusivity, inv_volume, source, is_fuel):
    scaled = diffusivity[:, None, None]
    cell_index = jnp.arange(BJ * BK)
    wall_rows = cell_index // BK == 0
    wall_columns = cell_index % BK == 0
    fluxes = []
    for difference, middle, weight, velocity, diffusion in zip(differences, averages, weights, velocity_faces, diffusion_faces):
        fluxes.append(velocity * middle - diffusion * (scaled * difference - middle * weight))
    flux_layer, flux_row, flux_column = fluxes
    flux_row = jnp.where(wall_rows, 0.0, flux_row)
    flux_column = jnp.where(wall_columns, 0.0, flux_column)
    divergence = (flux_layer[:, 1:] - flux_layer[:, :-1]) + (jnp.roll(flux_row, -BK, axis=-1) - flux_row) + (jnp.roll(flux_column, -1, axis=-1) - flux_column)
    tendency = inv_volume * (source * (is_fuel - values) - divergence)
    return values + section_step * tendency


def droplet_motion_update(droplet_table, evaporate_component, ambient_flow_speed, alive_indicator):
    boiled_off_quantity = jax.nn.softplus(droplet_table[:, 1]) * (jax.nn.sigmoid(droplet_table[:, 2]) - evaporate_component) * alive_indicator
    shifted_droplet_list = droplet_table.at[:, 0].add(-boiled_off_quantity)
    shifted_droplet_list = shifted_droplet_list.at[:, 3:6].add(friction_timescale * (jnp.transpose(ambient_flow_speed) - droplet_table[:, 3:6]))
    return boiled_off_quantity, shifted_droplet_list * alive_indicator[:, None]


def reference(species, interface_normal_flow, face_diffusion, inv_volume, diffusivity, low_partner, high_partner, low_orient, high_orient, droplet_table, parcel_block, parcel_cell, parcel_live):
    spec_blocks = species.reshape(NSPEC, NBLOCKS, CI, BJ * BK)
    velocity_blocks = interface_normal_flow.reshape(3, NBLOCKS, CI, BJ * BK)
    diffusion_blocks = face_diffusion.reshape(3, NBLOCKS, CI, BJ * BK)
    high_tiles = jnp.transpose(face_tiles(spec_blocks[:, :, CI - 1]), (1, 2, 0, 3))
    low_face = jnp.concatenate([spec_blocks[:, :, 0], velocity_blocks[0:1, :, 0], diffusion_blocks[0:1, :, 0]], axis=0)
    low_tiles = jnp.transpose(face_tiles(low_face), (1, 2, 0, 3))
    tile_number = jnp.arange(TILES)[None, :]
    picked_high = high_tiles[low_partner, tile_number]
    ghost_low = tile_face(jnp.transpose(orient(picked_high, low_orient, False), (0, 2, 1, 3)))
    picked_low = low_tiles[high_partner, tile_number]
    ghost_high = tile_face(jnp.transpose(orient(picked_low, high_orient, True), (0, 2, 1, 3)))

    device_count = NBLOCKS * N_SP
    total_rows = device_count * PAR_DEV
    row_number = jnp.arange(total_rows, dtype=jnp.int32)
    source_device = row_number // PAR_DEV
    source_block = source_device // N_SP
    source_group = source_device % N_SP
    target_block = parcel_block[:, 0]
    active_rows = parcel_live == 1
    onehot = ((target_block[:, None] == jnp.arange(NBLOCKS, dtype=jnp.int32)[None, :]) & active_rows[:, None]).astype(jnp.int32)
    onehot = onehot.reshape(device_count, PAR_DEV, NBLOCKS)
    before = jnp.cumsum(onehot, axis=1) - onehot
    rank_before = jnp.sum(before * onehot, axis=-1).reshape(total_rows)
    arrival_rows = NBLOCKS * N_SP * NBLOCKS * PCAP
    slot_index = ((target_block * N_SP + source_group) * NBLOCKS + source_block) * PCAP + rank_before
    slot_index = jnp.where(active_rows, slot_index, arrival_rows).astype(jnp.int32)
    overall_grid_number = (target_block * (CI * BJ * BK) + parcel_cell).astype(jnp.int32)
    evaporate_component = species[0].reshape(-1)[overall_grid_number]
    ambient_flow_speed = interface_normal_flow.reshape(3, -1)[:, overall_grid_number]
    alive_indicator = active_rows.astype(jnp.float32)
    boiled_off_quantity, shifted_droplet_list = droplet_motion_update(droplet_table, evaporate_component, ambient_flow_speed, alive_indicator)
    arrived = jnp.zeros((arrival_rows, PV), jnp.float32).at[slot_index].set(shifted_droplet_list, mode="drop")
    source = jnp.zeros((NBLOCKS * CI * BJ * BK,), jnp.float32).at[overall_grid_number].add(boiled_off_quantity)
    source = source.reshape(NBLOCKS, CI, BJ * BK)

    is_fuel = (jnp.arange(NSPEC) == 0).astype(jnp.float32)[:, None, None]

    def one_block(inputs):
        values, velocity, diffusion, volume, low_side, high_side, block_source = inputs
        differences, averages = face_terms(low_side, values, high_side[:NSPEC])
        weights = partial_weights(differences, diffusivity)
        velocity_faces = (jnp.concatenate([velocity[0], high_side[NSPEC:NSPEC + 1]], axis=0), velocity[1], velocity[2])
        diffusion_faces = (jnp.concatenate([diffusion[0], high_side[NSPEC + 1:NSPEC + 2]], axis=0), diffusion[1], diffusion[2])
        return advance(values, differences, averages, weights, velocity_faces, diffusion_faces, diffusivity, volume, block_source, is_fuel)

    updated = lax.map(one_block, (jnp.transpose(spec_blocks, (1, 0, 2, 3)), jnp.transpose(velocity_blocks, (1, 0, 2, 3)), jnp.transpose(diffusion_blocks, (1, 0, 2, 3)), inv_volume.reshape(NBLOCKS, CI, BJ * BK), ghost_low, ghost_high, source))
    new_species = jnp.transpose(updated, (1, 0, 2, 3)).reshape(NSPEC, NBLOCKS * CI, BJ * BK)
    return new_species, arrived
```

```python
import functools

import jax
import jax.numpy as jnp
import ml_dtypes
import numpy as np
from jax import lax
from jax.experimental import pallas as pl
from jax.experimental.pallas import tpu as pltpu
from jax.sharding import PartitionSpec as P

PV = 128
BJ = 64
BK = 64
TILE_SIDE = 8
TILES = 64
LANES = 128
FACE = BJ * BK
STRIP = TILE_SIDE * BK
PAIRS = 4

section_step = 0.5
friction_timescale = 0.3

F32 = jnp.float32
BF16 = jnp.bfloat16
VMEM_LIMIT = 63 * 1024 * 1024


def orient_table(inverse):
    table = np.zeros((8, 64, 64), np.float32)
    for code in range(8):
        for r in range(8):
            for c in range(8):
                if inverse:
                    r0, c0 = (c, r) if code // 4 else (r, c)
                    r0 = 7 - r0 if code % 2 else r0
                    c0 = 7 - c0 if code // 2 % 2 else c0
                else:
                    r0 = 7 - r if code % 2 else r
                    c0 = 7 - c if code // 2 % 2 else c
                    r0, c0 = (c0, r0) if code // 4 else (r0, c0)
                table[code, r0 * 8 + c0, r * 8 + c] = 1
    return table.reshape(512, 64)


def tables():
    tile, lane, cell = np.arange(64), np.arange(STRIP), np.arange(64)
    strip_of = (tile[:, None] // 8 == np.arange(8)[None]).astype(np.float32)
    column_of = (tile[:, None] % 8 == (lane[None] // 8) % 8).astype(np.float32)
    inside = ((lane // 64) * 8 + lane % 8)[:, None] == cell[None]
    inside = inside.astype(np.float32)
    code_of = (np.arange(8)[:, None] == lane[None] // 64).astype(np.float32)
    there, back = orient_table(False), orient_table(True)
    zero = np.zeros_like(there)

    def pair(first, second):
        return np.concatenate(
            [np.concatenate([first, zero], 1), np.concatenate([zero, second], 1)], 0
        )

    zero_cells = np.zeros_like(inside)
    return dict(
        strip_of=strip_of,
        column_of=column_of,
        inside2=np.concatenate([inside, inside], 1),
        code_of=code_of,
        pair_high=pair(there, there),
        pair_low=pair(back, back),
        pair_mixed=pair(there, back),
        spread_first=np.concatenate([inside, zero_cells], 1).T,
        spread_second=np.concatenate([zero_cells, inside], 1).T,
    )


def iota(shape, dim):
    return lax.broadcasted_iota(jnp.int32, shape, dim)


def mm(a, b):
    return lax.dot_general(a, b, (((1,), (0,)), ((), ())), preferred_element_type=F32)


def mm_nt(a, b):
    return lax.dot_general(a, b, (((1,), (1,)), ((), ())), preferred_element_type=F32)


def split(value, parts):
    out = []
    for _ in range(parts - 1):
        head = value.astype(BF16)
        out.append(head)
        value = value - head.astype(F32)
    out.append(value.astype(BF16))
    return out


def place_matrix(partner, blocks, cap):
    onehot = (iota((blocks, TILES), 0) == partner).astype(F32)
    earlier = (iota((TILES, TILES), 0) < iota((TILES, TILES), 1)).astype(BF16)
    rank = jnp.sum(onehot * mm(onehot.astype(BF16), earlier), axis=0, keepdims=True)
    slot = partner * cap + rank.astype(jnp.int32)
    return (iota((TILES, TILES), 0) == slot).astype(BF16)


def to_strips(row):
    return jnp.concatenate([row[:, i * STRIP : (i + 1) * STRIP] for i in range(8)], axis=0)


def from_strips(strips):
    return jnp.concatenate([strips[i : i + 1] for i in range(8)], axis=1)


def take_tiles(faces, place, codes, t):
    rows = mm(place, t["strip_of"][...]).astype(BF16)
    column = mm(place, t["column_of"][...])
    code = (iota((8, TILES), 0) == codes).astype(BF16)
    code = mm(mm_nt(place, code).astype(BF16), t["code_of"][...])
    parts = [part for face in faces for part in split(face, 3)]
    wide = mm(rows, jnp.concatenate(parts, axis=1))
    tall = jnp.concatenate(
        [(wide[:, i * STRIP : (i + 1) * STRIP] * column).astype(BF16) for i in range(len(parts))],
        axis=0,
    )
    cells = mm(tall, t["inside2"][...])
    out = []
    for i in range(len(parts)):
        one = cells[i * TILES : (i + 1) * TILES]
        out.append((jnp.concatenate([one] * 4, axis=1) * code).astype(BF16))
    return [out[3 * i : 3 * i + 3] for i in range(len(faces))]


def pair_tiles(first, second, table):
    total = None
    for part in (2, 1, 0):
        one = mm(jnp.concatenate([first[part], second[part]], axis=1), table)
        total = one if total is None else total + one
    return total


def pack_kernel(
    names,
    blocks,
    tile_cap,
    parcel_cap,
    bottom_ref,
    top_ref,
    flow_ref,
    diff_ref,
    d_ref,
    low_partner,
    high_partner,
    low_orient,
    high_orient,
    table_ref,
    block_ref,
    cell_ref,
    live_ref,
    *rest,
):
    t = dict(zip(names, rest[: len(names)]))
    out_ref, m_ref = rest[len(names) :]
    me = lax.axis_index("blk")
    d0, d1 = d_ref[0], d_ref[1]
    place_high = place_matrix(high_partner[...], blocks, tile_cap)
    place_low = place_matrix(low_partner[...], blocks, tile_cap)
    top0, top1 = to_strips(top_ref[0, 7:8, :]), to_strips(top_ref[1, 7:8, :])
    low0, low1 = to_strips(bottom_ref[0, 0:1, :]), to_strips(bottom_ref[1, 0:1, :])
    vel, dif = to_strips(flow_ref[0, 0:1, :]), to_strips(diff_ref[0, 0:1, :])
    high = take_tiles([top0, top1, d0 * top0 + d1 * top1], place_high, high_orient[...], t)
    low = take_tiles(
        [low0, low1, vel, dif, d0 * low0 + d1 * low1], place_low, low_orient[...], t
    )
    pairs = [
        pair_tiles(high[0], high[1], t["pair_high"][...]),
        pair_tiles(low[0], low[1], t["pair_low"][...]),
        pair_tiles(low[2], low[3], t["pair_low"][...]),
    ]
    m_ref[4 * blocks : 4 * blocks + TILES, :] = pair_tiles(high[2], low[4], t["pair_mixed"][...])
    rows = table_ref.shape[0]
    target = block_ref[...]
    live = live_ref[...] == 1
    onehot = ((iota((blocks, rows), 0) == target) & live).astype(F32)
    earlier = (iota((rows, rows), 0) < iota((rows, rows), 1)).astype(BF16)
    rank = jnp.sum(onehot * mm(onehot.astype(BF16), earlier), axis=0, keepdims=True)
    rank = rank.astype(jnp.int32)
    slot = jnp.where(live, target * parcel_cap + rank, -1)
    send = (iota((blocks * parcel_cap, rows), 0) == slot).astype(BF16)
    table = split(table_ref[...], 3)
    sent = mm(send, table[2]) + mm(send, table[1]) + mm(send, table[0])
    for b in range(blocks):
        out_ref[b, 0:parcel_cap, :] = sent[b * parcel_cap : (b + 1) * parcel_cap]
        for k in range(PAIRS - 1):
            at = parcel_cap + k * tile_cap
            out_ref[b, at : at + tile_cap, :] = pairs[k][b * tile_cap : (b + 1) * tile_cap]
    pick = (iota((8, PV), 1) == iota((8, PV), 0) + 1).astype(BF16)
    columns = mm_nt(pick, table[2]) + mm_nt(pick, table[1]) + mm_nt(pick, table[0])
    p1, p2 = columns[0:1], columns[1:2]
    soft = jnp.maximum(p1, 0.0) + jnp.log1p(jnp.exp(-jnp.abs(p1)))
    sig = 1.0 / (1.0 + jnp.exp(-p2))
    fields = jnp.concatenate(
        [(cell_ref[...] + 1).astype(F32), soft, sig, jnp.zeros((5, rows), F32)], axis=0
    )
    share = 48 // parcel_cap
    lane = rank + lax.rem(me, share) * parcel_cap + 64 * (lax.div(me, share) & 1)
    goal = jnp.where(live, target * LANES + lane, -1)
    spots = (iota((blocks * LANES, rows), 0) == goal).astype(BF16)
    meta = mm_nt(jnp.concatenate(split(fields, 3), axis=0), spots)
    meta = meta[16:24] + meta[8:16] + meta[0:8]
    for b in range(blocks):
        m_ref[4 * b : 4 * b + 4, :] = meta[0:4, b * LANES : (b + 1) * LANES]


def assemble_kernel(blocks, tile_cap, parcel_cap, buf_ref, m0, m1, m2, m3, out_ref):
    ghost = parcel_cap + (PAIRS - 1) * tile_cap
    z = slice(4 * blocks, 4 * blocks + TILES)
    total = (m0[z, :] + m1[z, :]) + (m2[z, :] + m3[z, :])
    near = m0[0 : 4 * blocks, :] + pltpu.roll(m1[0 : 4 * blocks, :], 64, 1)
    far = m2[0 : 4 * blocks, :] + pltpu.roll(m3[0 : 4 * blocks, :], 64, 1)
    for b in range(blocks):
        out_ref[b, 0:ghost, :] = buf_ref[b, 0:ghost, :]
        out_ref[b, ghost : ghost + tile_cap, :] = total[b * tile_cap : (b + 1) * tile_cap]
        at = ghost + tile_cap
        out_ref[b, at : at + 3, :] = near[4 * b : 4 * b + 3]
        out_ref[b, at + 3 : at + 6, :] = far[4 * b : 4 * b + 3]
        if at + 6 < out_ref.shape[1]:
            out_ref[b, at + 6 :, :] = jnp.zeros((out_ref.shape[1] - at - 6, LANES), F32)


def sum_kernel(own_ref, other_ref, d_ref, e_ref, z_ref, zh_ref, fh_ref):
    half = zh_ref.shape[0]
    core = lax.axis_index("sp") & 1
    z_ref[...] = (
        d_ref[0] * own_ref[0]
        + d_ref[1] * own_ref[1]
        + (e_ref[0] * other_ref[0] + e_ref[1] * other_ref[1])
    )

    @pl.when(core == 0)
    def _():
        zh_ref[...] = z_ref[0:half, :]
        fh_ref[...] = own_ref[0, 0:half, :]

    @pl.when(core == 1)
    def _():
        zh_ref[...] = z_ref[half:, :]
        fh_ref[...] = other_ref[0, half:, :]


def flux(velocity, diffusion, d, upper, lower, weight):
    middle = 0.5 * (upper + lower)
    return velocity * middle - diffusion * (d * (upper - lower) - middle * weight)


def inner_kernel(species_ref, flow_ref, diff_ref, vol_ref, zc_ref, za_ref, zb_ref, d_ref, base_ref, z_ref):
    layers = species_ref.shape[1]
    half = layers // 2
    core = lax.axis_index("sp") & 1
    first = core == 0
    z_ref[0:half, :] = zc_ref[0:half, :] + jnp.where(first, za_ref[...], zb_ref[...])
    z_ref[half:, :] = zc_ref[half:, :] + jnp.where(first, zb_ref[...], za_ref[...])
    shape = (layers, LANES)
    row, lane = iota(shape, 0), iota(shape, 1)
    left = lane < 64
    inner = row > 0
    not_last = row < layers - 1
    off_wall = (lane & 63) != 0
    tiles = FACE // LANES

    def step(i, carry):
        j = tiles - 1 - i
        here = pl.ds(pl.multiple_of(j * LANES, LANES), LANES)
        before = pl.ds(pl.multiple_of(jnp.maximum(j - 1, 0) * LANES, LANES), LANES)
        off_floor = (lane >= 64) | (j > 0)
        z, zb = z_ref[:, here], z_ref[:, before]
        w_layer = z - pltpu.roll(z, 1, 0)
        w_row = z - pltpu.roll(jnp.where(left, z, zb), 64, 1)
        w_column = z - pltpu.roll(z, 1, 1)
        vol = section_step * vol_ref[:, here]
        flows = [flow_ref[k, :, here] for k in range(3)]
        diffs = [diff_ref[k, :, here] for k in range(3)]
        out = []
        for s in range(2):
            y, yb, d = species_ref[s, :, here], species_ref[s, :, before], d_ref[s]
            f_layer = flux(flows[0], diffs[0], d, y, pltpu.roll(y, 1, 0), w_layer)
            f_layer = jnp.where(inner, f_layer, 0.0)
            under = pltpu.roll(jnp.where(left, y, yb), 64, 1)
            f_row = jnp.where(off_floor, flux(flows[1], diffs[1], d, y, under, w_row), 0.0)
            f_col = flux(flows[2], diffs[2], d, y, pltpu.roll(y, 1, 1), w_column)
            f_col = jnp.where(off_wall, f_col, 0.0)
            divergence = (
                (pltpu.roll(f_layer, layers - 1, 0) - f_layer)
                + (pltpu.roll(jnp.where(left, carry[s], f_row), 64, 1) - f_row)
                + (pltpu.roll(f_col, LANES - 1, 1) - f_col)
            )
            base_ref[s, :, here] = y - vol * divergence
            out.append(f_row)
        return tuple(out)

    zero = jnp.zeros(shape, F32)
    lax.fori_loop(0, tiles, step, (zero, zero))


def transposed_parts(get, out_ref, at, parts):
    for g in range(FACE // LANES // 4):
        square = jnp.concatenate([get(4 * g + i) for i in range(4)], axis=0).T
        for k, part in enumerate(split(square, parts)):
            out_ref[at + k * LANES : at + (k + 1) * LANES, g * LANES : (g + 1) * LANES] = part


def velocity_kernel(flow_ref, out_ref):
    for f in range(3):
        transposed_parts(
            lambda j: flow_ref[f, :, j * LANES : (j + 1) * LANES], out_ref, 2 * f * LANES, 2
        )


def fuel_kernel(own_ref, other_ref, fa_ref, fb_ref, out_ref, fuel):
    half = fa_ref.shape[0]
    q = lax.axis_index("sp")

    @pl.when(q == 0)
    def _():
        fuel[...] = own_ref[0]

    @pl.when(q == 1)
    def _():
        fuel[...] = other_ref[0]

    @pl.when(q == 2)
    def _():
        fuel[0:half, :] = fa_ref[...]
        fuel[half:, :] = fb_ref[...]

    @pl.when(q == 3)
    def _():
        fuel[0:half, :] = fb_ref[...]
        fuel[half:, :] = fa_ref[...]

    transposed_parts(lambda j: fuel[:, j * LANES : (j + 1) * LANES], out_ref, 0, 2)


def ghost_faces(pairs, place, t):
    column = mm(place, t["column_of"][...])
    strip = mm(place, t["strip_of"][...])
    parts = []
    for pair, name in pairs:
        for part in split(pair, 3):
            parts.append((mm(part, t[name][...]) * column).astype(BF16))
    wide = lax.dot_general(
        strip.astype(BF16),
        jnp.concatenate(parts, axis=1),
        (((0,), (0,)), ((), ())),
        preferred_element_type=F32,
    )
    wide = [wide[:, i * STRIP : (i + 1) * STRIP] for i in range(len(parts))]
    return [wide[3 * i + 2] + wide[3 * i + 1] + wide[3 * i] for i in range(len(pairs))]


def final_kernel(
    names,
    blocks,
    tile_cap,
    parcel_cap,
    got_ref,
    fuel_ref,
    velocity_ref,
    base_ref,
    species_ref,
    vol_ref,
    z_ref,
    flow_ref,
    diff_ref,
    d_ref,
    low_partner,
    high_partner,
    *rest,
):
    t = dict(zip(names, rest[: len(names)]))
    new_ref, arrived_ref, spots, loads, edge = rest[len(names) :]
    layers = species_ref.shape[1]
    cells = layers * FACE // LANES
    share = 48 // parcel_cap
    groups = blocks // share
    ghost = parcel_cap
    at = parcel_cap + PAIRS * tile_cap

    def pair(k):
        lo = ghost + k * tile_cap
        return jnp.concatenate([got_ref[b, lo : lo + tile_cap, :] for b in range(blocks)], axis=0)

    def meta(f):
        rows = []
        for h in range(2):
            for g in range(groups):
                total = None
                for i in range(share):
                    one = got_ref[g * share + i, at + 3 * h + f : at + 3 * h + f + 1, :]
                    total = one if total is None else total + one
                rows.append(total)
        return jnp.concatenate(rows, axis=0)

    chunks = 2 * groups
    number = meta(0).astype(jnp.int32) - 1
    soft, sig = meta(1), meta(2)
    cell_layer = lax.shift_right_arithmetic(number, 12)
    cell_row = (lax.shift_right_arithmetic(number, 7) & 31) * layers + cell_layer
    cell_row = jnp.where(number >= 0, cell_row, -1)
    cell_lane = number & (LANES - 1)
    sublane = iota((LANES, LANES), 0)
    tall = iota((cells, LANES), 0)
    for c in range(chunks):
        spots[:, c * LANES : (c + 1) * LANES] = (tall == cell_row[c : c + 1]).astype(BF16)
    place_low = place_matrix(low_partner[...], blocks, tile_cap)
    place_high = place_matrix(high_partner[...], blocks, tile_cap)
    p0, p1, p2, p3 = (pair(k) for k in range(PAIRS))
    below0, below1, below_z = ghost_faces(
        [(p0, "spread_first"), (p0, "spread_second"), (p3, "spread_first")], place_low, t
    )
    above0, above1, top_v, top_d, above_z = ghost_faces(
        [
            (p1, "spread_first"),
            (p1, "spread_second"),
            (p2, "spread_first"),
            (p2, "spread_second"),
            (p3, "spread_second"),
        ],
        place_high,
        t,
    )
    z_bottom = to_strips(z_ref[0:1, :])
    z_top = to_strips(z_ref[layers - 1 : layers, :])
    bottom_v, bottom_d = to_strips(flow_ref[0, 0:1, :]), to_strips(diff_ref[0, 0:1, :])
    for s, (below, above) in enumerate(((below0, above0), (below1, above1))):
        low = to_strips(species_ref[s, 0:1, :])
        high = to_strips(species_ref[s, layers - 1 : layers, :])
        f_low = flux(bottom_v, bottom_d, d_ref[s], low, below, z_bottom - below_z)
        f_high = flux(top_v, top_d, d_ref[s], above, high, above_z - z_top)
        edge[2 * s : 2 * s + 1, :] = from_strips(f_low)
        edge[2 * s + 1 : 2 * s + 2, :] = from_strips(f_high)
    width = 2 * LANES
    lefts = iota((1, LANES), 1) < 64
    evaporated = []
    for c in range(0, chunks, 2):
        both = mm(fuel_ref[...], spots[:, c * LANES : c * LANES + width])
        both = both[0:LANES] + both[LANES:]
        for i in range(2):
            mask = sublane == cell_lane[c + i : c + i + 1]
            fuel = jnp.sum(
                jnp.where(mask, both[:, i * LANES : (i + 1) * LANES], 0.0), axis=0, keepdims=True
            )
            gone = soft[c + i : c + i + 1] * (sig[c + i : c + i + 1] - fuel)
            evaporated.append(gone)
            for k, part in enumerate(split(jnp.where(mask, gone, 0.0), 2)):
                loads[k * LANES : (k + 1) * LANES, (c + i) * LANES : (c + i + 1) * LANES] = part
    column = iota((8, PV), 1)
    index = iota((8, PV), 0)
    target = ((index == 0) & (column == 0)) | (
        (index >= 1) & (index <= 3) & (column == index + 2)
    )
    target = target.astype(F32)
    drag = (iota((parcel_cap * share, PV), 1) >= 3) & (iota((parcel_cap * share, PV), 1) <= 5)
    keep = jnp.where(drag, 1.0 - friction_timescale, 1.0)
    for h in range(groups // 2):
        a, b = 2 * h, 2 * h + 1
        own = jnp.where(
            iota((cells, LANES), 1) < 64,
            spots[:, a * LANES : (a + 1) * LANES].astype(F32),
            spots[:, b * LANES : (b + 1) * LANES].astype(F32),
        ).astype(BF16)
        mask = sublane == jnp.where(lefts, cell_lane[a : a + 1], cell_lane[b : b + 1])
        u = mm(velocity_ref[...], own)
        rows = [-jnp.where(lefts, evaporated[a], evaporated[b])]
        for f in range(3):
            field = u[2 * f * LANES : (2 * f + 1) * LANES] + u[(2 * f + 1) * LANES : (2 * f + 2) * LANES]
            rows.append(
                friction_timescale * jnp.sum(jnp.where(mask, field, 0.0), axis=0, keepdims=True)
            )
        rows.append(jnp.zeros((4, LANES), F32))
        change = lax.dot_general(
            jnp.concatenate(rows, axis=0),
            target,
            (((0,), (0,)), ((), ())),
            precision=lax.Precision.HIGHEST,
            preferred_element_type=F32,
        )
        for i in range(2):
            g = 2 * h + i
            size = share * parcel_cap
            table = jnp.concatenate(
                [got_ref[g * share + k, 0:parcel_cap, :] for k in range(share)], axis=0
            )
            arrived_ref[g * size : (g + 1) * size, :] = table * keep + change[64 * i : 64 * i + size]
    source = mm_nt(spots[...], loads[...])
    source = source[:, 0:LANES] + source[:, LANES:]
    row = iota((layers, LANES), 0)
    fuel_group = jnp.where(lax.axis_index("sp") == 0, 1.0, 0.0)
    for j in range(FACE // LANES):
        here = slice(j * LANES, (j + 1) * LANES)
        vol = section_step * vol_ref[:, here]
        here_source = source[j * layers : (j + 1) * layers]
        for s in range(2):
            y = species_ref[s, :, here]
            delta = fuel_group if s == 0 else 0.0
            term = here_source * (delta - y)
            term = term + jnp.where(row == 0, edge[2 * s : 2 * s + 1, here], 0.0)
            term = term - jnp.where(row == layers - 1, edge[2 * s + 1 : 2 * s + 2, here], 0.0)
            new_ref[s, :, here] = base_ref[s, :, here] + vol * term


def whole(memory=pltpu.VMEM):
    return pl.BlockSpec(memory_space=memory)


def part(shape, index):
    return pl.BlockSpec(shape, lambda i: index)


def params(semantics=None):
    return pltpu.CompilerParams(vmem_limit_bytes=VMEM_LIMIT)


def body(
    species,
    interface_normal_flow,
    face_diffusion,
    inv_volume,
    diffusivity,
    low_partner,
    high_partner,
    low_orient,
    high_orient,
    droplet_table,
    parcel_block,
    parcel_cell,
    parcel_live,
):
    blocks = lax.axis_size("blk")
    local_species, layers, cells = species.shape
    parcels = droplet_table.shape[0]
    tile_cap = max(1, TILES // blocks)
    parcel_cap = 3 * parcels // (2 * blocks)
    last = layers // 8 - 1
    constants = tables()

    def use(*names):
        return names, [jnp.asarray(constants[n].astype(ml_dtypes.bfloat16)) for n in names]

    def swap(value, bit):
        return lax.ppermute(value, "sp", [(i, i ^ bit) for i in range(lax.axis_size("sp"))])

    other_species = swap(species, 1)
    other_diffusivity = swap(diffusivity, 1)

    names, values = use(
        "strip_of", "column_of", "inside2", "code_of", "pair_high", "pair_low", "pair_mixed"
    )
    rows = -(-(parcel_cap + PAIRS * tile_cap + 6) // 8) * 8
    meta_rows = 4 * blocks + TILES
    face = (1, 8, cells)

    def full(a):
        return pl.BlockSpec(a.shape, lambda i: (0,) * a.ndim)

    small = [low_partner, high_partner, low_orient, high_orient, droplet_table]
    small += [parcel_block.reshape(1, parcels), parcel_cell.reshape(1, parcels)]
    small += [parcel_live.reshape(1, parcels)] + values
    packed, m0 = pl.pallas_call(
        functools.partial(pack_kernel, names, blocks, tile_cap, parcel_cap),
        grid=(1,),
        out_shape=(
            jax.ShapeDtypeStruct((blocks, rows, LANES), F32),
            jax.ShapeDtypeStruct((meta_rows, LANES), F32),
        ),
        in_specs=[
            part((local_species, 8, cells), (0, 0, 0)),
            part((local_species, 8, cells), (0, last, 0)),
            part(face, (0, 0, 0)),
            part(face, (0, 0, 0)),
            whole(pltpu.SMEM),
        ]
        + [full(a) for a in small],
        out_specs=(
            pl.BlockSpec((blocks, rows, LANES), lambda i: (0, 0, 0)),
            pl.BlockSpec((meta_rows, LANES), lambda i: (0, 0)),
        ),
        compiler_params=params(),
        name="pack",
    )(species, species, interface_normal_flow, face_diffusion, diffusivity, *small)
    m1, m2, m3 = swap(m0, 1), swap(m0, 2), swap(m0, 3)

    z_chip, z_half, fuel_half = pl.pallas_call(
        sum_kernel,
        out_shape=(
            jax.ShapeDtypeStruct((layers, cells), F32),
            jax.ShapeDtypeStruct((layers // 2, cells), F32),
            jax.ShapeDtypeStruct((layers // 2, cells), F32),
        ),
        in_specs=[whole(), whole(), whole(pltpu.SMEM), whole(pltpu.SMEM)],
        out_specs=(whole(), whole(), whole()),
        compiler_params=params(),
        name="chip_sum",
    )(species, other_species, diffusivity, other_diffusivity)
    z_far = swap(z_half, 2)
    fuel_far = swap(fuel_half, 2)
    z_far_other = swap(z_far, 1)
    fuel_far_other = swap(fuel_far, 1)

    ready = pl.pallas_call(
        functools.partial(assemble_kernel, blocks, tile_cap, parcel_cap),
        out_shape=jax.ShapeDtypeStruct((blocks, rows, LANES), F32),
        in_specs=[whole()] * 5,
        out_specs=whole(),
        compiler_params=params(),
        name="assemble",
    )(packed, m0, m1, m2, m3)
    got = lax.all_to_all(ready, "blk", split_axis=0, concat_axis=0, tiled=True)

    velocity_parts = pl.pallas_call(
        velocity_kernel,
        out_shape=jax.ShapeDtypeStruct((6 * LANES, layers * cells // LANES), BF16),
        in_specs=[whole()],
        out_specs=whole(),
        compiler_params=params(),
        name="velocity_parts",
    )(interface_normal_flow)

    base, z_total = pl.pallas_call(
        inner_kernel,
        out_shape=(
            jax.ShapeDtypeStruct(species.shape, F32),
            jax.ShapeDtypeStruct((layers, cells), F32),
        ),
        in_specs=[whole()] * 7 + [whole(pltpu.SMEM)],
        out_specs=(whole(), whole()),
        compiler_params=params(),
        name="inner_flux",
    )(species, interface_normal_flow, face_diffusion, inv_volume, z_chip, z_far, z_far_other, diffusivity)

    fuel_parts = pl.pallas_call(
        fuel_kernel,
        out_shape=jax.ShapeDtypeStruct((2 * LANES, layers * cells // LANES), BF16),
        in_specs=[whole()] * 4,
        out_specs=whole(),
        scratch_shapes=[pltpu.VMEM((layers, cells), F32)],
        compiler_params=params(),
        name="fuel_parts",
    )(species, other_species, fuel_far, fuel_far_other)

    names, values = use("strip_of", "column_of", "spread_first", "spread_second")
    groups = blocks * parcel_cap // 48
    small = [low_partner, high_partner] + values
    return pl.pallas_call(
        functools.partial(final_kernel, names, blocks, tile_cap, parcel_cap),
        grid=(1,),
        out_shape=(
            jax.ShapeDtypeStruct(species.shape, F32),
            jax.ShapeDtypeStruct((blocks * parcel_cap, PV), F32),
        ),
        in_specs=[full(got), full(fuel_parts), full(velocity_parts), full(base), full(species)]
        + [full(inv_volume), full(z_total), part(face, (0, 0, 0)), part(face, (0, 0, 0))]
        + [whole(pltpu.SMEM)]
        + [full(a) for a in small],
        out_specs=(
            pl.BlockSpec(species.shape, lambda i: (0, 0, 0)),
            pl.BlockSpec((blocks * parcel_cap, PV), lambda i: (0, 0)),
        ),
        scratch_shapes=[
            pltpu.VMEM((layers * cells // LANES, 2 * groups * LANES), BF16),
            pltpu.VMEM((2 * LANES, 2 * groups * LANES), BF16),
            pltpu.VMEM((8, cells), F32),
        ],
        compiler_params=params(),
        name="final",
    )(
        got,
        fuel_parts,
        velocity_parts,
        base,
        species,
        inv_volume,
        z_total,
        interface_normal_flow,
        face_diffusion,
        diffusivity,
        *small,
    )


def solution(mesh):
    placed = (
        P("sp", "blk", None),
        P(None, "blk", None),
        P(None, "blk", None),
        P("blk", None),
        P("sp"),
        P("blk", None),
        P("blk", None),
        P("blk", None),
        P("blk", None),
        P(("blk", "sp"), None),
        P(("blk", "sp"), None),
        P(("blk", "sp")),
        P(("blk", "sp")),
    )
    return jax.shard_map(
        body,
        mesh=mesh,
        in_specs=placed,
        out_specs=(P("sp", "blk", None), P(("blk", "sp"), None)),
        check_vma=False,
    )
```

```python
import functools

import jax
import jax.numpy as jnp
from jax import lax
from jax.experimental import pallas as pl
from jax.experimental.pallas import tpu as pltpu
from jax.sharding import PartitionSpec as P

PV = 128
BJ = 64
BK = 64
TILE_SIDE = 8
TILES = 64
LANES = 128
FACE = BJ * BK
STRIP = TILE_SIDE * BK
PAIRS = 4

section_step = 0.5
friction_timescale = 0.3

F32 = jnp.float32
BF16 = jnp.bfloat16
VMEM_LIMIT = 16 * 1024 * 1024


def iota(shape, dim):
    return lax.broadcasted_iota(jnp.int32, shape, dim)


def mm(a, b):
    return lax.dot_general(a, b, (((1,), (0,)), ((), ())), preferred_element_type=F32)


def mm_nt(a, b):
    return lax.dot_general(a, b, (((1,), (1,)), ((), ())), preferred_element_type=F32)


def mm_tn(a, b):
    return lax.dot_general(a, b, (((0,), (0,)), ((), ())), preferred_element_type=F32)


def ones(condition, kind=BF16):
    return jnp.where(condition, 1.0, 0.0).astype(kind)


def split(value, parts):
    out = []
    for _ in range(parts - 1):
        head = value.astype(BF16)
        out.append(head)
        value = value - head.astype(F32)
    out.append(value.astype(BF16))
    return out


def inside_table():
    lane, cell = iota((STRIP, LANES), 0), iota((STRIP, LANES), 1) & 63
    return ones(((lane >> 6) == (cell >> 3)) & ((lane & 7) == (cell & 7)))


def orient_table():
    shape = (8 * TILES, LANES)
    code, source = iota(shape, 0) >> 6, iota(shape, 0) & 63
    column = iota(shape, 1)
    r, c = (column >> 3) & 7, column & 7
    back = column >= 64
    turned = code >= 4
    flip_r, flip_c = (code & 1) * 7, ((code >> 1) & 1) * 7
    there = jnp.where(turned, (c ^ flip_c) * 8 + (r ^ flip_r), (r ^ flip_r) * 8 + (c ^ flip_c))
    r0, c0 = jnp.where(turned, c, r), jnp.where(turned, r, c)
    return ones(source == jnp.where(back, (r0 ^ flip_r) * 8 + (c0 ^ flip_c), there))


def place_matrix(partner, blocks, cap):
    onehot = ones(iota((blocks, TILES), 0) == partner, F32)
    earlier = ones(iota((TILES, TILES), 0) < iota((TILES, TILES), 1))
    rank = jnp.sum(onehot * mm(onehot.astype(BF16), earlier), axis=0, keepdims=True)
    slot = partner * cap + rank.astype(jnp.int32)
    return ones(iota((TILES, TILES), 0) == slot)


def to_strips(row):
    return jnp.concatenate([row[:, i * STRIP : (i + 1) * STRIP] for i in range(8)], axis=0)


def from_strips(strips):
    return jnp.concatenate([strips[i : i + 1] for i in range(8)], axis=1)


def take_tiles(faces, strip, column, code, inside):
    parts = [part for face in faces for part in split(face, 3)]
    wide = mm(strip, jnp.concatenate(parts, axis=1))
    tall = jnp.concatenate(
        [(wide[:, i * STRIP : (i + 1) * STRIP] * column).astype(BF16) for i in range(len(parts))],
        axis=0,
    )
    cells = mm(tall, inside)
    out = []
    for i in range(len(parts)):
        one = cells[i * TILES : (i + 1) * TILES]
        out.append((jnp.concatenate([one] * 4, axis=1) * code).astype(BF16))
    return out


def turn_tiles(tiles, table):
    turned = mm(jnp.concatenate(tiles, axis=0), table)
    turned = [turned[i * TILES : (i + 1) * TILES] for i in range(len(tiles))]
    return [turned[i + 2] + turned[i + 1] + turned[i] for i in range(0, len(tiles), 3)]


def begin(copies, sems):
    started = [pltpu.make_async_copy(a, b, sems.at[i]) for i, (a, b) in enumerate(copies)]
    for one in started:
        one.start()
    return started


def pack_rows_kernel(
    blocks,
    tile_cap,
    parcel_cap,
    species,
    flow,
    diff,
    low_partner,
    high_partner,
    low_orient,
    high_orient,
    table,
    block,
    live,
    out_ref,
    strips_ref,
    edge_ref,
    strip_ref,
    column_ref,
    code_ref,
    rank_ref,
    bottom,
    top,
    vel_in,
    dif_in,
    small,
    table_in,
    parcel,
    sems,
):
    layers = species.shape[1]
    copies = begin(
        [(high_partner, small.at[0]), (low_partner, small.at[1])]
        + [(high_orient, small.at[2]), (low_orient, small.at[3])]
        + [(block, parcel.at[0]), (live, parcel.at[1]), (table, table_in)]
        + [(species.at[:, layers - 8 :], top), (species.at[:, 0:8], bottom)]
        + [(flow.at[0, 0:8], vel_in), (diff.at[0, 0:8], dif_in)],
        sems,
    )
    inside, turn = inside_table(), orient_table()
    tile = iota((TILES, STRIP), 0)
    strip_of = ones((iota((TILES, LANES), 0) >> 3) == iota((TILES, LANES), 1))
    column_of = ones((tile & 7) == ((iota((TILES, STRIP), 1) >> 3) & 7))
    code_of = ones(iota((8, STRIP), 0) == (iota((8, STRIP), 1) >> 6))
    rows = table.shape[0]
    earlier = ones(iota((rows, rows), 0) < iota((rows, rows), 1))
    for copy in copies[0:4]:
        copy.wait()
    for k in range(2):
        place = place_matrix(small[k], blocks, tile_cap)
        strip_ref[k] = mm(place, strip_of)
        column_ref[k] = mm(place, column_of)
        code = ones(iota((8, TILES), 0) == small[2 + k])
        code_ref[k] = mm(mm_nt(place, code).astype(BF16), code_of)
    for copy in copies[4:7]:
        copy.wait()
    target = parcel[0]
    alive = parcel[1] == 1
    onehot = ones((iota((blocks, rows), 0) == target) & alive, F32)
    rank = jnp.sum(onehot * mm(onehot.astype(BF16), earlier), axis=0, keepdims=True)
    rank = rank.astype(jnp.int32)
    rank_ref[...] = jnp.broadcast_to(jnp.where(alive, rank, -1), (8, rows))
    slot = jnp.where(alive, target * parcel_cap + rank, -1)
    send = ones(iota((blocks * parcel_cap, rows), 0) == slot)
    parts = split(table_in[...], 3)
    sent = mm(send, parts[2]) + mm(send, parts[1]) + mm(send, parts[0])
    for copy in copies[7:]:
        copy.wait()
    top0, top1 = to_strips(top[0, 7:8, :]), to_strips(top[1, 7:8, :])
    low0, low1 = to_strips(bottom[0, 0:1, :]), to_strips(bottom[1, 0:1, :])
    strips_ref[...] = jnp.concatenate([top0, top1, low0, low1], axis=0)
    vel, dif = to_strips(vel_in[0:1, :]), to_strips(dif_in[0:1, :])
    edge_ref[...] = jnp.concatenate([vel, dif], axis=0)
    tiles = []
    for k, some in enumerate(([top0, top1], [low0, low1, vel, dif])):
        strip = strip_ref[k][:, 0:8].astype(BF16)
        tiles += take_tiles(some, strip, column_ref[k], code_ref[k], inside)
    high0, high1, low0, low1, vel, dif = turn_tiles(tiles, turn)
    left = iota((TILES, LANES), 1) < 64
    pairs = [
        jnp.where(left, high0, pltpu.roll(high1, 64, 1)),
        jnp.where(left, pltpu.roll(low0, 64, 1), low1),
        jnp.where(left, pltpu.roll(vel, 64, 1), dif),
    ]
    for b in range(blocks):
        out_ref[b, 0:parcel_cap, :] = sent[b * parcel_cap : (b + 1) * parcel_cap]
        for k in range(PAIRS - 1):
            at = parcel_cap + k * tile_cap
            out_ref[b, at : at + tile_cap, :] = pairs[k][b * tile_cap : (b + 1) * tile_cap]


def pack_meta_kernel(
    blocks,
    parcel_cap,
    factors,
    table,
    block,
    cell,
    strips_ref,
    strip_ref,
    column_ref,
    code_ref,
    rank_ref,
    z_half,
    m_ref,
    d_own,
    table_in,
    parcel,
    sems,
):
    copies = begin(
        [(table, table_in), (block, parcel.at[0]), (cell, parcel.at[1]), (factors, d_own)], sems
    )
    rows = table.shape[0]
    me = lax.axis_index("blk")
    inside, turn = inside_table(), orient_table()
    pick = ones(iota((8, PV), 1) == iota((8, PV), 0) + 1)
    for copy in copies:
        copy.wait()
    d0, d1 = d_own[0:1, 0:1], d_own[0:1, 1:2]
    tiles = []
    for k in range(2):
        strip = strip_ref[k][:, 0:8].astype(BF16)
        face = d0 * strips_ref[16 * k : 16 * k + 8, :] + d1 * strips_ref[16 * k + 8 : 16 * k + 16, :]
        tiles += take_tiles([face], strip, column_ref[k], code_ref[k], inside)
    high, low = turn_tiles(tiles, turn)
    lanes = iota((1, LANES), 1)
    m_ref[4 * blocks : 4 * blocks + TILES, :] = jnp.where(lanes < 64, high, low)
    parts = split(table_in[...], 3)
    columns = mm_nt(pick, parts[2]) + mm_nt(pick, parts[1]) + mm_nt(pick, parts[0])
    p1, p2 = columns[0:1], columns[1:2]
    soft = jnp.maximum(p1, 0.0) + jnp.log1p(jnp.exp(-jnp.abs(p1)))
    sig = 1.0 / (1.0 + jnp.exp(-p2))
    fields = jnp.concatenate(
        [(parcel[1] + 1).astype(F32), soft, sig, jnp.zeros((5, rows), F32)], axis=0
    )
    rank = rank_ref[0:1, :]
    share = 48 // parcel_cap
    lane = rank + lax.rem(me, share) * parcel_cap + 64 * (lax.div(me, share) & 1)
    goal = jnp.where(rank >= 0, parcel[0] * LANES + lane, -1)
    spots = ones(iota((blocks * LANES, rows), 0) == goal)
    meta = mm_nt(jnp.concatenate(split(fields, 3), axis=0), spots)
    meta = meta[16:24] + meta[8:16] + meta[0:8]
    own = jnp.where(lanes == 0, d0, jnp.where(lanes == 1, d1, 0.0))
    for b in range(blocks):
        m_ref[4 * b : 4 * b + 3, :] = meta[0:3, b * LANES : (b + 1) * LANES]
        m_ref[4 * b + 3 : 4 * b + 4, :] = own


def assemble_kernel(
    blocks, tile_cap, parcel_cap, buf_ref, m0, m1, m2, m3, z_near, z_far, out_ref, z_ref
):
    z_ref[...] = z_near[...] + z_far[...]
    ghost = parcel_cap + (PAIRS - 1) * tile_cap
    z = slice(4 * blocks, 4 * blocks + TILES)
    total = (m0[z, :] + m1[z, :]) + (m2[z, :] + m3[z, :])
    near = m0[0 : 4 * blocks, :] + pltpu.roll(m1[0 : 4 * blocks, :], 64, 1)
    far = m2[0 : 4 * blocks, :] + pltpu.roll(m3[0 : 4 * blocks, :], 64, 1)
    for b in range(blocks):
        out_ref[b, 0:ghost, :] = buf_ref[b, 0:ghost, :]
        out_ref[b, ghost : ghost + tile_cap, :] = total[b * tile_cap : (b + 1) * tile_cap]
        at = ghost + tile_cap
        out_ref[b, at : at + 3, :] = near[4 * b : 4 * b + 3]
        out_ref[b, at + 3 : at + 6, :] = far[4 * b : 4 * b + 3]
        if at + 6 < out_ref.shape[1]:
            out_ref[b, at + 6 :, :] = jnp.zeros((out_ref.shape[1] - at - 6, LANES), F32)


def sum_kernel(
    species, other_ref, factors, d_other, strip, zh_ref, fh_ref, own_ref, d_own, sems
):
    half, cells = zh_ref.shape
    quarter = cells // 4
    parts = [slice(i * quarter, (i + 1) * quarter) for i in range(4)]
    copies = begin(
        [(factors, d_own)] + [(species.at[:, :, p], own_ref.at[:, :, p]) for p in parts], sems
    )
    first = (lax.axis_index("sp") & 1) == 0
    copies[0].wait()
    d0, d1, e0, e1 = d_own[0:1, 0:1], d_own[0:1, 1:2], d_other[0:1, 0:1], d_other[0:1, 1:2]
    for copy, p in zip(copies[1:], parts):
        copy.wait()
        for lo in range(p.start, p.stop, LANES):
            at = slice(lo, lo + LANES)
            own, other = own_ref[0, :, at], other_ref[0, :, at]
            z = d0 * own + d1 * own_ref[1, :, at] + (e0 * other + e1 * other_ref[1, :, at])
            zh_ref[:, at] = jnp.where(first, z[0:half], z[half:])
            fh_ref[:, at] = jnp.where(first, own[0:half], other[half:])


def flux(velocity, diffusion, d, upper, lower, weight):
    middle = 0.5 * (upper + lower)
    return velocity * middle - diffusion * (d * (upper - lower) - middle * weight)


def transposed_parts(get, out_ref, at, parts, group):
    square = jnp.concatenate([get(4 * group + i) for i in range(4)], axis=0).T
    for k, part in enumerate(split(square, parts)):
        out_ref[at + k * LANES : at + (k + 1) * LANES, group * LANES : (group + 1) * LANES] = part


def inner_kernel(
    flow,
    diff,
    vol,
    species,
    za_ref,
    zb_ref,
    m0,
    base_ref,
    edge_ref,
    flow_ref,
    diff_ref,
    vol_ref,
    species_ref,
    z_ref,
    sems,
):
    layers, cells = vol.shape
    half = layers // 2
    quarter = cells // 4
    parts = [slice(i * quarter, (i + 1) * quarter) for i in range(4)]
    copies = {}
    for n, i in enumerate((3, 2, 1, 0)):
        p = parts[i]
        copies[i] = begin(
            [
                (flow.at[:, :, p], flow_ref.at[:, :, p]),
                (diff.at[:, :, p], diff_ref.at[:, :, p]),
                (vol.at[:, p], vol_ref.at[:, p]),
                (species.at[:, :, p], species_ref.at[:, :, p]),
            ],
            sems.at[n],
        )
    first = (lax.axis_index("sp") & 1) == 0
    z_ref[0:half, :] = jnp.where(first, za_ref[...], zb_ref[...])
    z_ref[half:, :] = jnp.where(first, zb_ref[...], za_ref[...])
    shape = (layers, LANES)
    row, lane = iota(shape, 0), iota(shape, 1)
    left = lane < 64
    inner = row > 0
    off_wall = (lane & 63) != 0
    ds = (m0[3:4, 0:1], m0[3:4, 1:2])
    above = [jnp.zeros(shape, F32)] * 2
    for j in range(cells // LANES - 1, -1, -1):
        here = slice(j * LANES, (j + 1) * LANES)
        before = slice(max(j - 1, 0) * LANES, (max(j - 1, 0) + 1) * LANES)
        if here.stop % quarter == 0:
            for copy in copies[here.start // quarter][0:3]:
                copy.wait()
            if j == cells // LANES - 1:
                copies[here.start // quarter][3].wait()
        if here.start % quarter == 0 and j > 0:
            copies[before.start // quarter][3].wait()
        z = z_ref[:, here]
        unders = (
            lambda y: pltpu.roll(y, 1, 0),
            lambda y: pltpu.roll(y, 64, 1),
            lambda y: pltpu.roll(y, 1, 1),
        )
        z_under = (
            pltpu.roll(z, 1, 0),
            pltpu.roll(jnp.where(left, z, z_ref[:, before]), 64, 1),
            pltpu.roll(z, 1, 1),
        )
        masks = (inner, (lane >= 64) if j == 0 else None, off_wall)
        means, slopes = [], []
        for k in range(3):
            g = diff_ref[k, :, here]
            c = 0.5 * (flow_ref[k, :, here] + g * (z - z_under[k]))
            if masks[k] is not None:
                c, g = jnp.where(masks[k], c, 0.0), jnp.where(masks[k], g, 0.0)
            means.append(c)
            slopes.append(g)
        scale = section_step * vol_ref[:, here]
        for s in range(2):
            y = species_ref[s, :, here]
            under = (
                pltpu.roll(y, 1, 0),
                pltpu.roll(jnp.where(left, y, species_ref[s, :, before]), 64, 1),
                pltpu.roll(y, 1, 1),
            )
            f_layer, f_row, f_column = (
                (y + u) * c - (y - u) * (g * ds[s]) for u, c, g in zip(under, means, slopes)
            )
            divergence = (
                (pltpu.roll(f_layer, layers - 1, 0) - f_layer)
                + (pltpu.roll(jnp.where(left, above[s], f_row), 64, 1) - f_row)
                + (pltpu.roll(f_column, LANES - 1, 1) - f_column)
            )
            base_ref[s, :, here] = y - scale * divergence
            above[s] = f_row
    ends = [ref[i : i + 1, :] for ref in (z_ref, vol_ref) for i in (0, layers - 1)]
    edge_ref[...] = jnp.concatenate([to_strips(end) for end in ends], axis=0)


def fuel_half_kernel(near_ref, far_ref, edge_ref, out_ref):
    out_ref[...] = jnp.where(lax.axis_index("sp") < 2, near_ref[...], far_ref[...])


def fuel_kernel(own_ref, other_ref, out_ref):
    first = (lax.axis_index("sp") & 1) == 0

    def field(j):
        here = slice(j * LANES, (j + 1) * LANES)
        a, b = own_ref[:, here], other_ref[:, here]
        return jnp.concatenate([jnp.where(first, a, b), jnp.where(first, b, a)], axis=0)

    for group in range(FACE // LANES // 4):
        transposed_parts(field, out_ref, 0, 2, group)


def ghost_faces(pairs, strip, column, inside):
    lane = iota((TILES, LANES), 1)
    parts = []
    for pair, right in pairs:
        one = jnp.where((lane >= 64) if right else (lane < 64), pair, 0.0)
        parts += split(one, 3)
    wide = mm_nt(jnp.concatenate(parts, axis=0), inside)
    wide = [
        (wide[i * TILES : (i + 1) * TILES] * column).astype(BF16) for i in range(len(parts))
    ]
    wide = mm_tn(strip, jnp.concatenate(wide, axis=1))
    wide = [wide[:, i * STRIP : (i + 1) * STRIP] for i in range(len(parts))]
    return [wide[3 * i + 2] + wide[3 * i + 1] + wide[3 * i] for i in range(len(pairs))]


def final_kernel(
    blocks,
    tile_cap,
    parcel_cap,
    got_ref,
    fuel_ref,
    base_ref,
    species,
    vol,
    flow,
    zedge_ref,
    fedge_ref,
    strips_ref,
    strip_ref,
    column_ref,
    m0,
    new_hbm,
    arrived_hbm,
    new_ref,
    arrived_ref,
    spots,
    loads,
    edge,
    species_ref,
    vol_ref,
    flow_ref,
    number_ref,
    number_smem,
    rows_ref,
    sems,
    flow_sem,
    number_sem,
):
    layers, cells = base_ref.shape[1:]
    fetch = begin([(species, species_ref), (vol, vol_ref)], sems.at[1])
    fetch_flow = begin(
        [
            (flow.at[:, :, j * LANES : (j + 1) * LANES], flow_ref.at[:, j * layers : (j + 1) * layers])
            for j in range(cells // LANES)
        ],
        flow_sem,
    )
    tall_rows = layers * cells // LANES
    share = 48 // parcel_cap
    groups = blocks // share
    ghost = parcel_cap
    at = parcel_cap + PAIRS * tile_cap

    def pair(k):
        lo = ghost + k * tile_cap
        return jnp.concatenate([got_ref[b, lo : lo + tile_cap, :] for b in range(blocks)], axis=0)

    def meta(f):
        rows = []
        for h in range(2):
            for g in range(groups):
                total = None
                for i in range(share):
                    one = got_ref[g * share + i, at + 3 * h + f : at + 3 * h + f + 1, :]
                    total = one if total is None else total + one
                rows.append(total)
        return jnp.concatenate(rows, axis=0)

    chunks = 2 * groups
    number = meta(0).astype(jnp.int32) - 1
    soft, sig = meta(1), meta(2)
    cell_layer = lax.shift_right_arithmetic(number, 12)
    cell_row = (lax.shift_right_arithmetic(number, 7) & 31) * layers + cell_layer
    cell_row = jnp.where(number >= 0, cell_row, -1)
    number_ref[...] = jnp.maximum(cell_row, 0)
    fetch_number = pltpu.make_async_copy(number_ref, number_smem, number_sem)
    fetch_number.start()
    cell_lane = number & (LANES - 1)
    sublane = iota((LANES, LANES), 0)
    tall = iota((tall_rows, LANES), 0)
    for c in range(chunks):
        spots[:, c * LANES : (c + 1) * LANES] = ones(tall == cell_row[c : c + 1])
    inside = inside_table()
    p0, p1, p2, p3 = (pair(k) for k in range(PAIRS))
    below0, below1, below_z = ghost_faces(
        [(p0, 0), (p0, 1), (p3, 0)], strip_ref[1].astype(BF16)[:, 0:8], column_ref[1], inside
    )
    above0, above1, top_v, top_d, above_z = ghost_faces(
        [(p1, 0), (p1, 1), (p2, 0), (p2, 1), (p3, 1)],
        strip_ref[0].astype(BF16)[:, 0:8],
        column_ref[0],
        inside,
    )
    z_bottom, z_top = zedge_ref[0:8, :], zedge_ref[8:16, :]
    bottom_scale, top_scale = section_step * zedge_ref[16:24, :], section_step * zedge_ref[24:32, :]
    bottom_v, bottom_d = fedge_ref[0:8, :], fedge_ref[8:16, :]
    for s, (below, above) in enumerate(((below0, above0), (below1, above1))):
        d = m0[3:4, s : s + 1]
        high = strips_ref[8 * s : 8 * s + 8, :]
        low = strips_ref[16 + 8 * s : 24 + 8 * s, :]
        f_low = flux(bottom_v, bottom_d, d, low, below, z_bottom - below_z)
        f_high = flux(top_v, top_d, d, above, high, above_z - z_top)
        edge[2 * s : 2 * s + 1, :] = from_strips(bottom_scale * f_low)
        edge[2 * s + 1 : 2 * s + 2, :] = from_strips(top_scale * f_high)
    width = 2 * LANES
    lefts = iota((1, LANES), 1) < 64
    evaporated = []
    for c in range(0, chunks, 2):
        both = mm(fuel_ref[...], spots[:, c * LANES : c * LANES + width])
        both = both[0:LANES] + both[LANES:]
        for i in range(2):
            mask = sublane == cell_lane[c + i : c + i + 1]
            fuel = jnp.sum(
                jnp.where(mask, both[:, i * LANES : (i + 1) * LANES], 0.0), axis=0, keepdims=True
            )
            gone = soft[c + i : c + i + 1] * (sig[c + i : c + i + 1] - fuel)
            evaporated.append(gone)
            for k, part in enumerate(split(jnp.where(mask, gone, 0.0), 2)):
                loads[k * LANES : (k + 1) * LANES, (c + i) * LANES : (c + i + 1) * LANES] = part
    source = mm_nt(spots[...], loads[...])
    source = source[:, 0:LANES] + source[:, LANES:]
    row = iota((8, LANES), 0)
    delta = (jnp.where(lax.axis_index("sp") == 0, 1.0, 0.0), 0.0)
    for copy in fetch:
        copy.wait()
    quarter = cells // 4
    copies = []
    for j in range(cells // LANES):
        here = slice(j * LANES, (j + 1) * LANES)
        part = source[j * layers : (j + 1) * layers] * (section_step * vol_ref[:, here])
        for s in range(2):
            new = base_ref[s, :, here] + part * (delta[s] - species_ref[s, :, here])
            first = jnp.where(row == 0, edge[2 * s : 2 * s + 1, here], 0.0)
            last = jnp.where(row == 7, edge[2 * s + 1 : 2 * s + 2, here], 0.0)
            new_ref[s, 0:8, here] = new[0:8] + first
            new_ref[s, 8 : layers - 8, here] = new[8 : layers - 8]
            new_ref[s, layers - 8 :, here] = new[layers - 8 :] - last
        if here.stop % quarter == 0:
            p = slice(here.stop - quarter, here.stop)
            copies.append(
                pltpu.make_async_copy(
                    new_ref.at[:, :, p], new_hbm.at[:, :, p], sems.at[0, p.start // quarter]
                )
            )
            copies[-1].start()
    size = share * parcel_cap
    fetch_number.wait()
    for copy in fetch_flow:
        copy.wait()

    def group(g, carry):
        for i in range(size):
            where = number_smem[g, 64 * (g & 1) + i]
            for f in range(3):
                rows_ref[f, pl.ds(64 * g + i, 1), :] = flow_ref[f, pl.ds(where, 1), :]
        return carry

    lax.fori_loop(0, groups, group, 0)
    index, column = iota((8, PV), 0), iota((8, PV), 1)
    spread = ones(index == 0)
    take = ones((index < 2) & (column == 0))
    index, column = iota((3 * 2 * LANES, PV), 0), iota((3 * 2 * LANES, PV), 1)
    into = ones(column == 3 + lax.div(index, 2 * LANES))
    drag = (iota((size, PV), 1) >= 3) & (iota((size, PV), 1) <= 5)
    keep = jnp.where(drag, 1.0 - friction_timescale, 1.0)
    lane_of = jnp.where(number >= 0, cell_lane, -1).astype(F32)
    none = jnp.zeros((6, LANES), F32)
    for h in range(groups // 2):
        a, b = 2 * h, 2 * h + 1
        lanes = jnp.where(lefts, lane_of[a : a + 1], lane_of[b : b + 1])
        lanes = jnp.concatenate([lanes, lanes, none], axis=0).astype(BF16)
        mask = mm_tn(lanes, spread) == iota((LANES, PV), 1).astype(F32)
        gone = jnp.where(lefts, evaporated[a], evaporated[b])
        head = gone.astype(BF16).astype(F32)
        change = -mm_tn(jnp.concatenate([head, gone - head, none], axis=0).astype(BF16), take)
        fields = []
        for f in range(3):
            fields += split(jnp.where(mask, rows_ref[f, h * LANES : (h + 1) * LANES, :], 0.0), 2)
        change = change + friction_timescale * mm(jnp.concatenate(fields, axis=1), into)
        for i in range(2):
            g = 2 * h + i
            table = jnp.concatenate(
                [got_ref[g * share + k, 0:parcel_cap, :] for k in range(share)], axis=0
            )
            arrived_ref[g * size : (g + 1) * size, :] = table * keep + change[64 * i : 64 * i + size]
    copies.append(pltpu.make_async_copy(arrived_ref, arrived_hbm, sems.at[1, 2]))
    copies[-1].start()
    for copy in copies:
        copy.wait()


def fast(count=1):
    return [pl.BlockSpec(memory_space=pltpu.VMEM)] * count


def slow(count=1):
    return [pl.BlockSpec(memory_space=pltpu.HBM)] * count


def call(kernel, name, out, in_specs, scratch=(), out_specs=None, kib=1024):
    out_specs = out_specs or fast(len(out))
    run = pl.pallas_call(
        kernel,
        out_shape=tuple(
            (pltpu.HBM if spec.memory_space is pltpu.HBM else pltpu.VMEM)(s, t)
            for (s, t), spec in zip(out, out_specs, strict=True)
        ),
        in_specs=in_specs,
        out_specs=tuple(out_specs),
        scratch_shapes=list(scratch),
        compiler_params=pltpu.CompilerParams(vmem_limit_bytes=VMEM_LIMIT),
        cost_estimate=pl.CostEstimate(flops=0, transcendentals=0, bytes_accessed=kib * 1024),
        name=name,
    )

    def held(*operands):
        return run(
            *(
                pltpu.with_memory_space_constraint(a, spec.memory_space)
                for a, spec in zip(operands, in_specs, strict=True)
            )
        )

    return held


def dma(*count):
    return pltpu.SemaphoreType.DMA(count)


def body(
    species,
    interface_normal_flow,
    face_diffusion,
    inv_volume,
    diffusivity,
    low_partner,
    high_partner,
    low_orient,
    high_orient,
    droplet_table,
    parcel_block,
    parcel_cell,
    parcel_live,
):
    blocks = lax.axis_size("blk")
    local_species, layers, cells = species.shape
    parcels = droplet_table.shape[0]
    tile_cap = max(1, TILES // blocks)
    parcel_cap = 3 * parcels // (2 * blocks)
    sizes = (blocks, tile_cap, parcel_cap)
    tall = layers * cells // LANES
    rows = -(-(parcel_cap + PAIRS * tile_cap + 6) // 8) * 8
    groups = blocks * parcel_cap // 48
    int_row = (1, parcels)
    vmem = pltpu.VMEM

    def swap(value, bit):
        return lax.ppermute(value, "sp", [(i, i ^ bit) for i in range(lax.axis_size("sp"))])

    factors = diffusivity.reshape(1, local_species)
    other_species = swap(species, 1)
    other_factors = swap(factors, 1)

    target, cell = parcel_block.reshape(int_row), parcel_cell.reshape(int_row)
    packed, strips, edge_flow, strip, column, code, rank = call(
        functools.partial(pack_rows_kernel, *sizes),
        "pack_rows",
        [
            ((blocks, rows, LANES), F32),
            ((32, STRIP), F32),
            ((16, STRIP), F32),
            ((2, TILES, LANES), F32),
            ((2, TILES, STRIP), F32),
            ((2, TILES, STRIP), F32),
            ((8, parcels), jnp.int32),
        ],
        slow(10),
        [
            vmem((local_species, 8, cells), F32),
            vmem((local_species, 8, cells), F32),
            vmem((8, cells), F32),
            vmem((8, cells), F32),
            vmem((4, 1, TILES), jnp.int32),
            vmem(droplet_table.shape, F32),
            vmem((2,) + int_row, jnp.int32),
            dma(11),
        ],
        kib=13000,
    )(
        species,
        interface_normal_flow,
        face_diffusion,
        low_partner,
        high_partner,
        low_orient,
        high_orient,
        droplet_table,
        target,
        parcel_live.reshape(int_row),
    )

    z_half, fuel_half = call(
        sum_kernel,
        "chip_sum",
        [((layers // 2, cells), F32), ((layers // 2, cells), F32)],
        slow(1) + fast(1) + slow(1) + fast(2),
        [vmem(species.shape, F32), vmem((1, local_species), F32), dma(5)],
        kib=4680,
    )(species, other_species, factors, other_factors, strip)
    z_far = swap(z_half, 2)

    (m0,) = call(
        functools.partial(pack_meta_kernel, blocks, parcel_cap),
        "pack_meta",
        [((4 * blocks + TILES, LANES), F32)],
        slow(4) + fast(6),
        [
            vmem((1, local_species), F32),
            vmem(droplet_table.shape, F32),
            vmem((2,) + int_row, jnp.int32),
            dma(4),
        ],
        kib=6000,
    )(factors, droplet_table, target, cell, strips, strip, column, code, rank, z_half)
    m1, m2, m3 = swap(m0, 1), swap(m0, 2), swap(m0, 3)
    fuel_far = swap(fuel_half, 2)

    ready, z_own = call(
        functools.partial(assemble_kernel, *sizes),
        "assemble",
        [((blocks, rows, LANES), F32), ((layers // 2, cells), F32)],
        fast(7),
        kib=2880,
    )(packed, m0, m1, m2, m3, z_half, z_far)
    z_other = swap(z_own, 1)
    got = lax.all_to_all(ready, "blk", split_axis=0, concat_axis=0, tiled=True)

    base, edge_z = call(
        inner_kernel,
        "inner_flux",
        [(species.shape, F32), ((32, STRIP), F32)],
        slow(4) + fast(3),
        [
            vmem(interface_normal_flow.shape, F32),
            vmem(face_diffusion.shape, F32),
            vmem((layers, cells), F32),
            vmem(species.shape, F32),
            vmem((layers, cells), F32),
            dma(4, 4),
        ],
        kib=25200,
    )(
        interface_normal_flow,
        face_diffusion,
        inv_volume,
        species,
        z_own,
        z_other,
        m0,
    )

    (fuel_own,) = call(
        fuel_half_kernel,
        "fuel_half",
        [((layers // 2, cells), F32)],
        fast(3),
        kib=360,
    )(fuel_half, fuel_far, edge_z)
    fuel_other = swap(fuel_own, 1)
    (fuel_parts,) = call(
        fuel_kernel, "fuel_parts", [((2 * LANES, tall), BF16)], fast(2), kib=1080
    )(fuel_own, fuel_other)

    return call(
        functools.partial(final_kernel, *sizes),
        "final",
        [(species.shape, F32), ((blocks * parcel_cap, PV), F32)],
        fast(3) + slow(3) + fast(6),
        [
            vmem(species.shape, F32),
            vmem((blocks * parcel_cap, PV), F32),
            vmem((tall, 2 * groups * LANES), BF16),
            vmem((2 * LANES, 2 * groups * LANES), BF16),
            vmem((8, cells), F32),
            vmem(species.shape, F32),
            vmem((layers, cells), F32),
            vmem((3, tall, LANES), F32),
            vmem((2 * groups, LANES), jnp.int32),
            pltpu.SMEM((2 * groups, LANES), jnp.int32),
            vmem((3, 64 * groups, PV), F32),
            dma(2, 4),
            dma(cells // LANES),
            pltpu.SemaphoreType.DMA,
        ],
        slow(2),
        kib=32400,
    )(
        got,
        fuel_parts,
        base,
        species,
        inv_volume,
        interface_normal_flow,
        edge_z,
        edge_flow,
        strips,
        strip,
        column,
        m0,
    )


def solution(mesh):
    placed = (
        P("sp", "blk", None),
        P(None, "blk", None),
        P(None, "blk", None),
        P("blk", None),
        P("sp"),
        P("blk", None),
        P("blk", None),
        P("blk", None),
        P("blk", None),
        P(("blk", "sp"), None),
        P(("blk", "sp"), None),
        P(("blk", "sp")),
        P(("blk", "sp")),
    )
    return jax.shard_map(
        body,
        mesh=mesh,
        in_specs=placed,
        out_specs=(P("sp", "blk", None), P(("blk", "sp"), None)),
        check_vma=False,
    )
```

```python
import functools

import jax
import jax.numpy as jnp
from jax import lax
from jax.experimental import pallas as pl
from jax.experimental.pallas import tpu as pltpu
from jax.sharding import PartitionSpec as P

PV = 128
BJ = 64
BK = 64
TILE_SIDE = 8
TILES = 64
LANES = 128
FACE = BJ * BK
STRIP = TILE_SIDE * BK
PAIRS = 4

section_step = 0.5
friction_timescale = 0.3

F32 = jnp.float32
BF16 = jnp.bfloat16
VMEM_LIMIT = 16 * 1024 * 1024


def iota(shape, dim):
    return lax.broadcasted_iota(jnp.int32, shape, dim)


def mm(a, b):
    return lax.dot_general(a, b, (((1,), (0,)), ((), ())), preferred_element_type=F32)


def mm_nt(a, b):
    return lax.dot_general(a, b, (((1,), (1,)), ((), ())), preferred_element_type=F32)


def mm_tn(a, b):
    return lax.dot_general(a, b, (((0,), (0,)), ((), ())), preferred_element_type=F32)


def ones(condition, kind=BF16):
    return jnp.where(condition, 1.0, 0.0).astype(kind)


def split(value, parts):
    out = []
    for _ in range(parts - 1):
        head = value.astype(BF16)
        out.append(head)
        value = value - head.astype(F32)
    out.append(value.astype(BF16))
    return out


def inside_table():
    lane, cell = iota((STRIP, LANES), 0), iota((STRIP, LANES), 1) & 63
    return ones(((lane >> 6) == (cell >> 3)) & ((lane & 7) == (cell & 7)))


def orient_table():
    shape = (8 * TILES, LANES)
    code, source = iota(shape, 0) >> 6, iota(shape, 0) & 63
    column = iota(shape, 1)
    r, c = (column >> 3) & 7, column & 7
    back = column >= 64
    turned = code >= 4
    flip_r, flip_c = (code & 1) * 7, ((code >> 1) & 1) * 7
    there = jnp.where(turned, (c ^ flip_c) * 8 + (r ^ flip_r), (r ^ flip_r) * 8 + (c ^ flip_c))
    r0, c0 = jnp.where(turned, c, r), jnp.where(turned, r, c)
    return ones(source == jnp.where(back, (r0 ^ flip_r) * 8 + (c0 ^ flip_c), there))


def place_matrix(partner, blocks, cap):
    onehot = ones(iota((blocks, TILES), 0) == partner, F32)
    earlier = ones(iota((TILES, TILES), 0) < iota((TILES, TILES), 1))
    rank = jnp.sum(onehot * mm(onehot.astype(BF16), earlier), axis=0, keepdims=True)
    slot = partner * cap + rank.astype(jnp.int32)
    return ones(iota((TILES, TILES), 0) == slot)


def to_strips(row):
    return jnp.concatenate([row[:, i * STRIP : (i + 1) * STRIP] for i in range(8)], axis=0)


def from_strips(strips):
    return jnp.concatenate([strips[i : i + 1] for i in range(8)], axis=1)


def take_tiles(faces, strip, column, code, inside):
    parts = [part for face in faces for part in split(face, 3)]
    wide = mm(strip, jnp.concatenate(parts, axis=1))
    tall = jnp.concatenate(
        [(wide[:, i * STRIP : (i + 1) * STRIP] * column).astype(BF16) for i in range(len(parts))],
        axis=0,
    )
    cells = mm(tall, inside)
    out = []
    for i in range(len(parts)):
        one = cells[i * TILES : (i + 1) * TILES]
        out.append((jnp.concatenate([one] * 4, axis=1) * code).astype(BF16))
    return out


def turn_tiles(tiles, table):
    turned = mm(jnp.concatenate(tiles, axis=0), table)
    turned = [turned[i * TILES : (i + 1) * TILES] for i in range(len(tiles))]
    return [turned[i + 2] + turned[i + 1] + turned[i] for i in range(0, len(tiles), 3)]


def begin(copies, sems):
    started = [pltpu.make_async_copy(a, b, sems.at[i]) for i, (a, b) in enumerate(copies)]
    for one in started:
        one.start()
    return started


def pack_meta_kernel(
    blocks,
    tile_cap,
    parcel_cap,
    species,
    diffusivity,
    low_partner,
    high_partner,
    low_orient,
    high_orient,
    table,
    block,
    cell,
    live,
    m_ref,
    strips_ref,
    strip_ref,
    column_ref,
    code_ref,
    slot_ref,
    bottom,
    top,
    d_own,
    small,
    table_in,
    parcel,
    sems,
):
    layers = species.shape[1]
    copies = begin(
        [(high_partner, small.at[0]), (low_partner, small.at[1])]
        + [(high_orient, small.at[2]), (low_orient, small.at[3])]
        + [(block, parcel.at[0]), (live, parcel.at[1]), (cell, parcel.at[2])]
        + [(table, table_in), (diffusivity, d_own)]
        + [(species.at[:, layers - 8 :], top), (species.at[:, 0:8], bottom)],
        sems,
    )
    me = lax.axis_index("blk")
    inside, turn = inside_table(), orient_table()
    tile = iota((TILES, STRIP), 0)
    strip_of = ones((iota((TILES, LANES), 0) >> 3) == iota((TILES, LANES), 1))
    column_of = ones((tile & 7) == ((iota((TILES, STRIP), 1) >> 3) & 7))
    code_of = ones(iota((8, STRIP), 0) == (iota((8, STRIP), 1) >> 6))
    rows = table.shape[0]
    earlier = ones(iota((rows, rows), 0) < iota((rows, rows), 1))
    for copy in copies[0:4]:
        copy.wait()
    for k in range(2):
        place = place_matrix(small[k], blocks, tile_cap)
        strip_ref[k] = mm(place, strip_of)
        column_ref[k] = mm(place, column_of)
        code = ones(iota((8, TILES), 0) == small[2 + k])
        code_ref[k] = mm(mm_nt(place, code).astype(BF16), code_of)
    for copy in copies[4:8]:
        copy.wait()
    target = parcel[0]
    alive = parcel[1] == 1
    onehot = ones((iota((blocks, rows), 0) == target) & alive, F32)
    rank = jnp.sum(onehot * mm(onehot.astype(BF16), earlier), axis=0, keepdims=True)
    rank = rank.astype(jnp.int32)
    slot_ref[...] = jnp.broadcast_to(jnp.where(alive, target * parcel_cap + rank, -1), (8, rows))
    pick = ones(iota((8, PV), 1) == iota((8, PV), 0) + 1)
    parts = split(table_in[...], 3)
    columns = mm_nt(pick, parts[2]) + mm_nt(pick, parts[1]) + mm_nt(pick, parts[0])
    p1, p2 = columns[0:1], columns[1:2]
    soft = jnp.maximum(p1, 0.0) + jnp.log1p(jnp.exp(-jnp.abs(p1)))
    sig = 1.0 / (1.0 + jnp.exp(-p2))
    fields = jnp.concatenate(
        [(parcel[2] + 1).astype(F32), soft, sig, jnp.zeros((5, rows), F32)], axis=0
    )
    share = 48 // parcel_cap
    lane = rank + lax.rem(me, share) * parcel_cap + 64 * (lax.div(me, share) & 1)
    goal = jnp.where(alive, target * LANES + lane, -1)
    spots = ones(iota((blocks * LANES, rows), 0) == goal)
    meta = mm_nt(jnp.concatenate(split(fields, 3), axis=0), spots)
    meta = meta[16:24] + meta[8:16] + meta[0:8]
    copies[8].wait()
    d0, d1 = d_own[0:1, 0:1], d_own[0:1, 1:2]
    lanes = iota((1, LANES), 1)
    own = jnp.where(lanes == 0, d0, jnp.where(lanes == 1, d1, 0.0))
    for b in range(blocks):
        m_ref[4 * b : 4 * b + 3, :] = meta[0:3, b * LANES : (b + 1) * LANES]
        m_ref[4 * b + 3 : 4 * b + 4, :] = own
    copies[9].wait()
    copies[10].wait()
    top0, top1 = to_strips(top[0, 7:8, :]), to_strips(top[1, 7:8, :])
    low0, low1 = to_strips(bottom[0, 0:1, :]), to_strips(bottom[1, 0:1, :])
    strips_ref[...] = jnp.concatenate([top0, top1, low0, low1], axis=0)
    tiles = []
    for k, face in enumerate((d0 * top0 + d1 * top1, d0 * low0 + d1 * low1)):
        strip = strip_ref[k][:, 0:8].astype(BF16)
        tiles += take_tiles([face], strip, column_ref[k], code_ref[k], inside)
    high, low = turn_tiles(tiles, turn)
    m_ref[4 * blocks : 4 * blocks + TILES, :] = jnp.where(lanes < 64, high, low)


def pack_rows_kernel(
    blocks,
    tile_cap,
    parcel_cap,
    flow,
    diff,
    table,
    strips_ref,
    strip_ref,
    column_ref,
    code_ref,
    slot_ref,
    z_half,
    out_ref,
    edge_ref,
    vel_in,
    dif_in,
    table_in,
    sems,
):
    copies = begin(
        [(flow.at[0, 0:8], vel_in), (diff.at[0, 0:8], dif_in), (table, table_in)], sems
    )
    inside, turn = inside_table(), orient_table()
    faces = [strips_ref[8 * i : 8 * i + 8, :] for i in range(4)]
    copies[0].wait()
    copies[1].wait()
    vel, dif = to_strips(vel_in[0:1, :]), to_strips(dif_in[0:1, :])
    edge_ref[...] = jnp.concatenate([vel, dif], axis=0)
    tiles = []
    for k, some in enumerate((faces[0:2], faces[2:4] + [vel, dif])):
        strip = strip_ref[k][:, 0:8].astype(BF16)
        tiles += take_tiles(some, strip, column_ref[k], code_ref[k], inside)
    high0, high1, low0, low1, vel, dif = turn_tiles(tiles, turn)
    left = iota((TILES, LANES), 1) < 64
    pairs = [
        jnp.where(left, high0, pltpu.roll(high1, 64, 1)),
        jnp.where(left, pltpu.roll(low0, 64, 1), low1),
        jnp.where(left, pltpu.roll(vel, 64, 1), dif),
    ]
    copies[2].wait()
    rows = table.shape[0]
    send = ones(iota((blocks * parcel_cap, rows), 0) == slot_ref[0:1, :])
    parts = split(table_in[...], 3)
    sent = mm(send, parts[2]) + mm(send, parts[1]) + mm(send, parts[0])
    for b in range(blocks):
        out_ref[b, 0:parcel_cap, :] = sent[b * parcel_cap : (b + 1) * parcel_cap]
        for k in range(PAIRS - 1):
            at = parcel_cap + k * tile_cap
            out_ref[b, at : at + tile_cap, :] = pairs[k][b * tile_cap : (b + 1) * tile_cap]


def add_kernel(near_ref, far_ref, out_ref):
    out_ref[...] = near_ref[...] + far_ref[...]


def assemble_kernel(blocks, tile_cap, parcel_cap, buf_ref, m0, m1, m2, m3, z_half, out_ref):
    ghost = parcel_cap + (PAIRS - 1) * tile_cap
    z = slice(4 * blocks, 4 * blocks + TILES)
    total = (m0[z, :] + m1[z, :]) + (m2[z, :] + m3[z, :])
    near = m0[0 : 4 * blocks, :] + pltpu.roll(m1[0 : 4 * blocks, :], 64, 1)
    far = m2[0 : 4 * blocks, :] + pltpu.roll(m3[0 : 4 * blocks, :], 64, 1)
    for b in range(blocks):
        out_ref[b, 0:ghost, :] = buf_ref[b, 0:ghost, :]
        out_ref[b, ghost : ghost + tile_cap, :] = total[b * tile_cap : (b + 1) * tile_cap]
        at = ghost + tile_cap
        out_ref[b, at : at + 3, :] = near[4 * b : 4 * b + 3]
        out_ref[b, at + 3 : at + 6, :] = far[4 * b : 4 * b + 3]
        if at + 6 < out_ref.shape[1]:
            out_ref[b, at + 6 :, :] = jnp.zeros((out_ref.shape[1] - at - 6, LANES), F32)


def sum_kernel(
    species, other_ref, factors, d_other, after0, after1, after2, after3, zh_ref, fh_ref, own_ref, d_own, sems
):
    half, cells = zh_ref.shape
    quarter = cells // 4
    parts = [slice(i * quarter, (i + 1) * quarter) for i in range(4)]
    copies = begin(
        [(factors, d_own)] + [(species.at[:, :, p], own_ref.at[:, :, p]) for p in parts], sems
    )
    first = (lax.axis_index("sp") & 1) == 0
    copies[0].wait()
    d0, d1, e0, e1 = d_own[0:1, 0:1], d_own[0:1, 1:2], d_other[0:1, 0:1], d_other[0:1, 1:2]
    for copy, p in zip(copies[1:], parts):
        copy.wait()
        for lo in range(p.start, p.stop, LANES):
            at = slice(lo, lo + LANES)
            own, other = own_ref[0, :, at], other_ref[0, :, at]
            z = d0 * own + d1 * own_ref[1, :, at] + (e0 * other + e1 * other_ref[1, :, at])
            zh_ref[:, at] = jnp.where(first, z[0:half], z[half:])
            fh_ref[:, at] = jnp.where(first, own[0:half], other[half:])


def flux(velocity, diffusion, d, upper, lower, weight):
    middle = 0.5 * (upper + lower)
    return velocity * middle - diffusion * (d * (upper - lower) - middle * weight)


def transposed_parts(get, out_ref, at, parts, group):
    square = jnp.concatenate([get(4 * group + i) for i in range(4)], axis=0).T
    for k, part in enumerate(split(square, parts)):
        out_ref[at + k * LANES : at + (k + 1) * LANES, group * LANES : (group + 1) * LANES] = part


def inner_kernel(
    flow,
    diff,
    vol,
    species,
    za_ref,
    zb_ref,
    m0,
    base_ref,
    edge_ref,
    flow_ref,
    diff_ref,
    vol_ref,
    species_ref,
    z_ref,
    sems,
):
    layers, cells = vol.shape
    half = layers // 2
    quarter = cells // 4
    parts = [slice(i * quarter, (i + 1) * quarter) for i in range(4)]
    copies = {}
    for n, i in enumerate((3, 2, 1, 0)):
        p = parts[i]
        copies[i] = begin(
            [
                (flow.at[:, :, p], flow_ref.at[:, :, p]),
                (diff.at[:, :, p], diff_ref.at[:, :, p]),
                (vol.at[:, p], vol_ref.at[:, p]),
                (species.at[:, :, p], species_ref.at[:, :, p]),
            ],
            sems.at[n],
        )
    first = (lax.axis_index("sp") & 1) == 0
    z_ref[0:half, :] = jnp.where(first, za_ref[...], zb_ref[...])
    z_ref[half:, :] = jnp.where(first, zb_ref[...], za_ref[...])
    shape = (layers, LANES)
    row, lane = iota(shape, 0), iota(shape, 1)
    left = lane < 64
    inner = row > 0
    off_wall = (lane & 63) != 0
    ds = (m0[3:4, 0:1], m0[3:4, 1:2])
    above = [jnp.zeros(shape, F32)] * 2
    for j in range(cells // LANES - 1, -1, -1):
        here = slice(j * LANES, (j + 1) * LANES)
        before = slice(max(j - 1, 0) * LANES, (max(j - 1, 0) + 1) * LANES)
        if here.stop % quarter == 0:
            for copy in copies[here.start // quarter][0:3]:
                copy.wait()
            if j == cells // LANES - 1:
                copies[here.start // quarter][3].wait()
        if here.start % quarter == 0 and j > 0:
            copies[before.start // quarter][3].wait()
        z = z_ref[:, here]
        unders = (
            lambda y: pltpu.roll(y, 1, 0),
            lambda y: pltpu.roll(y, 64, 1),
            lambda y: pltpu.roll(y, 1, 1),
        )
        z_under = (
            pltpu.roll(z, 1, 0),
            pltpu.roll(jnp.where(left, z, z_ref[:, before]), 64, 1),
            pltpu.roll(z, 1, 1),
        )
        masks = (inner, (lane >= 64) if j == 0 else None, off_wall)
        means, slopes = [], []
        for k in range(3):
            g = diff_ref[k, :, here]
            c = 0.5 * (flow_ref[k, :, here] + g * (z - z_under[k]))
            if masks[k] is not None:
                c, g = jnp.where(masks[k], c, 0.0), jnp.where(masks[k], g, 0.0)
            means.append(c)
            slopes.append(g)
        scale = section_step * vol_ref[:, here]
        for s in range(2):
            y = species_ref[s, :, here]
            under = (
                pltpu.roll(y, 1, 0),
                pltpu.roll(jnp.where(left, y, species_ref[s, :, before]), 64, 1),
                pltpu.roll(y, 1, 1),
            )
            f_layer, f_row, f_column = (
                (y + u) * c - (y - u) * (g * ds[s]) for u, c, g in zip(under, means, slopes)
            )
            divergence = (
                (pltpu.roll(f_layer, layers - 1, 0) - f_layer)
                + (pltpu.roll(jnp.where(left, above[s], f_row), 64, 1) - f_row)
                + (pltpu.roll(f_column, LANES - 1, 1) - f_column)
            )
            base_ref[s, :, here] = y - scale * divergence
            above[s] = f_row
    ends = [ref[i : i + 1, :] for ref in (z_ref, vol_ref) for i in (0, layers - 1)]
    edge_ref[...] = jnp.concatenate([to_strips(end) for end in ends], axis=0)


def fuel_half_kernel(near_ref, far_ref, edge_ref, out_ref):
    out_ref[...] = jnp.where(lax.axis_index("sp") < 2, near_ref[...], far_ref[...])


def fuel_kernel(own_ref, other_ref, out_ref):
    first = (lax.axis_index("sp") & 1) == 0

    def field(j):
        here = slice(j * LANES, (j + 1) * LANES)
        a, b = own_ref[:, here], other_ref[:, here]
        return jnp.concatenate([jnp.where(first, a, b), jnp.where(first, b, a)], axis=0)

    for group in range(FACE // LANES // 4):
        transposed_parts(field, out_ref, 0, 2, group)


def ghost_faces(pairs, strip, column, inside):
    lane = iota((TILES, LANES), 1)
    parts = []
    for pair, right in pairs:
        one = jnp.where((lane >= 64) if right else (lane < 64), pair, 0.0)
        parts += split(one, 3)
    wide = mm_nt(jnp.concatenate(parts, axis=0), inside)
    wide = [
        (wide[i * TILES : (i + 1) * TILES] * column).astype(BF16) for i in range(len(parts))
    ]
    wide = mm_tn(strip, jnp.concatenate(wide, axis=1))
    wide = [wide[:, i * STRIP : (i + 1) * STRIP] for i in range(len(parts))]
    return [wide[3 * i + 2] + wide[3 * i + 1] + wide[3 * i] for i in range(len(pairs))]


def final_kernel(
    blocks,
    tile_cap,
    parcel_cap,
    got_ref,
    fuel_ref,
    base_ref,
    species,
    vol,
    flow,
    zedge_ref,
    fedge_ref,
    strips_ref,
    strip_ref,
    column_ref,
    m0,
    new_hbm,
    arrived_hbm,
    new_ref,
    arrived_ref,
    spots,
    loads,
    edge,
    species_ref,
    vol_ref,
    flow_ref,
    number_ref,
    number_smem,
    rows_ref,
    sems,
    flow_sem,
    number_sem,
):
    layers, cells = base_ref.shape[1:]
    fetch = begin([(species, species_ref), (vol, vol_ref)], sems.at[1])
    fetch_flow = begin(
        [
            (flow.at[:, :, j * LANES : (j + 1) * LANES], flow_ref.at[:, j * layers : (j + 1) * layers])
            for j in range(cells // LANES)
        ],
        flow_sem,
    )
    tall_rows = layers * cells // LANES
    share = 48 // parcel_cap
    groups = blocks // share
    ghost = parcel_cap
    at = parcel_cap + PAIRS * tile_cap

    def pair(k):
        lo = ghost + k * tile_cap
        return jnp.concatenate([got_ref[b, lo : lo + tile_cap, :] for b in range(blocks)], axis=0)

    def meta(f):
        rows = []
        for h in range(2):
            for g in range(groups):
                total = None
                for i in range(share):
                    one = got_ref[g * share + i, at + 3 * h + f : at + 3 * h + f + 1, :]
                    total = one if total is None else total + one
                rows.append(total)
        return jnp.concatenate(rows, axis=0)

    chunks = 2 * groups
    number = meta(0).astype(jnp.int32) - 1
    soft, sig = meta(1), meta(2)
    cell_layer = lax.shift_right_arithmetic(number, 12)
    cell_row = (lax.shift_right_arithmetic(number, 7) & 31) * layers + cell_layer
    cell_row = jnp.where(number >= 0, cell_row, -1)
    number_ref[...] = jnp.maximum(cell_row, 0)
    fetch_number = pltpu.make_async_copy(number_ref, number_smem, number_sem)
    fetch_number.start()
    cell_lane = number & (LANES - 1)
    sublane = iota((LANES, LANES), 0)
    tall = iota((tall_rows, LANES), 0)
    for c in range(chunks):
        spots[:, c * LANES : (c + 1) * LANES] = ones(tall == cell_row[c : c + 1])
    inside = inside_table()
    p0, p1, p2, p3 = (pair(k) for k in range(PAIRS))
    below0, below1, below_z = ghost_faces(
        [(p0, 0), (p0, 1), (p3, 0)], strip_ref[1].astype(BF16)[:, 0:8], column_ref[1], inside
    )
    above0, above1, top_v, top_d, above_z = ghost_faces(
        [(p1, 0), (p1, 1), (p2, 0), (p2, 1), (p3, 1)],
        strip_ref[0].astype(BF16)[:, 0:8],
        column_ref[0],
        inside,
    )
    z_bottom, z_top = zedge_ref[0:8, :], zedge_ref[8:16, :]
    bottom_scale, top_scale = section_step * zedge_ref[16:24, :], section_step * zedge_ref[24:32, :]
    bottom_v, bottom_d = fedge_ref[0:8, :], fedge_ref[8:16, :]
    for s, (below, above) in enumerate(((below0, above0), (below1, above1))):
        d = m0[3:4, s : s + 1]
        high = strips_ref[8 * s : 8 * s + 8, :]
        low = strips_ref[16 + 8 * s : 24 + 8 * s, :]
        f_low = flux(bottom_v, bottom_d, d, low, below, z_bottom - below_z)
        f_high = flux(top_v, top_d, d, above, high, above_z - z_top)
        edge[2 * s : 2 * s + 1, :] = from_strips(bottom_scale * f_low)
        edge[2 * s + 1 : 2 * s + 2, :] = from_strips(top_scale * f_high)
    width = 2 * LANES
    lefts = iota((1, LANES), 1) < 64
    evaporated = []
    for c in range(0, chunks, 2):
        both = mm(fuel_ref[...], spots[:, c * LANES : c * LANES + width])
        both = both[0:LANES] + both[LANES:]
        for i in range(2):
            mask = sublane == cell_lane[c + i : c + i + 1]
            fuel = jnp.sum(
                jnp.where(mask, both[:, i * LANES : (i + 1) * LANES], 0.0), axis=0, keepdims=True
            )
            gone = soft[c + i : c + i + 1] * (sig[c + i : c + i + 1] - fuel)
            evaporated.append(gone)
            for k, part in enumerate(split(jnp.where(mask, gone, 0.0), 2)):
                loads[k * LANES : (k + 1) * LANES, (c + i) * LANES : (c + i + 1) * LANES] = part
    source = mm_nt(spots[...], loads[...])
    source = source[:, 0:LANES] + source[:, LANES:]
    row = iota((8, LANES), 0)
    delta = (jnp.where(lax.axis_index("sp") == 0, 1.0, 0.0), 0.0)
    for copy in fetch:
        copy.wait()
    quarter = cells // 4
    copies = []
    for j in range(cells // LANES):
        here = slice(j * LANES, (j + 1) * LANES)
        part = source[j * layers : (j + 1) * layers] * (section_step * vol_ref[:, here])
        for s in range(2):
            new = base_ref[s, :, here] + part * (delta[s] - species_ref[s, :, here])
            first = jnp.where(row == 0, edge[2 * s : 2 * s + 1, here], 0.0)
            last = jnp.where(row == 7, edge[2 * s + 1 : 2 * s + 2, here], 0.0)
            new_ref[s, 0:8, here] = new[0:8] + first
            new_ref[s, 8 : layers - 8, here] = new[8 : layers - 8]
            new_ref[s, layers - 8 :, here] = new[layers - 8 :] - last
        if here.stop % quarter == 0:
            p = slice(here.stop - quarter, here.stop)
            copies.append(
                pltpu.make_async_copy(
                    new_ref.at[:, :, p], new_hbm.at[:, :, p], sems.at[0, p.start // quarter]
                )
            )
            copies[-1].start()
    size = share * parcel_cap
    fetch_number.wait()
    for copy in fetch_flow:
        copy.wait()

    def group(g, carry):
        for i in range(size):
            where = number_smem[g, 64 * (g & 1) + i]
            for f in range(3):
                rows_ref[f, pl.ds(64 * g + i, 1), :] = flow_ref[f, pl.ds(where, 1), :]
        return carry

    lax.fori_loop(0, groups, group, 0)
    index, column = iota((8, PV), 0), iota((8, PV), 1)
    spread = ones(index == 0)
    take = ones((index < 2) & (column == 0))
    index, column = iota((3 * 2 * LANES, PV), 0), iota((3 * 2 * LANES, PV), 1)
    into = ones(column == 3 + lax.div(index, 2 * LANES))
    drag = (iota((size, PV), 1) >= 3) & (iota((size, PV), 1) <= 5)
    keep = jnp.where(drag, 1.0 - friction_timescale, 1.0)
    lane_of = jnp.where(number >= 0, cell_lane, -1).astype(F32)
    none = jnp.zeros((6, LANES), F32)
    for h in range(groups // 2):
        a, b = 2 * h, 2 * h + 1
        lanes = jnp.where(lefts, lane_of[a : a + 1], lane_of[b : b + 1])
        lanes = jnp.concatenate([lanes, lanes, none], axis=0).astype(BF16)
        mask = mm_tn(lanes, spread) == iota((LANES, PV), 1).astype(F32)
        gone = jnp.where(lefts, evaporated[a], evaporated[b])
        head = gone.astype(BF16).astype(F32)
        change = -mm_tn(jnp.concatenate([head, gone - head, none], axis=0).astype(BF16), take)
        fields = []
        for f in range(3):
            fields += split(jnp.where(mask, rows_ref[f, h * LANES : (h + 1) * LANES, :], 0.0), 2)
        change = change + friction_timescale * mm(jnp.concatenate(fields, axis=1), into)
        for i in range(2):
            g = 2 * h + i
            table = jnp.concatenate(
                [got_ref[g * share + k, 0:parcel_cap, :] for k in range(share)], axis=0
            )
            arrived_ref[g * size : (g + 1) * size, :] = table * keep + change[64 * i : 64 * i + size]
    copies.append(pltpu.make_async_copy(arrived_ref, arrived_hbm, sems.at[1, 2]))
    copies[-1].start()
    for copy in copies:
        copy.wait()


def fast(count=1):
    return [pl.BlockSpec(memory_space=pltpu.VMEM)] * count


def slow(count=1):
    return [pl.BlockSpec(memory_space=pltpu.HBM)] * count


def call(kernel, name, out, in_specs, scratch=(), out_specs=None, kib=1024):
    out_specs = out_specs or fast(len(out))
    run = pl.pallas_call(
        kernel,
        out_shape=tuple(
            (pltpu.HBM if spec.memory_space is pltpu.HBM else pltpu.VMEM)(s, t)
            for (s, t), spec in zip(out, out_specs, strict=True)
        ),
        in_specs=in_specs,
        out_specs=tuple(out_specs),
        scratch_shapes=list(scratch),
        compiler_params=pltpu.CompilerParams(vmem_limit_bytes=VMEM_LIMIT),
        cost_estimate=pl.CostEstimate(flops=0, transcendentals=0, bytes_accessed=kib * 1024),
        name=name,
    )

    def held(*operands):
        return run(
            *(
                pltpu.with_memory_space_constraint(a, spec.memory_space)
                for a, spec in zip(operands, in_specs, strict=True)
            )
        )

    return held


def dma(*count):
    return pltpu.SemaphoreType.DMA(count)


def body(
    species,
    interface_normal_flow,
    face_diffusion,
    inv_volume,
    diffusivity,
    low_partner,
    high_partner,
    low_orient,
    high_orient,
    droplet_table,
    parcel_block,
    parcel_cell,
    parcel_live,
):
    blocks = lax.axis_size("blk")
    local_species, layers, cells = species.shape
    parcels = droplet_table.shape[0]
    tile_cap = max(1, TILES // blocks)
    parcel_cap = 3 * parcels // (2 * blocks)
    sizes = (blocks, tile_cap, parcel_cap)
    tall = layers * cells // LANES
    rows = -(-(parcel_cap + PAIRS * tile_cap + 6) // 8) * 8
    groups = blocks * parcel_cap // 48
    int_row = (1, parcels)
    vmem = pltpu.VMEM

    def swap(value, bit):
        return lax.ppermute(value, "sp", [(i, i ^ bit) for i in range(lax.axis_size("sp"))])

    factors = diffusivity.reshape(1, local_species)
    other_species = swap(species, 1)
    other_factors = swap(factors, 1)

    m0, strips, strip, column, code, slot = call(
        functools.partial(pack_meta_kernel, *sizes),
        "pack_meta",
        [
            ((4 * blocks + TILES, LANES), F32),
            ((32, STRIP), F32),
            ((2, TILES, LANES), F32),
            ((2, TILES, STRIP), F32),
            ((2, TILES, STRIP), F32),
            ((8, parcels), jnp.int32),
        ],
        slow(10),
        [
            vmem((local_species, 8, cells), F32),
            vmem((local_species, 8, cells), F32),
            vmem((1, local_species), F32),
            vmem((4, 1, TILES), jnp.int32),
            vmem(droplet_table.shape, F32),
            vmem((3,) + int_row, jnp.int32),
            dma(11),
        ],
        kib=10000,
    )(
        species,
        factors,
        low_partner,
        high_partner,
        low_orient,
        high_orient,
        droplet_table,
        parcel_block.reshape(int_row),
        parcel_cell.reshape(int_row),
        parcel_live.reshape(int_row),
    )
    m1, m2, m3 = swap(m0, 1), swap(m0, 2), swap(m0, 3)


    packed, edge_flow = call(
        functools.partial(pack_rows_kernel, *sizes),
        "pack_rows",
        [((blocks, rows, LANES), F32), ((16, STRIP), F32)],
        slow(3) + fast(6),
        [
            vmem((8, cells), F32),
            vmem((8, cells), F32),
            vmem(droplet_table.shape, F32),
            dma(3),
        ],
        kib=10000,
    )(
        interface_normal_flow,
        face_diffusion,
        droplet_table,
        strips,
        strip,
        column,
        code,
        slot,
        m0,
    )
    z_half, fuel_half = call(
        sum_kernel,
        "chip_sum",
        [((layers // 2, cells), F32), ((layers // 2, cells), F32)],
        slow(1) + fast(1) + slow(1) + fast(5),
        [vmem(species.shape, F32), vmem((1, local_species), F32), dma(5)],
        kib=4680,
    )(species, other_species, factors, other_factors, m1, m2, m3, edge_flow)
    z_far = swap(z_half, 2)
    fuel_far = swap(fuel_half, 2)

    (z_own,) = call(
        add_kernel, "z_own", [((layers // 2, cells), F32)], fast(2), kib=1000
    )(z_half, z_far)
    (ready,) = call(
        functools.partial(assemble_kernel, *sizes),
        "assemble",
        [((blocks, rows, LANES), F32)],
        fast(6),
        kib=2880,
    )(packed, m0, m1, m2, m3, z_half)
    z_other = swap(z_own, 1)
    got = lax.all_to_all(ready, "blk", split_axis=0, concat_axis=0, tiled=True)

    base, edge_z = call(
        inner_kernel,
        "inner_flux",
        [(species.shape, F32), ((32, STRIP), F32)],
        slow(4) + fast(3),
        [
            vmem(interface_normal_flow.shape, F32),
            vmem(face_diffusion.shape, F32),
            vmem((layers, cells), F32),
            vmem(species.shape, F32),
            vmem((layers, cells), F32),
            dma(4, 4),
        ],
        kib=25200,
    )(
        interface_normal_flow,
        face_diffusion,
        inv_volume,
        species,
        z_own,
        z_other,
        m0,
    )

    (fuel_own,) = call(
        fuel_half_kernel,
        "fuel_half",
        [((layers // 2, cells), F32)],
        fast(3),
        kib=360,
    )(fuel_half, fuel_far, edge_z)
    fuel_other = swap(fuel_own, 1)
    (fuel_parts,) = call(
        fuel_kernel, "fuel_parts", [((2 * LANES, tall), BF16)], fast(2), kib=1080
    )(fuel_own, fuel_other)

    return call(
        functools.partial(final_kernel, *sizes),
        "final",
        [(species.shape, F32), ((blocks * parcel_cap, PV), F32)],
        fast(3) + slow(3) + fast(6),
        [
            vmem(species.shape, F32),
            vmem((blocks * parcel_cap, PV), F32),
            vmem((tall, 2 * groups * LANES), BF16),
            vmem((2 * LANES, 2 * groups * LANES), BF16),
            vmem((8, cells), F32),
            vmem(species.shape, F32),
            vmem((layers, cells), F32),
            vmem((3, tall, LANES), F32),
            vmem((2 * groups, LANES), jnp.int32),
            pltpu.SMEM((2 * groups, LANES), jnp.int32),
            vmem((3, 64 * groups, PV), F32),
            dma(2, 4),
            dma(cells // LANES),
            pltpu.SemaphoreType.DMA,
        ],
        slow(2),
        kib=32400,
    )(
        got,
        fuel_parts,
        base,
        species,
        inv_volume,
        interface_normal_flow,
        edge_z,
        edge_flow,
        strips,
        strip,
        column,
        m0,
    )


def solution(mesh):
    placed = (
        P("sp", "blk", None),
        P(None, "blk", None),
        P(None, "blk", None),
        P("blk", None),
        P("sp"),
        P("blk", None),
        P("blk", None),
        P("blk", None),
        P("blk", None),
        P(("blk", "sp"), None),
        P(("blk", "sp"), None),
        P(("blk", "sp")),
        P(("blk", "sp")),
    )
    return jax.shard_map(
        body,
        mesh=mesh,
        in_specs=placed,
        out_specs=(P("sp", "blk", None), P(("blk", "sp"), None)),
        check_vma=False,
    )
```

```python
import functools

import jax
import jax.numpy as jnp
from jax import lax
from jax.experimental import pallas as pl
from jax.experimental.pallas import tpu as pltpu
from jax.sharding import PartitionSpec as P

PV = 128
BJ = 64
BK = 64
TILE_SIDE = 8
TILES = 64
LANES = 128
FACE = BJ * BK
STRIP = TILE_SIDE * BK
PAIRS = 4

section_step = 0.5
friction_timescale = 0.3

F32 = jnp.float32
BF16 = jnp.bfloat16
VMEM_LIMIT = 16 * 1024 * 1024


def iota(shape, dim):
    return lax.broadcasted_iota(jnp.int32, shape, dim)


def mm(a, b):
    return lax.dot_general(a, b, (((1,), (0,)), ((), ())), preferred_element_type=F32)


def mm_nt(a, b):
    return lax.dot_general(a, b, (((1,), (1,)), ((), ())), preferred_element_type=F32)


def mm_tn(a, b):
    return lax.dot_general(a, b, (((0,), (0,)), ((), ())), preferred_element_type=F32)


def ones(condition, kind=BF16):
    return jnp.where(condition, 1.0, 0.0).astype(kind)


def split(value, parts):
    out = []
    for _ in range(parts - 1):
        head = value.astype(BF16)
        out.append(head)
        value = value - head.astype(F32)
    out.append(value.astype(BF16))
    return out


def inside_table():
    lane, cell = iota((STRIP, LANES), 0), iota((STRIP, LANES), 1) & 63
    return ones(((lane >> 6) == (cell >> 3)) & ((lane & 7) == (cell & 7)))


def orient_table():
    shape = (8 * TILES, LANES)
    code, source = iota(shape, 0) >> 6, iota(shape, 0) & 63
    column = iota(shape, 1)
    r, c = (column >> 3) & 7, column & 7
    back = column >= 64
    turned = code >= 4
    flip_r, flip_c = (code & 1) * 7, ((code >> 1) & 1) * 7
    there = jnp.where(turned, (c ^ flip_c) * 8 + (r ^ flip_r), (r ^ flip_r) * 8 + (c ^ flip_c))
    r0, c0 = jnp.where(turned, c, r), jnp.where(turned, r, c)
    return ones(source == jnp.where(back, (r0 ^ flip_r) * 8 + (c0 ^ flip_c), there))


def place_matrix(partner, blocks, cap):
    onehot = ones(iota((blocks, TILES), 0) == partner, F32)
    earlier = ones(iota((TILES, TILES), 0) < iota((TILES, TILES), 1))
    rank = jnp.sum(onehot * mm(onehot.astype(BF16), earlier), axis=0, keepdims=True)
    slot = partner * cap + rank.astype(jnp.int32)
    return ones(iota((TILES, TILES), 0) == slot)


def to_strips(row):
    return jnp.concatenate([row[:, i * STRIP : (i + 1) * STRIP] for i in range(8)], axis=0)


def from_strips(strips):
    return jnp.concatenate([strips[i : i + 1] for i in range(8)], axis=1)


def take_tiles(faces, strip, column, code, inside):
    parts = [part for face in faces for part in split(face, 3)]
    wide = mm(strip, jnp.concatenate(parts, axis=1))
    tall = jnp.concatenate(
        [(wide[:, i * STRIP : (i + 1) * STRIP] * column).astype(BF16) for i in range(len(parts))],
        axis=0,
    )
    cells = mm(tall, inside)
    out = []
    for i in range(len(parts)):
        one = cells[i * TILES : (i + 1) * TILES]
        out.append((jnp.concatenate([one] * 4, axis=1) * code).astype(BF16))
    return out


def turn_tiles(tiles, table):
    turned = mm(jnp.concatenate(tiles, axis=0), table)
    turned = [turned[i * TILES : (i + 1) * TILES] for i in range(len(tiles))]
    return [turned[i + 2] + turned[i + 1] + turned[i] for i in range(0, len(tiles), 3)]


def begin(copies, sems):
    started = [pltpu.make_async_copy(a, b, sems.at[i]) for i, (a, b) in enumerate(copies)]
    for one in started:
        one.start()
    return started


def pack_meta_kernel(
    blocks,
    tile_cap,
    parcel_cap,
    species,
    diffusivity,
    low_partner,
    high_partner,
    low_orient,
    high_orient,
    table,
    block,
    cell,
    live,
    flow,
    diff,
    m_ref,
    strips_ref,
    strip_ref,
    column_ref,
    code_ref,
    slot_ref,
    table_in,
    vel_in,
    dif_in,
    bottom,
    top,
    d_own,
    small,
    parcel,
    sems,
):
    layers = species.shape[1]
    copies = begin(
        [(high_partner, small.at[0]), (low_partner, small.at[1])]
        + [(high_orient, small.at[2]), (low_orient, small.at[3])]
        + [(block, parcel.at[0]), (live, parcel.at[1]), (cell, parcel.at[2])]
        + [(table, table_in), (diffusivity, d_own)]
        + [(species.at[:, layers - 8 :], top), (species.at[:, 0:8], bottom)]
        + [(flow.at[0, 0:8], vel_in), (diff.at[0, 0:8], dif_in)],
        sems,
    )
    me = lax.axis_index("blk")
    inside, turn = inside_table(), orient_table()
    tile = iota((TILES, STRIP), 0)
    strip_of = ones((iota((TILES, LANES), 0) >> 3) == iota((TILES, LANES), 1))
    column_of = ones((tile & 7) == ((iota((TILES, STRIP), 1) >> 3) & 7))
    code_of = ones(iota((8, STRIP), 0) == (iota((8, STRIP), 1) >> 6))
    rows = table.shape[0]
    earlier = ones(iota((rows, rows), 0) < iota((rows, rows), 1))
    for copy in copies[0:4]:
        copy.wait()
    for k in range(2):
        place = place_matrix(small[k], blocks, tile_cap)
        strip_ref[k] = mm(place, strip_of)
        column_ref[k] = mm(place, column_of)
        code = ones(iota((8, TILES), 0) == small[2 + k])
        code_ref[k] = mm(mm_nt(place, code).astype(BF16), code_of)
    for copy in copies[4:8]:
        copy.wait()
    target = parcel[0]
    alive = parcel[1] == 1
    onehot = ones((iota((blocks, rows), 0) == target) & alive, F32)
    rank = jnp.sum(onehot * mm(onehot.astype(BF16), earlier), axis=0, keepdims=True)
    rank = rank.astype(jnp.int32)
    slot_ref[...] = jnp.broadcast_to(jnp.where(alive, target * parcel_cap + rank, -1), (8, rows))
    pick = ones(iota((8, PV), 1) == iota((8, PV), 0) + 1)
    parts = split(table_in[...], 3)
    columns = mm_nt(pick, parts[2]) + mm_nt(pick, parts[1]) + mm_nt(pick, parts[0])
    p1, p2 = columns[0:1], columns[1:2]
    soft = jnp.maximum(p1, 0.0) + jnp.log1p(jnp.exp(-jnp.abs(p1)))
    sig = 1.0 / (1.0 + jnp.exp(-p2))
    fields = jnp.concatenate(
        [(parcel[2] + 1).astype(F32), soft, sig, jnp.zeros((5, rows), F32)], axis=0
    )
    share = 48 // parcel_cap
    lane = rank + lax.rem(me, share) * parcel_cap + 64 * (lax.div(me, share) & 1)
    goal = jnp.where(alive, target * LANES + lane, -1)
    spots = ones(iota((blocks * LANES, rows), 0) == goal)
    meta = mm_nt(jnp.concatenate(split(fields, 3), axis=0), spots)
    meta = meta[16:24] + meta[8:16] + meta[0:8]
    copies[8].wait()
    d0, d1 = d_own[0:1, 0:1], d_own[0:1, 1:2]
    lanes = iota((1, LANES), 1)
    own = jnp.where(lanes == 0, d0, jnp.where(lanes == 1, d1, 0.0))
    for b in range(blocks):
        m_ref[4 * b : 4 * b + 3, :] = meta[0:3, b * LANES : (b + 1) * LANES]
        m_ref[4 * b + 3 : 4 * b + 4, :] = own
    copies[9].wait()
    copies[10].wait()
    top0, top1 = to_strips(top[0, 7:8, :]), to_strips(top[1, 7:8, :])
    low0, low1 = to_strips(bottom[0, 0:1, :]), to_strips(bottom[1, 0:1, :])
    strips_ref[...] = jnp.concatenate([top0, top1, low0, low1], axis=0)
    tiles = []
    for k, face in enumerate((d0 * top0 + d1 * top1, d0 * low0 + d1 * low1)):
        strip = strip_ref[k][:, 0:8].astype(BF16)
        tiles += take_tiles([face], strip, column_ref[k], code_ref[k], inside)
    high, low = turn_tiles(tiles, turn)
    m_ref[4 * blocks : 4 * blocks + TILES, :] = jnp.where(lanes < 64, high, low)
    copies[11].wait()
    copies[12].wait()


def pack_rows_kernel(
    blocks,
    tile_cap,
    parcel_cap,
    table_in,
    vel_in,
    dif_in,
    strips_ref,
    strip_ref,
    column_ref,
    code_ref,
    slot_ref,
    z_half,
    out_ref,
    edge_ref,
):
    inside, turn = inside_table(), orient_table()
    faces = [strips_ref[8 * i : 8 * i + 8, :] for i in range(4)]
    vel, dif = to_strips(vel_in[0:1, :]), to_strips(dif_in[0:1, :])
    edge_ref[...] = jnp.concatenate([vel, dif], axis=0)
    tiles = []
    for k, some in enumerate((faces[0:2], faces[2:4] + [vel, dif])):
        strip = strip_ref[k][:, 0:8].astype(BF16)
        tiles += take_tiles(some, strip, column_ref[k], code_ref[k], inside)
    high0, high1, low0, low1, vel, dif = turn_tiles(tiles, turn)
    left = iota((TILES, LANES), 1) < 64
    pairs = [
        jnp.where(left, high0, pltpu.roll(high1, 64, 1)),
        jnp.where(left, pltpu.roll(low0, 64, 1), low1),
        jnp.where(left, pltpu.roll(vel, 64, 1), dif),
    ]
    rows = table_in.shape[0]
    send = ones(iota((blocks * parcel_cap, rows), 0) == slot_ref[0:1, :])
    parts = split(table_in[...], 3)
    sent = mm(send, parts[2]) + mm(send, parts[1]) + mm(send, parts[0])
    for b in range(blocks):
        out_ref[b, 0:parcel_cap, :] = sent[b * parcel_cap : (b + 1) * parcel_cap]
        for k in range(PAIRS - 1):
            at = parcel_cap + k * tile_cap
            out_ref[b, at : at + tile_cap, :] = pairs[k][b * tile_cap : (b + 1) * tile_cap]


def pass_kernel(*refs):
    pass


def add_kernel(near_ref, far_ref, out_ref):
    out_ref[...] = near_ref[...] + far_ref[...]


def assemble_kernel(blocks, tile_cap, parcel_cap, buf_ref, m0, m1, m2, m3, z_half, out_ref):
    ghost = parcel_cap + (PAIRS - 1) * tile_cap
    z = slice(4 * blocks, 4 * blocks + TILES)
    total = (m0[z, :] + m1[z, :]) + (m2[z, :] + m3[z, :])
    near = m0[0 : 4 * blocks, :] + pltpu.roll(m1[0 : 4 * blocks, :], 64, 1)
    far = m2[0 : 4 * blocks, :] + pltpu.roll(m3[0 : 4 * blocks, :], 64, 1)
    for b in range(blocks):
        out_ref[b, 0:ghost, :] = buf_ref[b, 0:ghost, :]
        out_ref[b, ghost : ghost + tile_cap, :] = total[b * tile_cap : (b + 1) * tile_cap]
        at = ghost + tile_cap
        out_ref[b, at : at + 3, :] = near[4 * b : 4 * b + 3]
        out_ref[b, at + 3 : at + 6, :] = far[4 * b : 4 * b + 3]
        if at + 6 < out_ref.shape[1]:
            out_ref[b, at + 6 :, :] = jnp.zeros((out_ref.shape[1] - at - 6, LANES), F32)


def sum_kernel(
    own_ref, other_ref, factors, d_other, after0, after1, zh_ref, fh_ref, d_own, sem
):
    half, cells = zh_ref.shape
    copy = pltpu.make_async_copy(factors, d_own, sem)
    copy.start()
    first = (lax.axis_index("sp") & 1) == 0
    copy.wait()
    d0, d1, e0, e1 = d_own[0:1, 0:1], d_own[0:1, 1:2], d_other[0:1, 0:1], d_other[0:1, 1:2]
    for lo in range(0, cells, LANES):
        at = slice(lo, lo + LANES)
        own, other = own_ref[0, :, at], other_ref[0, :, at]
        z = d0 * own + d1 * own_ref[1, :, at] + (e0 * other + e1 * other_ref[1, :, at])
        zh_ref[:, at] = jnp.where(first, z[0:half], z[half:])
        fh_ref[:, at] = jnp.where(first, own[0:half], other[half:])


def flux(velocity, diffusion, d, upper, lower, weight):
    middle = 0.5 * (upper + lower)
    return velocity * middle - diffusion * (d * (upper - lower) - middle * weight)


def transposed_parts(get, out_ref, at, parts, group):
    square = jnp.concatenate([get(4 * group + i) for i in range(4)], axis=0).T
    for k, part in enumerate(split(square, parts)):
        out_ref[at + k * LANES : at + (k + 1) * LANES, group * LANES : (group + 1) * LANES] = part


def inner_kernel(
    flow,
    diff,
    vol,
    species,
    za_ref,
    zb_ref,
    m0,
    base_ref,
    edge_ref,
    flow_ref,
    diff_ref,
    vol_ref,
    species_ref,
    z_ref,
    sems,
):
    layers, cells = vol.shape
    half = layers // 2
    quarter = cells // 4
    parts = [slice(i * quarter, (i + 1) * quarter) for i in range(4)]
    copies = {}
    for n, i in enumerate((3, 2, 1, 0)):
        p = parts[i]
        copies[i] = begin(
            [
                (flow.at[:, :, p], flow_ref.at[:, :, p]),
                (diff.at[:, :, p], diff_ref.at[:, :, p]),
                (vol.at[:, p], vol_ref.at[:, p]),
                (species.at[:, :, p], species_ref.at[:, :, p]),
            ],
            sems.at[n],
        )
    first = (lax.axis_index("sp") & 1) == 0
    z_ref[0:half, :] = jnp.where(first, za_ref[...], zb_ref[...])
    z_ref[half:, :] = jnp.where(first, zb_ref[...], za_ref[...])
    shape = (layers, LANES)
    row, lane = iota(shape, 0), iota(shape, 1)
    left = lane < 64
    inner = row > 0
    off_wall = (lane & 63) != 0
    ds = (m0[3:4, 0:1], m0[3:4, 1:2])
    above = [jnp.zeros(shape, F32)] * 2
    for j in range(cells // LANES - 1, -1, -1):
        here = slice(j * LANES, (j + 1) * LANES)
        before = slice(max(j - 1, 0) * LANES, (max(j - 1, 0) + 1) * LANES)
        if here.stop % quarter == 0:
            for copy in copies[here.start // quarter][0:3]:
                copy.wait()
            if j == cells // LANES - 1:
                copies[here.start // quarter][3].wait()
        if here.start % quarter == 0 and j > 0:
            copies[before.start // quarter][3].wait()
        z = z_ref[:, here]
        unders = (
            lambda y: pltpu.roll(y, 1, 0),
            lambda y: pltpu.roll(y, 64, 1),
            lambda y: pltpu.roll(y, 1, 1),
        )
        z_under = (
            pltpu.roll(z, 1, 0),
            pltpu.roll(jnp.where(left, z, z_ref[:, before]), 64, 1),
            pltpu.roll(z, 1, 1),
        )
        masks = (inner, (lane >= 64) if j == 0 else None, off_wall)
        means, slopes = [], []
        for k in range(3):
            g = diff_ref[k, :, here]
            c = 0.5 * (flow_ref[k, :, here] + g * (z - z_under[k]))
            if masks[k] is not None:
                c, g = jnp.where(masks[k], c, 0.0), jnp.where(masks[k], g, 0.0)
            means.append(c)
            slopes.append(g)
        scale = section_step * vol_ref[:, here]
        for s in range(2):
            y = species_ref[s, :, here]
            under = (
                pltpu.roll(y, 1, 0),
                pltpu.roll(jnp.where(left, y, species_ref[s, :, before]), 64, 1),
                pltpu.roll(y, 1, 1),
            )
            f_layer, f_row, f_column = (
                (y + u) * c - (y - u) * (g * ds[s]) for u, c, g in zip(under, means, slopes)
            )
            divergence = (
                (pltpu.roll(f_layer, layers - 1, 0) - f_layer)
                + (pltpu.roll(jnp.where(left, above[s], f_row), 64, 1) - f_row)
                + (pltpu.roll(f_column, LANES - 1, 1) - f_column)
            )
            base_ref[s, :, here] = y - scale * divergence
            above[s] = f_row
    ends = [ref[i : i + 1, :] for ref in (z_ref, vol_ref) for i in (0, layers - 1)]
    edge_ref[...] = jnp.concatenate([to_strips(end) for end in ends], axis=0)


def fuel_half_kernel(near_ref, far_ref, edge_ref, out_ref):
    out_ref[...] = jnp.where(lax.axis_index("sp") < 2, near_ref[...], far_ref[...])


def fuel_kernel(own_ref, other_ref, out_ref):
    first = (lax.axis_index("sp") & 1) == 0

    def field(j):
        here = slice(j * LANES, (j + 1) * LANES)
        a, b = own_ref[:, here], other_ref[:, here]
        return jnp.concatenate([jnp.where(first, a, b), jnp.where(first, b, a)], axis=0)

    for group in range(FACE // LANES // 4):
        transposed_parts(field, out_ref, 0, 2, group)


def ghost_faces(pairs, strip, column, inside):
    lane = iota((TILES, LANES), 1)
    parts = []
    for pair, right in pairs:
        one = jnp.where((lane >= 64) if right else (lane < 64), pair, 0.0)
        parts += split(one, 3)
    wide = mm_nt(jnp.concatenate(parts, axis=0), inside)
    wide = [
        (wide[i * TILES : (i + 1) * TILES] * column).astype(BF16) for i in range(len(parts))
    ]
    wide = mm_tn(strip, jnp.concatenate(wide, axis=1))
    wide = [wide[:, i * STRIP : (i + 1) * STRIP] for i in range(len(parts))]
    return [wide[3 * i + 2] + wide[3 * i + 1] + wide[3 * i] for i in range(len(pairs))]


def final_kernel(
    blocks,
    tile_cap,
    parcel_cap,
    got_ref,
    fuel_ref,
    base_ref,
    species,
    vol,
    flow,
    zedge_ref,
    fedge_ref,
    strips_ref,
    strip_ref,
    column_ref,
    m0,
    new_hbm,
    arrived_hbm,
    new_ref,
    arrived_ref,
    spots,
    loads,
    edge,
    species_ref,
    vol_ref,
    flow_ref,
    number_ref,
    number_smem,
    rows_ref,
    sems,
    flow_sem,
    number_sem,
):
    layers, cells = base_ref.shape[1:]
    fetch = begin([(species, species_ref), (vol, vol_ref)], sems.at[1])
    fetch_flow = begin(
        [
            (flow.at[:, :, j * LANES : (j + 1) * LANES], flow_ref.at[:, j * layers : (j + 1) * layers])
            for j in range(cells // LANES)
        ],
        flow_sem,
    )
    tall_rows = layers * cells // LANES
    share = 48 // parcel_cap
    groups = blocks // share
    ghost = parcel_cap
    at = parcel_cap + PAIRS * tile_cap

    def pair(k):
        lo = ghost + k * tile_cap
        return jnp.concatenate([got_ref[b, lo : lo + tile_cap, :] for b in range(blocks)], axis=0)

    def meta(f, h, g):
        total = None
        for i in range(share):
            lo = at + 3 * h + f
            one = got_ref[g * share + i, lo : lo + 1, :]
            total = one if total is None else total + one
        return total

    quad = groups // 2
    order = [(h, g) for h in range(2) for g in range(groups)]
    four = [
        jnp.concatenate([meta(f, h, g) for f in range(3) for h, g in order[quad * i : quad * i + quad]], axis=0)
        for i in range(4)
    ]
    lane = iota((3 * quad, LANES), 1)
    a, b, c, d = four
    b_low, c_high = pltpu.roll(b, 96, 1), pltpu.roll(c, 48, 1)
    full = [
        jnp.where(lane < 48, a, jnp.where(lane < 96, pltpu.roll(a, 112, 1), b_low)),
        jnp.where(
            lane < 64,
            jnp.where(lane < 16, b_low, pltpu.roll(b, 80, 1)),
            jnp.where(lane < 112, pltpu.roll(c, 64, 1), c_high),
        ),
        jnp.where(
            lane < 32, c_high, jnp.where(lane < 80, pltpu.roll(d, 32, 1), pltpu.roll(d, 16, 1))
        ),
    ]

    def field(f, arrays):
        return jnp.concatenate([one[quad * f : quad * f + quad] for one in arrays], axis=0)

    def locate(numbers):
        number = numbers.astype(jnp.int32) - 1
        layer = lax.shift_right_arithmetic(number, 12)
        row = (lax.shift_right_arithmetic(number, 7) & 31) * layers + layer
        used = number >= 0
        return jnp.where(used, row, -1), jnp.where(used, number & (LANES - 1), -1)

    chunks = 3 * quad
    own_row, own_lane = locate(field(0, four[0:2]))
    number_ref[...] = jnp.maximum(own_row, 0)
    fetch_number = pltpu.make_async_copy(number_ref, number_smem, number_sem)
    fetch_number.start()
    cell_row, cell_lane = locate(field(0, full))
    soft, sig = field(1, full), field(2, full)
    sublane = iota((LANES, LANES), 0)
    tall = iota((tall_rows, LANES), 0)
    for c in range(chunks):
        spots[:, c * LANES : (c + 1) * LANES] = ones(tall == cell_row[c : c + 1])
    inside = inside_table()
    p0, p1, p2, p3 = (pair(k) for k in range(PAIRS))
    below0, below1, below_z = ghost_faces(
        [(p0, 0), (p0, 1), (p3, 0)], strip_ref[1].astype(BF16)[:, 0:8], column_ref[1], inside
    )
    above0, above1, top_v, top_d, above_z = ghost_faces(
        [(p1, 0), (p1, 1), (p2, 0), (p2, 1), (p3, 1)],
        strip_ref[0].astype(BF16)[:, 0:8],
        column_ref[0],
        inside,
    )
    z_bottom, z_top = zedge_ref[0:8, :], zedge_ref[8:16, :]
    bottom_scale, top_scale = section_step * zedge_ref[16:24, :], section_step * zedge_ref[24:32, :]
    bottom_v, bottom_d = fedge_ref[0:8, :], fedge_ref[8:16, :]
    for s, (below, above) in enumerate(((below0, above0), (below1, above1))):
        d = m0[3:4, s : s + 1]
        high = strips_ref[8 * s : 8 * s + 8, :]
        low = strips_ref[16 + 8 * s : 24 + 8 * s, :]
        f_low = flux(bottom_v, bottom_d, d, low, below, z_bottom - below_z)
        f_high = flux(top_v, top_d, d, above, high, above_z - z_top)
        edge[2 * s : 2 * s + 1, :] = from_strips(bottom_scale * f_low)
        edge[2 * s + 1 : 2 * s + 2, :] = from_strips(top_scale * f_high)
    width = 2 * LANES
    lefts = iota((1, LANES), 1) < 64
    evaporated = []
    for c in range(0, chunks, 2):
        both = mm(fuel_ref[...], spots[:, c * LANES : c * LANES + width])
        both = both[0:LANES] + both[LANES:]
        for i in range(2):
            mask = sublane == cell_lane[c + i : c + i + 1]
            fuel = jnp.sum(
                jnp.where(mask, both[:, i * LANES : (i + 1) * LANES], 0.0), axis=0, keepdims=True
            )
            gone = soft[c + i : c + i + 1] * (sig[c + i : c + i + 1] - fuel)
            evaporated.append(gone)
            for k, part in enumerate(split(jnp.where(mask, gone, 0.0), 2)):
                loads[k * LANES : (k + 1) * LANES, (c + i) * LANES : (c + i + 1) * LANES] = part
    source = mm_nt(spots[...], loads[...])
    source = source[:, 0:LANES] + source[:, LANES:]
    row = iota((8, LANES), 0)
    delta = (jnp.where(lax.axis_index("sp") == 0, 1.0, 0.0), 0.0)
    for copy in fetch:
        copy.wait()
    quarter = cells // 4
    copies = []
    for j in range(cells // LANES):
        here = slice(j * LANES, (j + 1) * LANES)
        part = source[j * layers : (j + 1) * layers] * (section_step * vol_ref[:, here])
        for s in range(2):
            new = base_ref[s, :, here] + part * (delta[s] - species_ref[s, :, here])
            first = jnp.where(row == 0, edge[2 * s : 2 * s + 1, here], 0.0)
            last = jnp.where(row == 7, edge[2 * s + 1 : 2 * s + 2, here], 0.0)
            new_ref[s, 0:8, here] = new[0:8] + first
            new_ref[s, 8 : layers - 8, here] = new[8 : layers - 8]
            new_ref[s, layers - 8 :, here] = new[layers - 8 :] - last
        if here.stop % quarter == 0:
            p = slice(here.stop - quarter, here.stop)
            copies.append(
                pltpu.make_async_copy(
                    new_ref.at[:, :, p], new_hbm.at[:, :, p], sems.at[0, p.start // quarter]
                )
            )
            copies[-1].start()
    size = share * parcel_cap
    fetch_number.wait()
    for copy in fetch_flow:
        copy.wait()

    for g in range(groups):
        for i in range(size):
            where = number_smem[g, 64 * (g & 1) + i]
            for f in range(3):
                rows_ref[f, 64 * g + i : 64 * g + i + 1, :] = flow_ref[f, pl.ds(where, 1), :]
    index, column = iota((8, PV), 0), iota((8, PV), 1)
    spread = ones(index == 0)
    take = ones((index < 2) & (column == 0))
    index, column = iota((3 * 2 * LANES, PV), 0), iota((3 * 2 * LANES, PV), 1)
    into = ones(column == 3 + lax.div(index, 2 * LANES))
    drag = (iota((size, PV), 1) >= 3) & (iota((size, PV), 1) <= 5)
    keep = jnp.where(drag, 1.0 - friction_timescale, 1.0)
    lane_of = own_lane.astype(F32)
    gone0 = jnp.concatenate(evaporated[0:quad], axis=0)
    gone1 = jnp.concatenate(evaporated[quad : 2 * quad], axis=0)
    lane = iota((quad, LANES), 1)
    evaporated = jnp.concatenate(
        [
            jnp.where(lane < 64, gone0, pltpu.roll(gone0, 16, 1)),
            jnp.where(
                lane < 32,
                pltpu.roll(gone0, 32, 1),
                jnp.where(lane < 64, pltpu.roll(gone1, 32, 1), pltpu.roll(gone1, 48, 1)),
            ),
        ],
        axis=0,
    )
    none = jnp.zeros((6, LANES), F32)
    for h in range(groups // 2):
        a, b = 2 * h, 2 * h + 1
        lanes = jnp.where(lefts, lane_of[a : a + 1], lane_of[b : b + 1])
        lanes = jnp.concatenate([lanes, lanes, none], axis=0).astype(BF16)
        mask = mm_tn(lanes, spread) == iota((LANES, PV), 1).astype(F32)
        gone = jnp.where(lefts, evaporated[a : a + 1], evaporated[b : b + 1])
        head = gone.astype(BF16).astype(F32)
        change = -mm_tn(jnp.concatenate([head, gone - head, none], axis=0).astype(BF16), take)
        fields = []
        for f in range(3):
            fields += split(jnp.where(mask, rows_ref[f, h * LANES : (h + 1) * LANES, :], 0.0), 2)
        change = change + friction_timescale * mm(jnp.concatenate(fields, axis=1), into)
        for i in range(2):
            g = 2 * h + i
            table = jnp.concatenate(
                [got_ref[g * share + k, 0:parcel_cap, :] for k in range(share)], axis=0
            )
            arrived_ref[g * size : (g + 1) * size, :] = table * keep + change[64 * i : 64 * i + size]
    copies.append(pltpu.make_async_copy(arrived_ref, arrived_hbm, sems.at[1, 2]))
    copies[-1].start()
    for copy in copies:
        copy.wait()


def fast(count=1):
    return [pl.BlockSpec(memory_space=pltpu.VMEM)] * count


def slow(count=1):
    return [pl.BlockSpec(memory_space=pltpu.HBM)] * count


def call(kernel, name, out, in_specs, scratch=(), out_specs=None, kib=1024):
    out_specs = out_specs or fast(len(out))
    run = pl.pallas_call(
        kernel,
        out_shape=tuple(
            (pltpu.HBM if spec.memory_space is pltpu.HBM else pltpu.VMEM)(s, t)
            for (s, t), spec in zip(out, out_specs, strict=True)
        ),
        in_specs=in_specs,
        out_specs=tuple(out_specs),
        scratch_shapes=list(scratch),
        compiler_params=pltpu.CompilerParams(vmem_limit_bytes=VMEM_LIMIT),
        cost_estimate=pl.CostEstimate(flops=0, transcendentals=0, bytes_accessed=kib * 1024),
        name=name,
    )

    def held(*operands):
        return run(
            *(
                pltpu.with_memory_space_constraint(a, spec.memory_space)
                for a, spec in zip(operands, in_specs, strict=True)
            )
        )

    return held


def after(value, *others):
    return pl.pallas_call(
        pass_kernel,
        out_shape=pltpu.VMEM(value.shape, value.dtype),
        in_specs=fast(1 + len(others)),
        out_specs=fast()[0],
        input_output_aliases={0: 0},
        name="after",
    )(*(pltpu.with_memory_space_constraint(a, pltpu.VMEM) for a in (value, *others)))


def dma(*count):
    return pltpu.SemaphoreType.DMA(count)


def body(
    species,
    interface_normal_flow,
    face_diffusion,
    inv_volume,
    diffusivity,
    low_partner,
    high_partner,
    low_orient,
    high_orient,
    droplet_table,
    parcel_block,
    parcel_cell,
    parcel_live,
):
    blocks = lax.axis_size("blk")
    local_species, layers, cells = species.shape
    parcels = droplet_table.shape[0]
    tile_cap = max(1, TILES // blocks)
    parcel_cap = 3 * parcels // (2 * blocks)
    sizes = (blocks, tile_cap, parcel_cap)
    tall = layers * cells // LANES
    rows = -(-(parcel_cap + PAIRS * tile_cap + 6) // 8) * 8
    groups = blocks * parcel_cap // 48
    int_row = (1, parcels)
    vmem = pltpu.VMEM

    def swap(value, bit):
        return lax.ppermute(value, "sp", [(i, i ^ bit) for i in range(lax.axis_size("sp"))])

    factors = diffusivity.reshape(1, local_species)
    other_species = swap(species, 1)
    other_factors = swap(factors, 1)

    m0, strips, strip, column, code, slot, table, vel, dif = call(
        functools.partial(pack_meta_kernel, *sizes),
        "pack_meta",
        [
            ((4 * blocks + TILES, LANES), F32),
            ((32, STRIP), F32),
            ((2, TILES, LANES), F32),
            ((2, TILES, STRIP), F32),
            ((2, TILES, STRIP), F32),
            ((8, parcels), jnp.int32),
            (droplet_table.shape, F32),
            ((8, cells), F32),
            ((8, cells), F32),
        ],
        slow(12),
        [
            vmem((local_species, 8, cells), F32),
            vmem((local_species, 8, cells), F32),
            vmem((1, local_species), F32),
            vmem((4, 1, TILES), jnp.int32),
            vmem((3,) + int_row, jnp.int32),
            dma(13),
        ],
        kib=10000,
    )(
        species,
        factors,
        low_partner,
        high_partner,
        low_orient,
        high_orient,
        droplet_table,
        parcel_block.reshape(int_row),
        parcel_cell.reshape(int_row),
        parcel_live.reshape(int_row),
        interface_normal_flow,
        face_diffusion,
    )
    m1, m2, m3 = swap(m0, 1), swap(m0, 2), swap(m0, 3)


    packed, edge_flow = call(
        functools.partial(pack_rows_kernel, *sizes),
        "pack_rows",
        [((blocks, rows, LANES), F32), ((16, STRIP), F32)],
        fast(9),
        kib=10000,
    )(
        table,
        vel,
        dif,
        strips,
        strip,
        column,
        code,
        slot,
        m0,
    )
    z_half, fuel_half = call(
        sum_kernel,
        "chip_sum",
        [((layers // 2, cells), F32), ((layers // 2, cells), F32)],
        fast(2) + slow(1) + fast(3),
        [vmem((1, local_species), F32), pltpu.SemaphoreType.DMA],
        kib=4680,
    )(species, other_species, factors, other_factors, m1, edge_flow)
    z_half = after(z_half, m2, m3)
    z_far = swap(z_half, 2)
    fuel_far = swap(fuel_half, 2)

    (z_own,) = call(
        add_kernel, "z_own", [((layers // 2, cells), F32)], fast(2), kib=1000
    )(z_half, z_far)
    (ready,) = call(
        functools.partial(assemble_kernel, *sizes),
        "assemble",
        [((blocks, rows, LANES), F32)],
        fast(6),
        kib=2880,
    )(packed, m0, m1, m2, m3, z_half)
    z_other = swap(z_own, 1)
    got = lax.all_to_all(ready, "blk", split_axis=0, concat_axis=0, tiled=True)

    base, edge_z = call(
        inner_kernel,
        "inner_flux",
        [(species.shape, F32), ((32, STRIP), F32)],
        slow(4) + fast(3),
        [
            vmem(interface_normal_flow.shape, F32),
            vmem(face_diffusion.shape, F32),
            vmem((layers, cells), F32),
            vmem(species.shape, F32),
            vmem((layers, cells), F32),
            dma(4, 4),
        ],
        kib=25200,
    )(
        interface_normal_flow,
        face_diffusion,
        inv_volume,
        species,
        z_own,
        z_other,
        m0,
    )

    (fuel_own,) = call(
        fuel_half_kernel,
        "fuel_half",
        [((layers // 2, cells), F32)],
        fast(3),
        kib=360,
    )(fuel_half, fuel_far, edge_z)
    fuel_other = swap(fuel_own, 1)
    (fuel_parts,) = call(
        fuel_kernel, "fuel_parts", [((2 * LANES, tall), BF16)], fast(2), kib=1080
    )(fuel_own, fuel_other)

    return call(
        functools.partial(final_kernel, *sizes),
        "final",
        [(species.shape, F32), ((blocks * parcel_cap, PV), F32)],
        fast(3) + slow(3) + fast(6),
        [
            vmem(species.shape, F32),
            vmem((blocks * parcel_cap, PV), F32),
            vmem((tall, 3 * groups // 2 * LANES), BF16),
            vmem((2 * LANES, 3 * groups // 2 * LANES), BF16),
            vmem((8, cells), F32),
            vmem(species.shape, F32),
            vmem((layers, cells), F32),
            vmem((3, tall, LANES), F32),
            vmem((groups, LANES), jnp.int32),
            pltpu.SMEM((groups, LANES), jnp.int32),
            vmem((3, 64 * groups, PV), F32),
            dma(2, 4),
            dma(cells // LANES),
            pltpu.SemaphoreType.DMA,
        ],
        slow(2),
        kib=32400,
    )(
        got,
        fuel_parts,
        base,
        species,
        inv_volume,
        interface_normal_flow,
        edge_z,
        edge_flow,
        strips,
        strip,
        column,
        m0,
    )


def solution(mesh):
    placed = (
        P("sp", "blk", None),
        P(None, "blk", None),
        P(None, "blk", None),
        P("blk", None),
        P("sp"),
        P("blk", None),
        P("blk", None),
        P("blk", None),
        P("blk", None),
        P(("blk", "sp"), None),
        P(("blk", "sp"), None),
        P(("blk", "sp")),
        P(("blk", "sp")),
    )
    return jax.shard_map(
        body,
        mesh=mesh,
        in_specs=placed,
        out_specs=(P("sp", "blk", None), P(("blk", "sp"), None)),
        check_vma=False,
    )
```

```python
import functools

import jax
import jax.numpy as jnp
from jax import lax
from jax.experimental import pallas as pl
from jax.experimental.pallas import tpu as pltpu
from jax.sharding import PartitionSpec as P

PV = 128
BJ = 64
BK = 64
TILE_SIDE = 8
TILES = 64
LANES = 128
FACE = BJ * BK
STRIP = TILE_SIDE * BK
PAIRS = 4

section_step = 0.5
friction_timescale = 0.3

F32 = jnp.float32
BF16 = jnp.bfloat16
VMEM_LIMIT = 16 * 1024 * 1024


def iota(shape, dim):
    return lax.broadcasted_iota(jnp.int32, shape, dim)


def mm(a, b):
    return lax.dot_general(a, b, (((1,), (0,)), ((), ())), preferred_element_type=F32)


def mm_nt(a, b):
    return lax.dot_general(a, b, (((1,), (1,)), ((), ())), preferred_element_type=F32)


def mm_tn(a, b):
    return lax.dot_general(a, b, (((0,), (0,)), ((), ())), preferred_element_type=F32)


def ones(condition, kind=BF16):
    return jnp.where(condition, 1.0, 0.0).astype(kind)


def split(value, parts):
    out = []
    for _ in range(parts - 1):
        head = value.astype(BF16)
        out.append(head)
        value = value - head.astype(F32)
    out.append(value.astype(BF16))
    return out


def inside_table():
    lane, cell = iota((STRIP, LANES), 0), iota((STRIP, LANES), 1) & 63
    return ones(((lane >> 6) == (cell >> 3)) & ((lane & 7) == (cell & 7)))


def orient_table():
    shape = (8 * TILES, LANES)
    code, source = iota(shape, 0) >> 6, iota(shape, 0) & 63
    column = iota(shape, 1)
    r, c = (column >> 3) & 7, column & 7
    back = column >= 64
    turned = code >= 4
    flip_r, flip_c = (code & 1) * 7, ((code >> 1) & 1) * 7
    there = jnp.where(turned, (c ^ flip_c) * 8 + (r ^ flip_r), (r ^ flip_r) * 8 + (c ^ flip_c))
    r0, c0 = jnp.where(turned, c, r), jnp.where(turned, r, c)
    return ones(source == jnp.where(back, (r0 ^ flip_r) * 8 + (c0 ^ flip_c), there))


def place_matrix(partner, blocks, cap):
    onehot = ones(iota((blocks, TILES), 0) == partner, F32)
    earlier = ones(iota((TILES, TILES), 0) < iota((TILES, TILES), 1))
    rank = jnp.sum(onehot * mm(onehot.astype(BF16), earlier), axis=0, keepdims=True)
    slot = partner * cap + rank.astype(jnp.int32)
    return ones(iota((TILES, TILES), 0) == slot)


def to_strips(row):
    return jnp.concatenate([row[:, i * STRIP : (i + 1) * STRIP] for i in range(8)], axis=0)


def from_strips(strips):
    return jnp.concatenate([strips[i : i + 1] for i in range(8)], axis=1)


def take_tiles(faces, strip, column, code, inside):
    parts = [part for face in faces for part in split(face, 2)]
    wide = mm(strip, jnp.concatenate(parts, axis=1))
    tall = jnp.concatenate(
        [(wide[:, i * STRIP : (i + 1) * STRIP] * column).astype(BF16) for i in range(len(parts))],
        axis=0,
    )
    cells = mm(tall, inside)
    out = []
    for i in range(len(parts)):
        one = cells[i * TILES : (i + 1) * TILES]
        out.append((jnp.concatenate([one] * 4, axis=1) * code).astype(BF16))
    return out


def turn_tiles(tiles, table):
    turned = mm(jnp.concatenate(tiles, axis=0), table)
    turned = [turned[i * TILES : (i + 1) * TILES] for i in range(len(tiles))]
    return [turned[i + 1] + turned[i] for i in range(0, len(tiles), 2)]


def begin(copies, sems):
    started = [pltpu.make_async_copy(a, b, sems.at[i]) for i, (a, b) in enumerate(copies)]
    for one in started:
        one.start()
    return started


def z_row(blocks):
    return (3 * blocks // 2) // 8 * 8 + 8


def pack_meta_kernel(
    blocks,
    tile_cap,
    parcel_cap,
    species,
    diffusivity,
    low_partner,
    high_partner,
    low_orient,
    high_orient,
    table,
    block,
    cell,
    live,
    flow,
    diff,
    m_ref,
    factor_ref,
    strips_ref,
    strip_ref,
    column_ref,
    code_ref,
    slot_ref,
    table_in,
    vel_in,
    dif_in,
    bottom,
    top,
    d_own,
    small,
    parcel,
    sems,
):
    layers = species.shape[1]
    copies = begin(
        [(high_partner, small.at[0]), (low_partner, small.at[1])]
        + [(high_orient, small.at[2]), (low_orient, small.at[3])]
        + [(block, parcel.at[0]), (live, parcel.at[1]), (cell, parcel.at[2])]
        + [(table, table_in), (diffusivity, d_own)]
        + [(species.at[:, layers - 8 :], top), (species.at[:, 0:8], bottom)]
        + [(flow.at[0, 0:8], vel_in), (diff.at[0, 0:8], dif_in)],
        sems,
    )
    me = lax.axis_index("blk")
    inside, turn = inside_table(), orient_table()
    tile = iota((TILES, STRIP), 0)
    strip_of = ones((iota((TILES, LANES), 0) >> 3) == iota((TILES, LANES), 1))
    column_of = ones((tile & 7) == ((iota((TILES, STRIP), 1) >> 3) & 7))
    code_of = ones(iota((8, STRIP), 0) == (iota((8, STRIP), 1) >> 6))
    rows = table.shape[0]
    earlier = ones(iota((rows, rows), 0) < iota((rows, rows), 1))
    for copy in copies[0:4]:
        copy.wait()
    for k in range(2):
        place = place_matrix(small[k], blocks, tile_cap)
        strip_ref[k] = mm(place, strip_of)
        column_ref[k] = mm(place, column_of)
        code = ones(iota((8, TILES), 0) == small[2 + k])
        code_ref[k] = mm(mm_nt(place, code).astype(BF16), code_of)
    for copy in copies[4:8]:
        copy.wait()
    target = parcel[0]
    alive = parcel[1] == 1
    onehot = ones((iota((blocks, rows), 0) == target) & alive, F32)
    rank = jnp.sum(onehot * mm(onehot.astype(BF16), earlier), axis=0, keepdims=True)
    rank = rank.astype(jnp.int32)
    slot_ref[...] = jnp.broadcast_to(jnp.where(alive, target * parcel_cap + rank, -1), (8, rows))
    pick = ones(iota((8, PV), 1) == iota((8, PV), 0) + 1)
    parts = split(table_in[...], 3)
    columns = mm_nt(pick, parts[2]) + mm_nt(pick, parts[1]) + mm_nt(pick, parts[0])
    p1, p2 = columns[0:1], columns[1:2]
    soft = jnp.maximum(p1, 0.0) + jnp.log1p(jnp.exp(-jnp.abs(p1)))
    sig = 1.0 / (1.0 + jnp.exp(-p2))
    fields = jnp.concatenate(
        [(parcel[2] + 1).astype(F32), soft, sig, jnp.zeros((5, rows), F32)], axis=0
    )
    share = 48 // parcel_cap
    lane = rank + lax.rem(me, share) * parcel_cap
    goal = jnp.where(alive, target * 64 + lane, -1)
    spots = ones(iota((blocks * 64, rows), 0) == goal)
    meta = mm_nt(jnp.concatenate(split(fields, 3), axis=0), spots)
    meta = meta[16:24] + meta[8:16] + meta[0:8]
    copies[8].wait()
    d0, d1 = d_own[0:1, 0:1], d_own[0:1, 1:2]
    lanes = iota((1, LANES), 1)
    own = jnp.where(lanes == 0, d0, jnp.where(lanes == 1, d1, 0.0))
    for k in range(blocks // 2):
        m_ref[3 * k : 3 * k + 3, :] = meta[0:3, k * LANES : (k + 1) * LANES]
    factor_ref[...] = jnp.broadcast_to(own, (8, LANES))
    z_at = z_row(blocks)
    m_ref[3 * blocks // 2 : z_at, :] = jnp.broadcast_to(own, (z_at - 3 * blocks // 2, LANES))
    copies[9].wait()
    copies[10].wait()
    top0, top1 = to_strips(top[0, 7:8, :]), to_strips(top[1, 7:8, :])
    low0, low1 = to_strips(bottom[0, 0:1, :]), to_strips(bottom[1, 0:1, :])
    strips_ref[...] = jnp.concatenate([top0, top1, low0, low1], axis=0)
    tiles = []
    for k, face in enumerate((d0 * top0 + d1 * top1, d0 * low0 + d1 * low1)):
        strip = strip_ref[k][:, 0:8].astype(BF16)
        tiles += take_tiles([face], strip, column_ref[k], code_ref[k], inside)
    high, low = turn_tiles(tiles, turn)
    m_ref[z_at : z_at + TILES, :] = jnp.where(lanes < 64, high, low)
    copies[11].wait()
    copies[12].wait()


def pack_rows_kernel(
    blocks,
    tile_cap,
    parcel_cap,
    table_in,
    vel_in,
    dif_in,
    strips_ref,
    strip_ref,
    column_ref,
    code_ref,
    slot_ref,
    z_half,
    out_ref,
    edge_ref,
):
    inside, turn = inside_table(), orient_table()
    faces = [strips_ref[8 * i : 8 * i + 8, :] for i in range(4)]
    vel, dif = to_strips(vel_in[0:1, :]), to_strips(dif_in[0:1, :])
    edge_ref[...] = jnp.concatenate([vel, dif], axis=0)
    tiles = []
    for k, some in enumerate((faces[0:2], faces[2:4] + [vel, dif])):
        strip = strip_ref[k][:, 0:8].astype(BF16)
        tiles += take_tiles(some, strip, column_ref[k], code_ref[k], inside)
    high0, high1, low0, low1, vel, dif = turn_tiles(tiles, turn)
    left = iota((TILES, LANES), 1) < 64
    pairs = [
        jnp.where(left, high0, pltpu.roll(high1, 64, 1)),
        jnp.where(left, pltpu.roll(low0, 64, 1), low1),
        jnp.where(left, pltpu.roll(vel, 64, 1), dif),
    ]
    rows = table_in.shape[0]
    send = ones(iota((blocks * parcel_cap, rows), 0) == slot_ref[0:1, :])
    parts = split(table_in[...], 3)
    sent = mm(send, parts[2]) + mm(send, parts[1]) + mm(send, parts[0])
    for b in range(blocks):
        out_ref[b, 0:parcel_cap, :] = sent[b * parcel_cap : (b + 1) * parcel_cap]
        for k in range(PAIRS - 1):
            at = parcel_cap + k * tile_cap
            out_ref[b, at : at + tile_cap, :] = pairs[k][b * tile_cap : (b + 1) * tile_cap]


def pass_kernel(*refs):
    pass


def add_kernel(near_ref, far_ref, out_ref):
    out_ref[...] = near_ref[...] + far_ref[...]


def assemble_kernel(blocks, tile_cap, parcel_cap, buf_ref, m0, m1, m2, m3, z_half, out_ref):
    ghost = parcel_cap + (PAIRS - 1) * tile_cap
    z = slice(z_row(blocks), z_row(blocks) + TILES)
    total = (m0[z, :] + m1[z, :]) + (m2[z, :] + m3[z, :])
    used = 3 * blocks // 2
    right = lax.div(lax.axis_index("blk"), 48 // parcel_cap) & 1
    here = (iota((used, LANES), 1) >> 6) == right
    near, far = [], []
    for out, a, b in ((near, m0, m1), (far, m2, m3)):
        a, b = a[0:used, :], b[0:used, :]
        a_turned, b_turned = pltpu.roll(a, 64, 1), pltpu.roll(b, 64, 1)
        for half in range(2):
            same = right == half
            out.append(
                jnp.where(here, jnp.where(same, a, a_turned), jnp.where(same, b_turned, b))
            )
    for b in range(blocks):
        out_ref[b, 0:ghost, :] = buf_ref[b, 0:ghost, :]
        out_ref[b, ghost : ghost + tile_cap, :] = total[b * tile_cap : (b + 1) * tile_cap]
        at = ghost + tile_cap
        row = b // 2 * 3
        out_ref[b, at : at + 3, :] = near[b % 2][row : row + 3]
        out_ref[b, at + 3 : at + 6, :] = far[b % 2][row : row + 3]
        if at + 6 < out_ref.shape[1]:
            out_ref[b, at + 6 :, :] = jnp.zeros((out_ref.shape[1] - at - 6, LANES), F32)


def sum_kernel(
    own_ref, other_ref, factors, d_other, after0, after1, zh_ref, fh_ref, d_own, sem
):
    half, cells = zh_ref.shape
    copy = pltpu.make_async_copy(factors, d_own, sem)
    copy.start()
    first = (lax.axis_index("sp") & 1) == 0
    copy.wait()
    d0, d1, e0, e1 = d_own[0:1, 0:1], d_own[0:1, 1:2], d_other[0:1, 0:1], d_other[0:1, 1:2]
    for lo in range(0, cells, LANES):
        at = slice(lo, lo + LANES)
        own, other = own_ref[0, :, at], other_ref[0, :, at]
        z = d0 * own + d1 * own_ref[1, :, at] + (e0 * other + e1 * other_ref[1, :, at])
        zh_ref[:, at] = jnp.where(first, z[0:half], z[half:])
        fh_ref[:, at] = jnp.where(first, own[0:half], other[half:])


def flux(velocity, diffusion, d, upper, lower, weight):
    middle = 0.5 * (upper + lower)
    return velocity * middle - diffusion * (d * (upper - lower) - middle * weight)


def transposed_parts(get, out_ref, at, parts, group):
    square = jnp.concatenate([get(4 * group + i) for i in range(4)], axis=0).T
    for k, part in enumerate(split(square, parts)):
        out_ref[at + k * LANES : at + (k + 1) * LANES, group * LANES : (group + 1) * LANES] = part


def inner_kernel(
    flow,
    diff,
    vol,
    species,
    za_ref,
    zb_ref,
    m0,
    base_ref,
    edge_ref,
    flow_ref,
    diff_ref,
    vol_ref,
    species_ref,
    z_ref,
    sems,
):
    layers, cells = vol.shape
    half = layers // 2
    quarter = cells // 4
    parts = [slice(i * quarter, (i + 1) * quarter) for i in range(4)]
    copies = {}
    for n, i in enumerate((3, 2, 1, 0)):
        p = parts[i]
        copies[i] = begin(
            [
                (flow.at[:, :, p], flow_ref.at[:, :, p]),
                (diff.at[:, :, p], diff_ref.at[:, :, p]),
                (vol.at[:, p], vol_ref.at[:, p]),
                (species.at[:, :, p], species_ref.at[:, :, p]),
            ],
            sems.at[n],
        )
    first = (lax.axis_index("sp") & 1) == 0
    z_ref[0:half, :] = jnp.where(first, za_ref[...], zb_ref[...])
    z_ref[half:, :] = jnp.where(first, zb_ref[...], za_ref[...])
    shape = (layers, LANES)
    row, lane = iota(shape, 0), iota(shape, 1)
    left = lane < 64
    inner = row > 0
    off_wall = (lane & 63) != 0
    ds = (m0[0:1, 0:1], m0[0:1, 1:2])
    above = [jnp.zeros(shape, F32)] * 2
    for j in range(cells // LANES - 1, -1, -1):
        here = slice(j * LANES, (j + 1) * LANES)
        before = slice(max(j - 1, 0) * LANES, (max(j - 1, 0) + 1) * LANES)
        if here.stop % quarter == 0:
            for copy in copies[here.start // quarter][0:3]:
                copy.wait()
            if j == cells // LANES - 1:
                copies[here.start // quarter][3].wait()
        if here.start % quarter == 0 and j > 0:
            copies[before.start // quarter][3].wait()
        z = z_ref[:, here]
        unders = (
            lambda y: pltpu.roll(y, 1, 0),
            lambda y: pltpu.roll(y, 64, 1),
            lambda y: pltpu.roll(y, 1, 1),
        )
        z_under = (
            pltpu.roll(z, 1, 0),
            pltpu.roll(jnp.where(left, z, z_ref[:, before]), 64, 1),
            pltpu.roll(z, 1, 1),
        )
        masks = (inner, (lane >= 64) if j == 0 else None, off_wall)
        means, slopes = [], []
        for k in range(3):
            g = diff_ref[k, :, here]
            c = 0.5 * (flow_ref[k, :, here] + g * (z - z_under[k]))
            if masks[k] is not None:
                c, g = jnp.where(masks[k], c, 0.0), jnp.where(masks[k], g, 0.0)
            means.append(c)
            slopes.append(g)
        scale = section_step * vol_ref[:, here]
        for s in range(2):
            y = species_ref[s, :, here]
            under = (
                pltpu.roll(y, 1, 0),
                pltpu.roll(jnp.where(left, y, species_ref[s, :, before]), 64, 1),
                pltpu.roll(y, 1, 1),
            )
            f_layer, f_row, f_column = (
                (y + u) * c - (y - u) * (g * ds[s]) for u, c, g in zip(under, means, slopes)
            )
            divergence = (
                (pltpu.roll(f_layer, layers - 1, 0) - f_layer)
                + (pltpu.roll(jnp.where(left, above[s], f_row), 64, 1) - f_row)
                + (pltpu.roll(f_column, LANES - 1, 1) - f_column)
            )
            base_ref[s, :, here] = y - scale * divergence
            above[s] = f_row
    ends = [ref[i : i + 1, :] for ref in (z_ref, vol_ref) for i in (0, layers - 1)]
    edge_ref[...] = jnp.concatenate([to_strips(end) for end in ends], axis=0)


def fuel_half_kernel(near_ref, far_ref, edge_ref, out_ref):
    out_ref[...] = jnp.where(lax.axis_index("sp") < 2, near_ref[...], far_ref[...])


def fuel_kernel(own_ref, other_ref, out_ref):
    first = (lax.axis_index("sp") & 1) == 0

    def field(j):
        here = slice(j * LANES, (j + 1) * LANES)
        a, b = own_ref[:, here], other_ref[:, here]
        return jnp.concatenate([jnp.where(first, a, b), jnp.where(first, b, a)], axis=0)

    for group in range(FACE // LANES // 4):
        transposed_parts(field, out_ref, 0, 2, group)


def ghost_faces(pairs, strip, column, inside):
    lane = iota((TILES, LANES), 1)
    parts = []
    for pair, right in pairs:
        one = jnp.where((lane >= 64) if right else (lane < 64), pair, 0.0)
        parts += split(one, 2)
    wide = mm_nt(jnp.concatenate(parts, axis=0), inside)
    wide = [
        (wide[i * TILES : (i + 1) * TILES] * column).astype(BF16) for i in range(len(parts))
    ]
    wide = mm_tn(strip, jnp.concatenate(wide, axis=1))
    wide = [wide[:, i * STRIP : (i + 1) * STRIP] for i in range(len(parts))]
    return [wide[2 * i + 1] + wide[2 * i] for i in range(len(pairs))]


def final_kernel(
    blocks,
    tile_cap,
    parcel_cap,
    got_ref,
    fuel_ref,
    base_ref,
    species,
    vol,
    flow,
    zedge_ref,
    fedge_ref,
    strips_ref,
    strip_ref,
    column_ref,
    m0,
    new_hbm,
    arrived_hbm,
    new_ref,
    arrived_ref,
    spots,
    loads,
    edge,
    species_ref,
    vol_ref,
    flow_ref,
    number_ref,
    number_smem,
    rows_ref,
    sems,
    flow_sem,
    number_sem,
):
    layers, cells = base_ref.shape[1:]
    fetch = begin([(species, species_ref), (vol, vol_ref)], sems.at[1])
    fetch_flow = begin(
        [
            (flow.at[:, :, j * LANES : (j + 1) * LANES], flow_ref.at[:, j * layers : (j + 1) * layers])
            for j in range(cells // LANES)
        ],
        flow_sem,
    )
    tall_rows = layers * cells // LANES
    share = 48 // parcel_cap
    groups = blocks // share
    ghost = parcel_cap
    at = parcel_cap + PAIRS * tile_cap

    def pair(k):
        lo = ghost + k * tile_cap
        return jnp.concatenate([got_ref[b, lo : lo + tile_cap, :] for b in range(blocks)], axis=0)

    def meta(f, h, g):
        total = None
        for i in range(share):
            lo = at + 3 * h + f
            one = got_ref[g * share + i, lo : lo + 1, :]
            total = one if total is None else total + one
        return total

    quad = groups // 2
    order = [(h, g) for h in range(2) for g in range(groups)]
    four = [
        jnp.concatenate([meta(f, h, g) for f in range(3) for h, g in order[quad * i : quad * i + quad]], axis=0)
        for i in range(4)
    ]
    lane = iota((3 * quad, LANES), 1)
    a, b, c, d = four
    b_low, c_high = pltpu.roll(b, 96, 1), pltpu.roll(c, 48, 1)
    full = [
        jnp.where(lane < 48, a, jnp.where(lane < 96, pltpu.roll(a, 112, 1), b_low)),
        jnp.where(
            lane < 64,
            jnp.where(lane < 16, b_low, pltpu.roll(b, 80, 1)),
            jnp.where(lane < 112, pltpu.roll(c, 64, 1), c_high),
        ),
        jnp.where(
            lane < 32, c_high, jnp.where(lane < 80, pltpu.roll(d, 32, 1), pltpu.roll(d, 16, 1))
        ),
    ]

    def field(f, arrays):
        return jnp.concatenate([one[quad * f : quad * f + quad] for one in arrays], axis=0)

    def locate(numbers):
        number = numbers.astype(jnp.int32) - 1
        layer = lax.shift_right_arithmetic(number, 12)
        row = (lax.shift_right_arithmetic(number, 7) & 31) * layers + layer
        used = number >= 0
        return jnp.where(used, row, -1), jnp.where(used, number & (LANES - 1), -1)

    chunks = 3 * quad
    own_row, own_lane = locate(field(0, four[0:2]))
    number_ref[...] = jnp.maximum(own_row, 0)
    fetch_number = pltpu.make_async_copy(number_ref, number_smem, number_sem)
    fetch_number.start()
    cell_row, cell_lane = locate(field(0, full))
    soft, sig = field(1, full), field(2, full)
    sublane = iota((LANES, LANES), 0)
    tall = iota((tall_rows, LANES), 0)
    for c in range(chunks):
        spots[:, c * LANES : (c + 1) * LANES] = ones(tall == cell_row[c : c + 1])
    inside = inside_table()
    p0, p1, p2, p3 = (pair(k) for k in range(PAIRS))
    below0, below1, below_z = ghost_faces(
        [(p0, 0), (p0, 1), (p3, 0)], strip_ref[1].astype(BF16)[:, 0:8], column_ref[1], inside
    )
    above0, above1, top_v, top_d, above_z = ghost_faces(
        [(p1, 0), (p1, 1), (p2, 0), (p2, 1), (p3, 1)],
        strip_ref[0].astype(BF16)[:, 0:8],
        column_ref[0],
        inside,
    )
    z_bottom, z_top = zedge_ref[0:8, :], zedge_ref[8:16, :]
    bottom_scale, top_scale = section_step * zedge_ref[16:24, :], section_step * zedge_ref[24:32, :]
    bottom_v, bottom_d = fedge_ref[0:8, :], fedge_ref[8:16, :]
    for s, (below, above) in enumerate(((below0, above0), (below1, above1))):
        d = m0[0:1, s : s + 1]
        high = strips_ref[8 * s : 8 * s + 8, :]
        low = strips_ref[16 + 8 * s : 24 + 8 * s, :]
        f_low = flux(bottom_v, bottom_d, d, low, below, z_bottom - below_z)
        f_high = flux(top_v, top_d, d, above, high, above_z - z_top)
        edge[2 * s : 2 * s + 1, :] = from_strips(bottom_scale * f_low)
        edge[2 * s + 1 : 2 * s + 2, :] = from_strips(top_scale * f_high)
    width = 2 * LANES
    lefts = iota((1, LANES), 1) < 64
    evaporated = []
    for c in range(0, chunks, 2):
        both = mm(fuel_ref[...], spots[:, c * LANES : c * LANES + width])
        both = both[0:LANES] + both[LANES:]
        for i in range(2):
            mask = sublane == cell_lane[c + i : c + i + 1]
            fuel = jnp.sum(
                jnp.where(mask, both[:, i * LANES : (i + 1) * LANES], 0.0), axis=0, keepdims=True
            )
            gone = soft[c + i : c + i + 1] * (sig[c + i : c + i + 1] - fuel)
            evaporated.append(gone)
            for k, part in enumerate(split(jnp.where(mask, gone, 0.0), 2)):
                loads[k * LANES : (k + 1) * LANES, (c + i) * LANES : (c + i + 1) * LANES] = part
    source = mm_nt(spots[...], loads[...])
    source = source[:, 0:LANES] + source[:, LANES:]
    row = iota((8, LANES), 0)
    delta = (jnp.where(lax.axis_index("sp") == 0, 1.0, 0.0), 0.0)
    for copy in fetch:
        copy.wait()
    quarter = cells // 4
    copies = []
    for j in range(cells // LANES):
        here = slice(j * LANES, (j + 1) * LANES)
        part = source[j * layers : (j + 1) * layers] * (section_step * vol_ref[:, here])
        for s in range(2):
            new = base_ref[s, :, here] + part * (delta[s] - species_ref[s, :, here])
            first = jnp.where(row == 0, edge[2 * s : 2 * s + 1, here], 0.0)
            last = jnp.where(row == 7, edge[2 * s + 1 : 2 * s + 2, here], 0.0)
            new_ref[s, 0:8, here] = new[0:8] + first
            new_ref[s, 8 : layers - 8, here] = new[8 : layers - 8]
            new_ref[s, layers - 8 :, here] = new[layers - 8 :] - last
        if here.stop % quarter == 0:
            p = slice(here.stop - quarter, here.stop)
            copies.append(
                pltpu.make_async_copy(
                    new_ref.at[:, :, p], new_hbm.at[:, :, p], sems.at[0, p.start // quarter]
                )
            )
            copies[-1].start()
    size = share * parcel_cap
    fetch_number.wait()
    for copy in fetch_flow:
        copy.wait()

    for g in range(groups):
        for i in range(size):
            where = number_smem[g, 64 * (g & 1) + i]
            for f in range(3):
                rows_ref[f, 64 * g + i : 64 * g + i + 1, :] = flow_ref[f, pl.ds(where, 1), :]
    index, column = iota((8, PV), 0), iota((8, PV), 1)
    spread = ones(index == 0)
    take = ones((index < 2) & (column == 0))
    index, column = iota((3 * 2 * LANES, PV), 0), iota((3 * 2 * LANES, PV), 1)
    into = ones(column == 3 + lax.div(index, 2 * LANES))
    drag = (iota((size, PV), 1) >= 3) & (iota((size, PV), 1) <= 5)
    keep = jnp.where(drag, 1.0 - friction_timescale, 1.0)
    lane_of = own_lane.astype(F32)
    gone0 = jnp.concatenate(evaporated[0:quad], axis=0)
    gone1 = jnp.concatenate(evaporated[quad : 2 * quad], axis=0)
    lane = iota((quad, LANES), 1)
    evaporated = jnp.concatenate(
        [
            jnp.where(lane < 64, gone0, pltpu.roll(gone0, 16, 1)),
            jnp.where(
                lane < 32,
                pltpu.roll(gone0, 32, 1),
                jnp.where(lane < 64, pltpu.roll(gone1, 32, 1), pltpu.roll(gone1, 48, 1)),
            ),
        ],
        axis=0,
    )
    none = jnp.zeros((6, LANES), F32)
    for h in range(groups // 2):
        a, b = 2 * h, 2 * h + 1
        lanes = jnp.where(lefts, lane_of[a : a + 1], lane_of[b : b + 1])
        lanes = jnp.concatenate([lanes, lanes, none], axis=0).astype(BF16)
        mask = mm_tn(lanes, spread) == iota((LANES, PV), 1).astype(F32)
        gone = jnp.where(lefts, evaporated[a : a + 1], evaporated[b : b + 1])
        head = gone.astype(BF16).astype(F32)
        change = -mm_tn(jnp.concatenate([head, gone - head, none], axis=0).astype(BF16), take)
        fields = []
        for f in range(3):
            fields += split(jnp.where(mask, rows_ref[f, h * LANES : (h + 1) * LANES, :], 0.0), 2)
        change = change + friction_timescale * mm(jnp.concatenate(fields, axis=1), into)
        for i in range(2):
            g = 2 * h + i
            table = jnp.concatenate(
                [got_ref[g * share + k, 0:parcel_cap, :] for k in range(share)], axis=0
            )
            arrived_ref[g * size : (g + 1) * size, :] = table * keep + change[64 * i : 64 * i + size]
    copies.append(pltpu.make_async_copy(arrived_ref, arrived_hbm, sems.at[1, 2]))
    copies[-1].start()
    for copy in copies:
        copy.wait()


def fast(count=1):
    return [pl.BlockSpec(memory_space=pltpu.VMEM)] * count


def slow(count=1):
    return [pl.BlockSpec(memory_space=pltpu.HBM)] * count


def call(kernel, name, out, in_specs, scratch=(), out_specs=None, kib=1024):
    out_specs = out_specs or fast(len(out))
    run = pl.pallas_call(
        kernel,
        out_shape=tuple(
            (pltpu.HBM if spec.memory_space is pltpu.HBM else pltpu.VMEM)(s, t)
            for (s, t), spec in zip(out, out_specs, strict=True)
        ),
        in_specs=in_specs,
        out_specs=tuple(out_specs),
        scratch_shapes=list(scratch),
        compiler_params=pltpu.CompilerParams(vmem_limit_bytes=VMEM_LIMIT),
        cost_estimate=pl.CostEstimate(flops=0, transcendentals=0, bytes_accessed=kib * 1024),
        name=name,
    )

    def held(*operands):
        return run(
            *(
                pltpu.with_memory_space_constraint(a, spec.memory_space)
                for a, spec in zip(operands, in_specs, strict=True)
            )
        )

    return held


def after(value, *others):
    return pl.pallas_call(
        pass_kernel,
        out_shape=pltpu.VMEM(value.shape, value.dtype),
        in_specs=fast(1 + len(others)),
        out_specs=fast()[0],
        input_output_aliases={0: 0},
        name="after",
    )(*(pltpu.with_memory_space_constraint(a, pltpu.VMEM) for a in (value, *others)))


def dma(*count):
    return pltpu.SemaphoreType.DMA(count)


def body(
    species,
    interface_normal_flow,
    face_diffusion,
    inv_volume,
    diffusivity,
    low_partner,
    high_partner,
    low_orient,
    high_orient,
    droplet_table,
    parcel_block,
    parcel_cell,
    parcel_live,
):
    blocks = lax.axis_size("blk")
    local_species, layers, cells = species.shape
    parcels = droplet_table.shape[0]
    tile_cap = max(1, TILES // blocks)
    parcel_cap = 3 * parcels // (2 * blocks)
    sizes = (blocks, tile_cap, parcel_cap)
    tall = layers * cells // LANES
    rows = -(-(parcel_cap + PAIRS * tile_cap + 6) // 8) * 8
    groups = blocks * parcel_cap // 48
    int_row = (1, parcels)
    vmem = pltpu.VMEM

    def swap(value, bit):
        return lax.ppermute(value, "sp", [(i, i ^ bit) for i in range(lax.axis_size("sp"))])

    factors = diffusivity.reshape(1, local_species)
    other_species = swap(species, 1)
    other_factors = swap(factors, 1)

    m0, own_factors, strips, strip, column, code, slot, table, vel, dif = call(
        functools.partial(pack_meta_kernel, *sizes),
        "pack_meta",
        [
            ((z_row(blocks) + TILES, LANES), F32),
            ((8, LANES), F32),
            ((32, STRIP), F32),
            ((2, TILES, LANES), F32),
            ((2, TILES, STRIP), F32),
            ((2, TILES, STRIP), F32),
            ((8, parcels), jnp.int32),
            (droplet_table.shape, F32),
            ((8, cells), F32),
            ((8, cells), F32),
        ],
        slow(12),
        [
            vmem((local_species, 8, cells), F32),
            vmem((local_species, 8, cells), F32),
            vmem((1, local_species), F32),
            vmem((4, 1, TILES), jnp.int32),
            vmem((3,) + int_row, jnp.int32),
            dma(13),
        ],
        kib=10000,
    )(
        species,
        factors,
        low_partner,
        high_partner,
        low_orient,
        high_orient,
        droplet_table,
        parcel_block.reshape(int_row),
        parcel_cell.reshape(int_row),
        parcel_live.reshape(int_row),
        interface_normal_flow,
        face_diffusion,
    )
    m1, m2, m3 = swap(m0, 1), swap(m0, 2), swap(m0, 3)


    packed, edge_flow = call(
        functools.partial(pack_rows_kernel, *sizes),
        "pack_rows",
        [((blocks, rows, LANES), F32), ((16, STRIP), F32)],
        fast(9),
        kib=10000,
    )(
        table,
        vel,
        dif,
        strips,
        strip,
        column,
        code,
        slot,
        m0,
    )
    z_half, fuel_half = call(
        sum_kernel,
        "chip_sum",
        [((layers // 2, cells), F32), ((layers // 2, cells), F32)],
        fast(2) + slow(1) + fast(3),
        [vmem((1, local_species), F32), pltpu.SemaphoreType.DMA],
        kib=4680,
    )(species, other_species, factors, other_factors, m1, edge_flow)
    z_half = after(z_half, m2, m3)
    z_far = swap(z_half, 2)
    fuel_far = swap(fuel_half, 2)

    (z_own,) = call(
        add_kernel, "z_own", [((layers // 2, cells), F32)], fast(2), kib=1000
    )(z_half, z_far)
    (ready,) = call(
        functools.partial(assemble_kernel, *sizes),
        "assemble",
        [((blocks, rows, LANES), F32)],
        fast(6),
        kib=2880,
    )(packed, m0, m1, m2, m3, z_half)
    z_other = swap(z_own, 1)
    got = lax.all_to_all(ready, "blk", split_axis=0, concat_axis=0, tiled=True)

    base, edge_z = call(
        inner_kernel,
        "inner_flux",
        [(species.shape, F32), ((32, STRIP), F32)],
        slow(4) + fast(3),
        [
            vmem(interface_normal_flow.shape, F32),
            vmem(face_diffusion.shape, F32),
            vmem((layers, cells), F32),
            vmem(species.shape, F32),
            vmem((layers, cells), F32),
            dma(4, 4),
        ],
        kib=25200,
    )(
        interface_normal_flow,
        face_diffusion,
        inv_volume,
        species,
        z_own,
        z_other,
        own_factors,
    )

    (fuel_own,) = call(
        fuel_half_kernel,
        "fuel_half",
        [((layers // 2, cells), F32)],
        fast(3),
        kib=360,
    )(fuel_half, fuel_far, edge_z)
    fuel_other = swap(fuel_own, 1)
    (fuel_parts,) = call(
        fuel_kernel, "fuel_parts", [((2 * LANES, tall), BF16)], fast(2), kib=1080
    )(fuel_own, fuel_other)

    return call(
        functools.partial(final_kernel, *sizes),
        "final",
        [(species.shape, F32), ((blocks * parcel_cap, PV), F32)],
        fast(3) + slow(3) + fast(6),
        [
            vmem(species.shape, F32),
            vmem((blocks * parcel_cap, PV), F32),
            vmem((tall, 3 * groups // 2 * LANES), BF16),
            vmem((2 * LANES, 3 * groups // 2 * LANES), BF16),
            vmem((8, cells), F32),
            vmem(species.shape, F32),
            vmem((layers, cells), F32),
            vmem((3, tall, LANES), F32),
            vmem((groups, LANES), jnp.int32),
            pltpu.SMEM((groups, LANES), jnp.int32),
            vmem((3, 64 * groups, PV), F32),
            dma(2, 4),
            dma(cells // LANES),
            pltpu.SemaphoreType.DMA,
        ],
        slow(2),
        kib=32400,
    )(
        got,
        fuel_parts,
        base,
        species,
        inv_volume,
        interface_normal_flow,
        edge_z,
        edge_flow,
        strips,
        strip,
        column,
        own_factors,
    )


def solution(mesh):
    placed = (
        P("sp", "blk", None),
        P(None, "blk", None),
        P(None, "blk", None),
        P("blk", None),
        P("sp"),
        P("blk", None),
        P("blk", None),
        P("blk", None),
        P("blk", None),
        P(("blk", "sp"), None),
        P(("blk", "sp"), None),
        P(("blk", "sp")),
        P(("blk", "sp")),
    )
    return jax.shard_map(
        body,
        mesh=mesh,
        in_specs=placed,
        out_specs=(P("sp", "blk", None), P(("blk", "sp"), None)),
        check_vma=False,
    )
```

```python
import functools

import jax
import jax.numpy as jnp
from jax import lax
from jax.experimental import pallas as pl
from jax.experimental.pallas import tpu as pltpu
from jax.sharding import PartitionSpec as P

PV = 128
BJ = 64
BK = 64
TILE_SIDE = 8
TILES = 64
LANES = 128
FACE = BJ * BK
STRIP = TILE_SIDE * BK
PAIRS = 4

section_step = 0.5
friction_timescale = 0.3

F32 = jnp.float32
BF16 = jnp.bfloat16
VMEM_LIMIT = 16 * 1024 * 1024


def iota(shape, dim):
    return lax.broadcasted_iota(jnp.int32, shape, dim)


def mm(a, b):
    return lax.dot_general(a, b, (((1,), (0,)), ((), ())), preferred_element_type=F32)


def mm_nt(a, b):
    return lax.dot_general(a, b, (((1,), (1,)), ((), ())), preferred_element_type=F32)


def mm_tn(a, b):
    return lax.dot_general(a, b, (((0,), (0,)), ((), ())), preferred_element_type=F32)


def ones(condition, kind=BF16):
    return jnp.where(condition, 1.0, 0.0).astype(kind)


def split(value, parts):
    out = []
    for _ in range(parts - 1):
        head = value.astype(BF16)
        out.append(head)
        value = value - head.astype(F32)
    out.append(value.astype(BF16))
    return out


def inside_table():
    lane, cell = iota((STRIP, LANES), 0), iota((STRIP, LANES), 1) & 63
    return ones(((lane >> 6) == (cell >> 3)) & ((lane & 7) == (cell & 7)))


def orient_table():
    shape = (8 * TILES, LANES)
    code, source = iota(shape, 0) >> 6, iota(shape, 0) & 63
    column = iota(shape, 1)
    r, c = (column >> 3) & 7, column & 7
    back = column >= 64
    turned = code >= 4
    flip_r, flip_c = (code & 1) * 7, ((code >> 1) & 1) * 7
    there = jnp.where(turned, (c ^ flip_c) * 8 + (r ^ flip_r), (r ^ flip_r) * 8 + (c ^ flip_c))
    r0, c0 = jnp.where(turned, c, r), jnp.where(turned, r, c)
    return ones(source == jnp.where(back, (r0 ^ flip_r) * 8 + (c0 ^ flip_c), there))


def place_matrix(partner, blocks, cap):
    onehot = ones(iota((blocks, TILES), 0) == partner, F32)
    earlier = ones(iota((TILES, TILES), 0) < iota((TILES, TILES), 1))
    rank = jnp.sum(onehot * mm(onehot.astype(BF16), earlier), axis=0, keepdims=True)
    slot = partner * cap + rank.astype(jnp.int32)
    return ones(iota((TILES, TILES), 0) == slot)


def to_strips(row):
    return jnp.concatenate([row[:, i * STRIP : (i + 1) * STRIP] for i in range(8)], axis=0)


def from_strips(strips):
    return jnp.concatenate([strips[i : i + 1] for i in range(8)], axis=1)


def take_tiles(faces, strip, column, code, inside):
    parts = [part for face in faces for part in split(face, 2)]
    wide = mm(strip, jnp.concatenate(parts, axis=1))
    tall = jnp.concatenate(
        [(wide[:, i * STRIP : (i + 1) * STRIP] * column).astype(BF16) for i in range(len(parts))],
        axis=0,
    )
    cells = mm(tall, inside)
    out = []
    for i in range(len(parts)):
        one = cells[i * TILES : (i + 1) * TILES]
        out.append((jnp.concatenate([one] * 4, axis=1) * code).astype(BF16))
    return out


def turn_tiles(tiles, table):
    turned = mm(jnp.concatenate(tiles, axis=0), table)
    turned = [turned[i * TILES : (i + 1) * TILES] for i in range(len(tiles))]
    return [turned[i + 1] + turned[i] for i in range(0, len(tiles), 2)]


def begin(copies, sems):
    started = [pltpu.make_async_copy(a, b, sems.at[i]) for i, (a, b) in enumerate(copies)]
    for one in started:
        one.start()
    return started


def z_row(blocks):
    return (3 * blocks // 2) // 8 * 8 + 8


def pack_meta_kernel(
    blocks,
    tile_cap,
    parcel_cap,
    species,
    diffusivity,
    low_partner,
    high_partner,
    low_orient,
    high_orient,
    table,
    block,
    cell,
    live,
    flow,
    diff,
    m_ref,
    factor_ref,
    strips_ref,
    strip_ref,
    column_ref,
    code_ref,
    slot_ref,
    table_in,
    vel_in,
    dif_in,
    bottom,
    top,
    d_own,
    small,
    parcel,
    sems,
):
    layers = species.shape[1]
    copies = begin(
        [(high_partner, small.at[0]), (low_partner, small.at[1])]
        + [(high_orient, small.at[2]), (low_orient, small.at[3])]
        + [(block, parcel.at[0]), (live, parcel.at[1]), (cell, parcel.at[2])]
        + [(table, table_in), (diffusivity, d_own)]
        + [(species.at[:, layers - 8 :], top), (species.at[:, 0:8], bottom)]
        + [(flow.at[0, 0:8], vel_in), (diff.at[0, 0:8], dif_in)],
        sems,
    )
    me = lax.axis_index("blk")
    inside, turn = inside_table(), orient_table()
    tile = iota((TILES, STRIP), 0)
    strip_of = ones((iota((TILES, LANES), 0) >> 3) == iota((TILES, LANES), 1))
    column_of = ones((tile & 7) == ((iota((TILES, STRIP), 1) >> 3) & 7))
    code_of = ones(iota((8, STRIP), 0) == (iota((8, STRIP), 1) >> 6))
    rows = table.shape[0]
    earlier = ones(iota((rows, rows), 0) < iota((rows, rows), 1))
    for copy in copies[0:4]:
        copy.wait()
    for k in range(2):
        place = place_matrix(small[k], blocks, tile_cap)
        strip_ref[k] = mm(place, strip_of)
        column_ref[k] = mm(place, column_of)
        code = ones(iota((8, TILES), 0) == small[2 + k])
        code_ref[k] = mm(mm_nt(place, code).astype(BF16), code_of)
    for copy in copies[4:8]:
        copy.wait()
    target = parcel[0]
    alive = parcel[1] == 1
    onehot = ones((iota((blocks, rows), 0) == target) & alive, F32)
    rank = jnp.sum(onehot * mm(onehot.astype(BF16), earlier), axis=0, keepdims=True)
    rank = rank.astype(jnp.int32)
    slot_ref[...] = jnp.broadcast_to(jnp.where(alive, target * parcel_cap + rank, -1), (8, rows))
    pick = ones(iota((8, PV), 1) == iota((8, PV), 0) + 1)
    parts = split(table_in[...], 3)
    columns = mm_nt(pick, parts[2]) + mm_nt(pick, parts[1]) + mm_nt(pick, parts[0])
    p1, p2 = columns[0:1], columns[1:2]
    soft = jnp.maximum(p1, 0.0) + jnp.log1p(jnp.exp(-jnp.abs(p1)))
    sig = 1.0 / (1.0 + jnp.exp(-p2))
    fields = jnp.concatenate(
        [(parcel[2] + 1).astype(F32), soft, sig, jnp.zeros((5, rows), F32)], axis=0
    )
    share = 48 // parcel_cap
    lane = rank + lax.rem(me, share) * parcel_cap
    goal = jnp.where(alive, target * 64 + lane, -1)
    spots = ones(iota((blocks * 64, rows), 0) == goal)
    meta = mm_nt(jnp.concatenate(split(fields, 3), axis=0), spots)
    meta = meta[16:24] + meta[8:16] + meta[0:8]
    copies[8].wait()
    d0, d1 = d_own[0:1, 0:1], d_own[0:1, 1:2]
    lanes = iota((1, LANES), 1)
    own = jnp.where(lanes == 0, d0, jnp.where(lanes == 1, d1, 0.0))
    for k in range(blocks // 2):
        m_ref[3 * k : 3 * k + 3, :] = meta[0:3, k * LANES : (k + 1) * LANES]
    factor_ref[...] = jnp.broadcast_to(own, (8, LANES))
    z_at = z_row(blocks)
    m_ref[3 * blocks // 2 : z_at, :] = jnp.broadcast_to(own, (z_at - 3 * blocks // 2, LANES))
    copies[9].wait()
    copies[10].wait()
    top0, top1 = to_strips(top[0, 7:8, :]), to_strips(top[1, 7:8, :])
    low0, low1 = to_strips(bottom[0, 0:1, :]), to_strips(bottom[1, 0:1, :])
    strips_ref[...] = jnp.concatenate([top0, top1, low0, low1], axis=0)
    tiles = []
    for k, face in enumerate((d0 * top0 + d1 * top1, d0 * low0 + d1 * low1)):
        strip = strip_ref[k][:, 0:8].astype(BF16)
        tiles += take_tiles([face], strip, column_ref[k], code_ref[k], inside)
    high, low = turn_tiles(tiles, turn)
    m_ref[z_at : z_at + TILES, :] = jnp.where(lanes < 64, high, low)
    copies[11].wait()
    copies[12].wait()


def pack_rows_kernel(
    blocks,
    tile_cap,
    parcel_cap,
    table_in,
    vel_in,
    dif_in,
    strips_ref,
    strip_ref,
    column_ref,
    code_ref,
    slot_ref,
    z_half,
    out_ref,
    edge_ref,
):
    inside, turn = inside_table(), orient_table()
    faces = [strips_ref[8 * i : 8 * i + 8, :] for i in range(4)]
    vel, dif = to_strips(vel_in[0:1, :]), to_strips(dif_in[0:1, :])
    edge_ref[...] = jnp.concatenate([vel, dif], axis=0)
    tiles = []
    for k, some in enumerate((faces[0:2], faces[2:4] + [vel, dif])):
        strip = strip_ref[k][:, 0:8].astype(BF16)
        tiles += take_tiles(some, strip, column_ref[k], code_ref[k], inside)
    high0, high1, low0, low1, vel, dif = turn_tiles(tiles, turn)
    left = iota((TILES, LANES), 1) < 64
    pairs = [
        jnp.where(left, high0, pltpu.roll(high1, 64, 1)),
        jnp.where(left, pltpu.roll(low0, 64, 1), low1),
        jnp.where(left, pltpu.roll(vel, 64, 1), dif),
    ]
    rows = table_in.shape[0]
    send = ones(iota((blocks * parcel_cap, rows), 0) == slot_ref[0:1, :])
    parts = split(table_in[...], 3)
    sent = mm(send, parts[2]) + mm(send, parts[1]) + mm(send, parts[0])
    for b in range(blocks):
        out_ref[b, 0:parcel_cap, :] = sent[b * parcel_cap : (b + 1) * parcel_cap]
        for k in range(PAIRS - 1):
            at = parcel_cap + k * tile_cap
            out_ref[b, at : at + tile_cap, :] = pairs[k][b * tile_cap : (b + 1) * tile_cap]


def pass_kernel(*refs):
    pass


def add_kernel(near_ref, far_ref, out_ref):
    out_ref[...] = near_ref[...] + far_ref[...]


def assemble_kernel(blocks, tile_cap, parcel_cap, buf_ref, m0, m1, m2, m3, z_half, out_ref):
    ghost = parcel_cap + (PAIRS - 1) * tile_cap
    z = slice(z_row(blocks), z_row(blocks) + TILES)
    total = (m0[z, :] + m1[z, :]) + (m2[z, :] + m3[z, :])
    used = 3 * blocks // 2
    right = lax.div(lax.axis_index("blk"), 48 // parcel_cap) & 1
    here = (iota((used, LANES), 1) >> 6) == right
    near, far = [], []
    for out, a, b in ((near, m0, m1), (far, m2, m3)):
        a, b = a[0:used, :], b[0:used, :]
        a_turned, b_turned = pltpu.roll(a, 64, 1), pltpu.roll(b, 64, 1)
        for half in range(2):
            same = right == half
            out.append(
                jnp.where(here, jnp.where(same, a, a_turned), jnp.where(same, b_turned, b))
            )
    for b in range(blocks):
        out_ref[b, 0:ghost, :] = buf_ref[b, 0:ghost, :]
        out_ref[b, ghost : ghost + tile_cap, :] = total[b * tile_cap : (b + 1) * tile_cap]
        at = ghost + tile_cap
        row = b // 2 * 3
        out_ref[b, at : at + 3, :] = near[b % 2][row : row + 3]
        out_ref[b, at + 3 : at + 6, :] = far[b % 2][row : row + 3]
        if at + 6 < out_ref.shape[1]:
            out_ref[b, at + 6 :, :] = jnp.zeros((out_ref.shape[1] - at - 6, LANES), F32)


def sum_kernel(
    own_ref, other_ref, factors, d_other, after0, after1, zh_ref, fh_ref, d_own, sem
):
    half, cells = zh_ref.shape
    copy = pltpu.make_async_copy(factors, d_own, sem)
    copy.start()
    first = (lax.axis_index("sp") & 1) == 0
    copy.wait()
    d0, d1, e0, e1 = d_own[0:1, 0:1], d_own[0:1, 1:2], d_other[0:1, 0:1], d_other[0:1, 1:2]
    for lo in range(0, cells, LANES):
        at = slice(lo, lo + LANES)
        own, other = own_ref[0, :, at], other_ref[0, :, at]
        z = d0 * own + d1 * own_ref[1, :, at] + (e0 * other + e1 * other_ref[1, :, at])
        zh_ref[:, at] = jnp.where(first, z[0:half], z[half:])
        fh_ref[:, at] = jnp.where(first, own[0:half], other[half:])


def flux(velocity, diffusion, d, upper, lower, weight):
    middle = 0.5 * (upper + lower)
    return velocity * middle - diffusion * (d * (upper - lower) - middle * weight)


def transposed_parts(get, out_ref, at, parts, group):
    square = jnp.concatenate([get(4 * group + i) for i in range(4)], axis=0).T
    for k, part in enumerate(split(square, parts)):
        out_ref[at + k * LANES : at + (k + 1) * LANES, group * LANES : (group + 1) * LANES] = part


def inner_kernel(
    flow,
    diff,
    vol,
    species,
    za_ref,
    zb_ref,
    m0,
    base_ref,
    edge_ref,
    flow_ref,
    diff_ref,
    vol_ref,
    species_ref,
    z_ref,
    sems,
):
    layers, cells = vol.shape
    half = layers // 2
    quarter = cells // 4
    parts = [slice(i * quarter, (i + 1) * quarter) for i in range(4)]
    copies = {}
    for n, i in enumerate((3, 2, 1, 0)):
        p = parts[i]
        copies[i] = begin(
            [
                (flow.at[:, :, p], flow_ref.at[:, :, p]),
                (diff.at[:, :, p], diff_ref.at[:, :, p]),
                (vol.at[:, p], vol_ref.at[:, p]),
                (species.at[:, :, p], species_ref.at[:, :, p]),
            ],
            sems.at[n],
        )
    first = (lax.axis_index("sp") & 1) == 0
    z_ref[0:half, :] = jnp.where(first, za_ref[...], zb_ref[...])
    z_ref[half:, :] = jnp.where(first, zb_ref[...], za_ref[...])
    shape = (layers, LANES)
    row, lane = iota(shape, 0), iota(shape, 1)
    left = lane < 64
    inner = row > 0
    off_wall = (lane & 63) != 0
    ds = (m0[0:1, 0:1], m0[0:1, 1:2])
    above = [jnp.zeros(shape, F32)] * 2
    for j in range(cells // LANES - 1, -1, -1):
        here = slice(j * LANES, (j + 1) * LANES)
        before = slice(max(j - 1, 0) * LANES, (max(j - 1, 0) + 1) * LANES)
        if here.stop % quarter == 0:
            for copy in copies[here.start // quarter][0:3]:
                copy.wait()
            if j == cells // LANES - 1:
                copies[here.start // quarter][3].wait()
        if here.start % quarter == 0 and j > 0:
            copies[before.start // quarter][3].wait()
        z = z_ref[:, here]
        unders = (
            lambda y: pltpu.roll(y, 1, 0),
            lambda y: pltpu.roll(y, 64, 1),
            lambda y: pltpu.roll(y, 1, 1),
        )
        z_under = (
            pltpu.roll(z, 1, 0),
            pltpu.roll(jnp.where(left, z, z_ref[:, before]), 64, 1),
            pltpu.roll(z, 1, 1),
        )
        masks = (inner, (lane >= 64) if j == 0 else None, off_wall)
        means, slopes = [], []
        for k in range(3):
            g = diff_ref[k, :, here]
            c = 0.5 * (flow_ref[k, :, here] + g * (z - z_under[k]))
            if masks[k] is not None:
                c, g = jnp.where(masks[k], c, 0.0), jnp.where(masks[k], g, 0.0)
            means.append(c)
            slopes.append(g)
        scale = section_step * vol_ref[:, here]
        for s in range(2):
            y = species_ref[s, :, here]
            under = (
                pltpu.roll(y, 1, 0),
                pltpu.roll(jnp.where(left, y, species_ref[s, :, before]), 64, 1),
                pltpu.roll(y, 1, 1),
            )
            f_layer, f_row, f_column = (
                (y + u) * c - (y - u) * (g * ds[s]) for u, c, g in zip(under, means, slopes)
            )
            divergence = (
                (pltpu.roll(f_layer, layers - 1, 0) - f_layer)
                + (pltpu.roll(jnp.where(left, above[s], f_row), 64, 1) - f_row)
                + (pltpu.roll(f_column, LANES - 1, 1) - f_column)
            )
            base_ref[s, :, here] = y - scale * divergence
            above[s] = f_row
    ends = [ref[i : i + 1, :] for ref in (z_ref, vol_ref) for i in (0, layers - 1)]
    edge_ref[...] = jnp.concatenate([to_strips(end) for end in ends], axis=0)


def fuel_half_kernel(near_ref, far_ref, edge_ref, out_ref):
    out_ref[...] = jnp.where(lax.axis_index("sp") < 2, near_ref[...], far_ref[...])


def fuel_kernel(own_ref, other_ref, out_ref):
    first = (lax.axis_index("sp") & 1) == 0

    def field(j):
        here = slice(j * LANES, (j + 1) * LANES)
        a, b = own_ref[:, here], other_ref[:, here]
        return jnp.concatenate([jnp.where(first, a, b), jnp.where(first, b, a)], axis=0)

    for group in range(FACE // LANES // 4):
        transposed_parts(field, out_ref, 0, 2, group)


def ghost_faces(pairs, strip, column, inside):
    lane = iota((TILES, LANES), 1)
    parts = []
    for pair, right in pairs:
        one = jnp.where((lane >= 64) if right else (lane < 64), pair, 0.0)
        parts += split(one, 2)
    wide = mm_nt(jnp.concatenate(parts, axis=0), inside)
    wide = [
        (wide[i * TILES : (i + 1) * TILES] * column).astype(BF16) for i in range(len(parts))
    ]
    wide = mm_tn(strip, jnp.concatenate(wide, axis=1))
    wide = [wide[:, i * STRIP : (i + 1) * STRIP] for i in range(len(parts))]
    return [wide[2 * i + 1] + wide[2 * i] for i in range(len(pairs))]


def final_kernel(
    blocks,
    tile_cap,
    parcel_cap,
    got_ref,
    fuel_ref,
    base_ref,
    species,
    vol,
    flow,
    zedge_ref,
    fedge_ref,
    strips_ref,
    strip_ref,
    column_ref,
    m0,
    new_hbm,
    arrived_hbm,
    new_ref,
    arrived_ref,
    spots,
    loads,
    edge,
    species_ref,
    vol_ref,
    flow_ref,
    number_ref,
    number_smem,
    rows_ref,
    sems,
    flow_sem,
    number_sem,
):
    layers, cells = base_ref.shape[1:]
    fetch = begin([(species, species_ref), (vol, vol_ref)], sems.at[1])
    fetch_flow = begin(
        [
            (flow.at[:, :, j * LANES : (j + 1) * LANES], flow_ref.at[:, j * layers : (j + 1) * layers])
            for j in range(cells // LANES)
        ],
        flow_sem,
    )
    tall_rows = layers * cells // LANES
    share = 48 // parcel_cap
    groups = blocks // share
    ghost = parcel_cap
    at = parcel_cap + PAIRS * tile_cap

    def pair(k):
        lo = ghost + k * tile_cap
        return jnp.concatenate([got_ref[b, lo : lo + tile_cap, :] for b in range(blocks)], axis=0)

    def meta(f, h, g):
        total = None
        for i in range(share):
            lo = at + 3 * h + f
            one = got_ref[g * share + i, lo : lo + 1, :]
            total = one if total is None else total + one
        return total

    quad = groups // 2
    order = [(h, g) for h in range(2) for g in range(groups)]
    four = [
        jnp.concatenate([meta(f, h, g) for f in range(3) for h, g in order[quad * i : quad * i + quad]], axis=0)
        for i in range(4)
    ]
    lane = iota((3 * quad, LANES), 1)
    a, b, c, d = four
    b_low, c_high = pltpu.roll(b, 96, 1), pltpu.roll(c, 48, 1)
    full = [
        jnp.where(lane < 48, a, jnp.where(lane < 96, pltpu.roll(a, 112, 1), b_low)),
        jnp.where(
            lane < 64,
            jnp.where(lane < 16, b_low, pltpu.roll(b, 80, 1)),
            jnp.where(lane < 112, pltpu.roll(c, 64, 1), c_high),
        ),
        jnp.where(
            lane < 32, c_high, jnp.where(lane < 80, pltpu.roll(d, 32, 1), pltpu.roll(d, 16, 1))
        ),
    ]

    def field(f, arrays):
        return jnp.concatenate([one[quad * f : quad * f + quad] for one in arrays], axis=0)

    def locate(numbers):
        number = numbers.astype(jnp.int32) - 1
        layer = lax.shift_right_arithmetic(number, 12)
        row = (lax.shift_right_arithmetic(number, 7) & 31) * layers + layer
        used = number >= 0
        return jnp.where(used, row, -1), jnp.where(used, number & (LANES - 1), -1)

    chunks = 3 * quad
    own_row, own_lane = locate(field(0, four[0:2]))
    number_ref[...] = jnp.maximum(own_row, 0)
    fetch_number = pltpu.make_async_copy(number_ref, number_smem, number_sem)
    fetch_number.start()
    cell_row, cell_lane = locate(field(0, full))
    soft, sig = field(1, full), field(2, full)
    sublane = iota((LANES, LANES), 0)
    tall = iota((tall_rows, LANES), 0)
    width = 2 * LANES
    lefts = iota((1, LANES), 1) < 64
    evaporated = []
    for c in range(0, chunks, 2):
        for i in range(c, c + 2):
            spots[:, i * LANES : (i + 1) * LANES] = ones(tall == cell_row[i : i + 1])
        both = mm(fuel_ref[...], spots[:, c * LANES : c * LANES + width])
        both = both[0:LANES] + both[LANES:]
        for i in range(2):
            mask = sublane == cell_lane[c + i : c + i + 1]
            fuel = jnp.sum(
                jnp.where(mask, both[:, i * LANES : (i + 1) * LANES], 0.0), axis=0, keepdims=True
            )
            gone = soft[c + i : c + i + 1] * (sig[c + i : c + i + 1] - fuel)
            evaporated.append(gone)
            for k, part in enumerate(split(jnp.where(mask, gone, 0.0), 2)):
                loads[k * LANES : (k + 1) * LANES, (c + i) * LANES : (c + i + 1) * LANES] = part
    source = mm_nt(spots[...], loads[...])
    source = source[:, 0:LANES] + source[:, LANES:]
    inside = inside_table()
    p0, p1, p2, p3 = (pair(k) for k in range(PAIRS))
    below0, below1, below_z = ghost_faces(
        [(p0, 0), (p0, 1), (p3, 0)], strip_ref[1].astype(BF16)[:, 0:8], column_ref[1], inside
    )
    above0, above1, top_v, top_d, above_z = ghost_faces(
        [(p1, 0), (p1, 1), (p2, 0), (p2, 1), (p3, 1)],
        strip_ref[0].astype(BF16)[:, 0:8],
        column_ref[0],
        inside,
    )
    z_bottom, z_top = zedge_ref[0:8, :], zedge_ref[8:16, :]
    bottom_scale, top_scale = section_step * zedge_ref[16:24, :], section_step * zedge_ref[24:32, :]
    bottom_v, bottom_d = fedge_ref[0:8, :], fedge_ref[8:16, :]
    for s, (below, above) in enumerate(((below0, above0), (below1, above1))):
        d = m0[0:1, s : s + 1]
        high = strips_ref[8 * s : 8 * s + 8, :]
        low = strips_ref[16 + 8 * s : 24 + 8 * s, :]
        f_low = flux(bottom_v, bottom_d, d, low, below, z_bottom - below_z)
        f_high = flux(top_v, top_d, d, above, high, above_z - z_top)
        edge[2 * s : 2 * s + 1, :] = from_strips(bottom_scale * f_low)
        edge[2 * s + 1 : 2 * s + 2, :] = from_strips(top_scale * f_high)
    row = iota((8, LANES), 0)
    delta = (jnp.where(lax.axis_index("sp") == 0, 1.0, 0.0), 0.0)
    for copy in fetch:
        copy.wait()
    quarter = cells // 4
    copies = []
    for j in range(cells // LANES):
        here = slice(j * LANES, (j + 1) * LANES)
        part = source[j * layers : (j + 1) * layers] * (section_step * vol_ref[:, here])
        for s in range(2):
            new = base_ref[s, :, here] + part * (delta[s] - species_ref[s, :, here])
            first = jnp.where(row == 0, edge[2 * s : 2 * s + 1, here], 0.0)
            last = jnp.where(row == 7, edge[2 * s + 1 : 2 * s + 2, here], 0.0)
            new_ref[s, 0:8, here] = new[0:8] + first
            new_ref[s, 8 : layers - 8, here] = new[8 : layers - 8]
            new_ref[s, layers - 8 :, here] = new[layers - 8 :] - last
        if here.stop % quarter == 0:
            p = slice(here.stop - quarter, here.stop)
            copies.append(
                pltpu.make_async_copy(
                    new_ref.at[:, :, p], new_hbm.at[:, :, p], sems.at[0, p.start // quarter]
                )
            )
            copies[-1].start()
    size = share * parcel_cap
    fetch_number.wait()
    for copy in fetch_flow:
        copy.wait()

    for g in range(groups):
        for i in range(size):
            where = number_smem[g, 64 * (g & 1) + i]
            for f in range(3):
                rows_ref[f, 64 * g + i : 64 * g + i + 1, :] = flow_ref[f, pl.ds(where, 1), :]
    index, column = iota((8, PV), 0), iota((8, PV), 1)
    spread = ones(index == 0)
    take = ones((index < 2) & (column == 0))
    index, column = iota((3 * 2 * LANES, PV), 0), iota((3 * 2 * LANES, PV), 1)
    into = ones(column == 3 + lax.div(index, 2 * LANES))
    drag = (iota((size, PV), 1) >= 3) & (iota((size, PV), 1) <= 5)
    keep = jnp.where(drag, 1.0 - friction_timescale, 1.0)
    lane_of = own_lane.astype(F32)
    gone0 = jnp.concatenate(evaporated[0:quad], axis=0)
    gone1 = jnp.concatenate(evaporated[quad : 2 * quad], axis=0)
    lane = iota((quad, LANES), 1)
    evaporated = jnp.concatenate(
        [
            jnp.where(lane < 64, gone0, pltpu.roll(gone0, 16, 1)),
            jnp.where(
                lane < 32,
                pltpu.roll(gone0, 32, 1),
                jnp.where(lane < 64, pltpu.roll(gone1, 32, 1), pltpu.roll(gone1, 48, 1)),
            ),
        ],
        axis=0,
    )
    none = jnp.zeros((6, LANES), F32)
    lost, gathered = [], []
    for h in range(groups // 2):
        a, b = 2 * h, 2 * h + 1
        lanes = jnp.where(lefts, lane_of[a : a + 1], lane_of[b : b + 1])
        lanes = jnp.concatenate([lanes, lanes, none], axis=0).astype(BF16)
        mask = mm_tn(lanes, spread) == iota((LANES, PV), 1).astype(F32)
        gone = jnp.where(lefts, evaporated[a : a + 1], evaporated[b : b + 1])
        head = gone.astype(BF16).astype(F32)
        lost.append(mm_tn(jnp.concatenate([head, gone - head, none], axis=0).astype(BF16), take))
        fields = []
        for f in range(3):
            fields += split(jnp.where(mask, rows_ref[f, h * LANES : (h + 1) * LANES, :], 0.0), 2)
        gathered.append(jnp.concatenate(fields, axis=1))
    pulled = friction_timescale * mm(jnp.concatenate(gathered, axis=0), into)
    for h in range(groups // 2):
        change = pulled[h * LANES : (h + 1) * LANES] - lost[h]
        for i in range(2):
            g = 2 * h + i
            table = jnp.concatenate(
                [got_ref[g * share + k, 0:parcel_cap, :] for k in range(share)], axis=0
            )
            arrived_ref[g * size : (g + 1) * size, :] = table * keep + change[64 * i : 64 * i + size]
    copies.append(pltpu.make_async_copy(arrived_ref, arrived_hbm, sems.at[1, 2]))
    copies[-1].start()
    for copy in copies:
        copy.wait()


def fast(count=1):
    return [pl.BlockSpec(memory_space=pltpu.VMEM)] * count


def slow(count=1):
    return [pl.BlockSpec(memory_space=pltpu.HBM)] * count


def call(kernel, name, out, in_specs, scratch=(), out_specs=None, kib=1024):
    out_specs = out_specs or fast(len(out))
    run = pl.pallas_call(
        kernel,
        out_shape=tuple(
            (pltpu.HBM if spec.memory_space is pltpu.HBM else pltpu.VMEM)(s, t)
            for (s, t), spec in zip(out, out_specs, strict=True)
        ),
        in_specs=in_specs,
        out_specs=tuple(out_specs),
        scratch_shapes=list(scratch),
        compiler_params=pltpu.CompilerParams(vmem_limit_bytes=VMEM_LIMIT),
        cost_estimate=pl.CostEstimate(flops=0, transcendentals=0, bytes_accessed=kib * 1024),
        name=name,
    )

    def held(*operands):
        return run(
            *(
                pltpu.with_memory_space_constraint(a, spec.memory_space)
                for a, spec in zip(operands, in_specs, strict=True)
            )
        )

    return held


def after(value, *others):
    return pl.pallas_call(
        pass_kernel,
        out_shape=pltpu.VMEM(value.shape, value.dtype),
        in_specs=fast(1 + len(others)),
        out_specs=fast()[0],
        input_output_aliases={0: 0},
        name="after",
    )(*(pltpu.with_memory_space_constraint(a, pltpu.VMEM) for a in (value, *others)))


def dma(*count):
    return pltpu.SemaphoreType.DMA(count)


def body(
    species,
    interface_normal_flow,
    face_diffusion,
    inv_volume,
    diffusivity,
    low_partner,
    high_partner,
    low_orient,
    high_orient,
    droplet_table,
    parcel_block,
    parcel_cell,
    parcel_live,
):
    blocks = lax.axis_size("blk")
    local_species, layers, cells = species.shape
    parcels = droplet_table.shape[0]
    tile_cap = max(1, TILES // blocks)
    parcel_cap = 3 * parcels // (2 * blocks)
    sizes = (blocks, tile_cap, parcel_cap)
    tall = layers * cells // LANES
    rows = -(-(parcel_cap + PAIRS * tile_cap + 6) // 8) * 8
    groups = blocks * parcel_cap // 48
    int_row = (1, parcels)
    vmem = pltpu.VMEM

    def swap(value, bit):
        return lax.ppermute(value, "sp", [(i, i ^ bit) for i in range(lax.axis_size("sp"))])

    factors = diffusivity.reshape(1, local_species)
    other_species = swap(species, 1)
    other_factors = swap(factors, 1)

    m0, own_factors, strips, strip, column, code, slot, table, vel, dif = call(
        functools.partial(pack_meta_kernel, *sizes),
        "pack_meta",
        [
            ((z_row(blocks) + TILES, LANES), F32),
            ((8, LANES), F32),
            ((32, STRIP), F32),
            ((2, TILES, LANES), F32),
            ((2, TILES, STRIP), F32),
            ((2, TILES, STRIP), F32),
            ((8, parcels), jnp.int32),
            (droplet_table.shape, F32),
            ((8, cells), F32),
            ((8, cells), F32),
        ],
        slow(12),
        [
            vmem((local_species, 8, cells), F32),
            vmem((local_species, 8, cells), F32),
            vmem((1, local_species), F32),
            vmem((4, 1, TILES), jnp.int32),
            vmem((3,) + int_row, jnp.int32),
            dma(13),
        ],
        kib=10000,
    )(
        species,
        factors,
        low_partner,
        high_partner,
        low_orient,
        high_orient,
        droplet_table,
        parcel_block.reshape(int_row),
        parcel_cell.reshape(int_row),
        parcel_live.reshape(int_row),
        interface_normal_flow,
        face_diffusion,
    )
    m1, m2, m3 = swap(m0, 1), swap(m0, 2), swap(m0, 3)


    packed, edge_flow = call(
        functools.partial(pack_rows_kernel, *sizes),
        "pack_rows",
        [((blocks, rows, LANES), F32), ((16, STRIP), F32)],
        fast(9),
        kib=10000,
    )(
        table,
        vel,
        dif,
        strips,
        strip,
        column,
        code,
        slot,
        m0,
    )
    z_half, fuel_half = call(
        sum_kernel,
        "chip_sum",
        [((layers // 2, cells), F32), ((layers // 2, cells), F32)],
        fast(2) + slow(1) + fast(3),
        [vmem((1, local_species), F32), pltpu.SemaphoreType.DMA],
        kib=4680,
    )(species, other_species, factors, other_factors, m1, edge_flow)
    z_half = after(z_half, m2, m3)
    z_far = swap(z_half, 2)
    fuel_far = swap(fuel_half, 2)

    (z_own,) = call(
        add_kernel, "z_own", [((layers // 2, cells), F32)], fast(2), kib=1000
    )(z_half, z_far)
    (ready,) = call(
        functools.partial(assemble_kernel, *sizes),
        "assemble",
        [((blocks, rows, LANES), F32)],
        fast(6),
        kib=2880,
    )(packed, m0, m1, m2, m3, z_half)
    z_other = swap(z_own, 1)
    got = lax.all_to_all(ready, "blk", split_axis=0, concat_axis=0, tiled=True)

    base, edge_z = call(
        inner_kernel,
        "inner_flux",
        [(species.shape, F32), ((32, STRIP), F32)],
        slow(4) + fast(3),
        [
            vmem(interface_normal_flow.shape, F32),
            vmem(face_diffusion.shape, F32),
            vmem((layers, cells), F32),
            vmem(species.shape, F32),
            vmem((layers, cells), F32),
            dma(4, 4),
        ],
        kib=25200,
    )(
        interface_normal_flow,
        face_diffusion,
        inv_volume,
        species,
        z_own,
        z_other,
        own_factors,
    )

    (fuel_own,) = call(
        fuel_half_kernel,
        "fuel_half",
        [((layers // 2, cells), F32)],
        fast(3),
        kib=360,
    )(fuel_half, fuel_far, edge_z)
    fuel_other = swap(fuel_own, 1)
    (fuel_parts,) = call(
        fuel_kernel, "fuel_parts", [((2 * LANES, tall), BF16)], fast(2), kib=1080
    )(fuel_own, fuel_other)

    return call(
        functools.partial(final_kernel, *sizes),
        "final",
        [(species.shape, F32), ((blocks * parcel_cap, PV), F32)],
        fast(3) + slow(3) + fast(6),
        [
            vmem(species.shape, F32),
            vmem((blocks * parcel_cap, PV), F32),
            vmem((tall, 3 * groups // 2 * LANES), BF16),
            vmem((2 * LANES, 3 * groups // 2 * LANES), BF16),
            vmem((8, cells), F32),
            vmem(species.shape, F32),
            vmem((layers, cells), F32),
            vmem((3, tall, LANES), F32),
            vmem((groups, LANES), jnp.int32),
            pltpu.SMEM((groups, LANES), jnp.int32),
            vmem((3, 64 * groups, PV), F32),
            dma(2, 4),
            dma(cells // LANES),
            pltpu.SemaphoreType.DMA,
        ],
        slow(2),
        kib=32400,
    )(
        got,
        fuel_parts,
        base,
        species,
        inv_volume,
        interface_normal_flow,
        edge_z,
        edge_flow,
        strips,
        strip,
        column,
        own_factors,
    )


def solution(mesh):
    placed = (
        P("sp", "blk", None),
        P(None, "blk", None),
        P(None, "blk", None),
        P("blk", None),
        P("sp"),
        P("blk", None),
        P("blk", None),
        P("blk", None),
        P("blk", None),
        P(("blk", "sp"), None),
        P(("blk", "sp"), None),
        P(("blk", "sp")),
        P(("blk", "sp")),
    )
    return jax.shard_map(
        body,
        mesh=mesh,
        in_specs=placed,
        out_specs=(P("sp", "blk", None), P(("blk", "sp"), None)),
        check_vma=False,
    )
```
